32 devices in a mesh: grp: 2 (over y), lat: 4 (over z), chan: 2 (over core), ens: 2 (over x).
Axes of the slice: x: 2, y: 2, z: 4, core: 2. Of those that a mesh axis runs over, the one named last changes fastest.
Arguments:
- grad_out: bfloat16 [4, 24, 48, 384], P(('grp', 'ens'), 'lat', None, 'chan'), parts along dimension 0, may hold values from -6 to 6
- pre_act: bfloat16 [4, 24, 48, 384], P(('grp', 'ens'), 'lat', None, 'chan'), parts along dimension 0, may hold values from -6 to 6
- coeffs: bfloat16 [4, 24, 24, 2, 384], P(('grp', 'ens'), ('lat', 'chan')), parts along dimension 0, may hold values from -6 to 6
- legendre: bfloat16 [24, 24, 24], P(('lat', 'chan'), None, 'ens'), may hold values from -1.25 to 1.25
- mixing: bfloat16 [384, 384], replicated, may hold values from -0.3125 to 0.3125
Outputs:
- grad_in: bfloat16 [4, 24, 48, 384], P(('grp', 'ens'), 'lat', None, 'chan'), parts along dimension 0
- mixing_grad: float32 [768, 384], P('grp'), parts along dimension 0
The draws below stay inside these ranges and needn't reach their ends.
There are 2 independent parts, one for each index of `grp`. The reference program is written for one: setup_inputs(seed, part) draws one part's arguments, and reference() takes and returns one part's arrays. A program takes and returns all parts, laid end to end along the dimension named above; an argument that names none is the same for every part. Nothing has to cross between parts.
All inputs are finite; a program needn't handle non-finite values.
Results may differ from the reference program's by a relative error of at most 0.0074.
Values may be sent and summed in bfloat16 or wider, within the bound.
No kernel may reach another device: no remote copies, remote signals or barrier semaphores. Data moves between devices by JAX's collectives and lax.ppermute only.
A program may use at most 64 MiB of HBM per device.

```python
import math
import jax
import jax.numpy as jnp
from jax import lax

C = 384
NLAT = 24
NLON = 48
MODES = 24
DEGREES = 24
ENS = 2


def block_scale(key, extent, cuts, low, top_value):
    loudness, own = 1.0, jax.random.fold_in(key, 6)
    for position, shards_of in cuts:
        steps = jnp.exp(jax.random.uniform(jax.random.fold_in(own, position), (shards_of,), jnp.float32, low / len(cuts), top_value / len(cuts)))
        loudness = loudness * jnp.repeat(steps, extent[position] // shards_of).reshape([-1 if axis == position else 1 for axis in range(len(extent))])
    return loudness


def gaussian(stream_key, dims, scale, bound, pieces=(), kind=jnp.bfloat16):
    values = jax.random.normal(stream_key, dims, jnp.float32) * scale
    if len(pieces) > 0:
        values = block_scale(stream_key, dims, pieces, -0.22, 0.18) * values
    return jnp.clip(values, min=-bound, max=bound).astype(kind)


def setup_inputs(seed: int = 0, part: int = 0) -> dict:
    splits = jax.random.split(jax.random.key(seed), 6)
    part_splits = jax.random.split(jax.random.fold_in(splits[5], part), 6)
    grad_out = gaussian(part_splits[0], (ENS, NLAT, NLON, C), 1.0, 6.0, ((0, 2), (1, 4), (3, 2)))
    pre_act = gaussian(part_splits[1], (ENS, NLAT, NLON, C), 1.5, 6.0, ((0, 2), (1, 4), (3, 2)))
    coeffs = gaussian(part_splits[2], (ENS, MODES, DEGREES, 2, C), 1.0, 6.0, ((0, 2), (1, 8)))
    legendre = gaussian(splits[3], (MODES, DEGREES, NLAT), NLAT ** -0.5, 1.25, ((0, 8), (2, 2)))
    mixing = gaussian(splits[4], (C, C), C ** -0.5, 0.3125)
    return dict(grad_out=grad_out, pre_act=pre_act, coeffs=coeffs, legendre=legendre, mixing=mixing)


def fourier_table(lon_count, mode_count):
    longitude = jnp.arange(lon_count, dtype=jnp.int32)[:, None]
    wavenumber = jnp.arange(mode_count, dtype=jnp.int32)[None, :]
    product_index = longitude * wavenumber % lon_count
    angles = 2.0 * math.pi / lon_count * product_index.astype(jnp.float32)
    factor = math.sqrt(2.0 / lon_count)
    stacked = jnp.stack([jnp.cos(angles), -jnp.sin(angles)], axis=2) * factor
    return stacked.reshape(lon_count, 2 * mode_count).astype(jnp.bfloat16)

def silu_backward(cotangent, preact):
    values = preact.astype(jnp.float32)
    gate_value = jax.nn.sigmoid(values)
    return (cotangent.astype(jnp.float32) * gate_value * (1.0 + values * (1.0 - gate_value))).astype(jnp.bfloat16)

def reference(grad_out, pre_act, coeffs, legendre, mixing):
    fourier = fourier_table(NLON, MODES)
    fourier_wide = fourier.astype(jnp.float32)
    legendre_wide = legendre.astype(jnp.float32)
    weight_scale = 1.0 / (ENS * MODES)

    def member(member_data):
        cotangent, preact, stored = member_data
        scaled = silu_backward(cotangent, preact)
        spectral = jnp.einsum('nk,anc->akc', fourier_wide, scaled.astype(jnp.float32)).astype(jnp.bfloat16)
        spectral = spectral.reshape(NLAT, MODES, 2, C)
        coef_grad = jnp.einsum('mla,amrc->mlrc', legendre_wide, spectral.astype(jnp.float32)).astype(jnp.bfloat16)
        flat_grad = coef_grad.reshape(-1, C)
        weight_grad = jnp.dot(stored.reshape(-1, C).T, flat_grad, preferred_element_type=jnp.float32) * weight_scale
        mixed_grad = jnp.dot(flat_grad, mixing.T, preferred_element_type=jnp.float32).astype(jnp.bfloat16)
        mixed_grad = mixed_grad.reshape(MODES, DEGREES, 2, C)
        returned = jnp.einsum('mla,mlrc->amrc', legendre_wide, mixed_grad.astype(jnp.float32)).astype(jnp.bfloat16)
        returned = returned.reshape(NLAT, 2 * MODES, C)
        spatial = jnp.einsum('nk,akc->anc', fourier_wide, returned.astype(jnp.float32))
        result = (cotangent.astype(jnp.float32) + spatial).astype(jnp.bfloat16)
        return (result, weight_grad)
    results, weight_grads = lax.map(member, (grad_out, pre_act, coeffs))
    return (results, lax.optimization_barrier(jnp.sum(weight_grads, axis=0)))
```

```python
import math

import jax
import jax.numpy as jnp
import numpy as np
from jax import lax
from jax.experimental import pallas as pl
from jax.experimental.pallas import tpu as pltpu
from jax.sharding import PartitionSpec as P

VMEM = pl.BlockSpec(memory_space=pltpu.VMEM)
BF16 = jnp.bfloat16
F32 = jnp.float32


def fourier_table(lon_count, mode_count):
    longitude = np.arange(lon_count, dtype=np.int32)[:, None]
    wavenumber = np.arange(mode_count, dtype=np.int32)[None, :]
    product_index = longitude * wavenumber % lon_count
    angles = np.float32(2.0 * math.pi / lon_count) * product_index.astype(np.float32)
    factor = np.float32(math.sqrt(2.0 / lon_count))
    stacked = np.stack([np.cos(angles), -np.sin(angles)], axis=2) * factor
    return stacked.reshape(lon_count, 2 * mode_count).astype(BF16)


def row_padding(rows):
    return -(-rows // 8) * 8


def analysis_matrix(lat_rows, lon_count, mode_count, owners):
    width = 2 * mode_count // owners
    table = np.asarray(fourier_table(lon_count, mode_count)).astype(np.float32)
    table = table.T.reshape(owners, width, lon_count)
    full = np.zeros((owners, lat_rows, width, lat_rows, lon_count), np.float32)
    for row in range(lat_rows):
        full[:, row, :, row, :] = table
    full = full.reshape(owners, lat_rows * width, lat_rows * lon_count)
    padded = np.zeros((owners, row_padding(lat_rows * width), lat_rows * lon_count), np.float32)
    padded[:, : lat_rows * width] = full
    return padded.astype(BF16)


def expansion_tables(local_modes, degrees, lat_rows, lat_devices, ens_devices):
    width = 2 * local_modes
    cols = row_padding(lat_rows * width)
    lat_count = lat_rows * lat_devices
    share = lat_count // ens_devices
    rows_of = np.arange(local_modes * degrees * 2)
    pick_rows = (rows_of[:, None] // 2 == np.arange(local_modes * degrees)[None, :])
    col = np.arange(lat_devices * cols)
    device, inner = col // cols, col % cols
    valid = inner < lat_rows * width
    lat = device * lat_rows + inner // width
    pick_lat = (np.arange(lat_count)[:, None] == lat[None, :]) & valid[None, :]
    mode_of_row, part_of_row = rows_of // (2 * degrees), rows_of % 2
    mode_of_col, part_of_col = inner % width // 2, inner % 2
    keep = (mode_of_row[:, None] == mode_of_col[None, :]) & (
        part_of_row[:, None] == part_of_col[None, :]
    )
    return (
        pick_rows.astype(BF16),
        pick_lat.reshape(ens_devices, share, lat_devices * cols).astype(BF16),
        keep.astype(np.float32),
    )


def analyse(grad_ref, pre_ref, table_ref, out_ref):
    rows = grad_ref.shape[0] * grad_ref.shape[1]
    values = pre_ref[...].reshape(rows, -1).astype(F32)
    gate = 1.0 / (1.0 + jnp.exp(-values))
    cotangent = grad_ref[...].reshape(rows, -1).astype(F32)
    scaled = (cotangent * gate * (1.0 + values * (1.0 - gate))).astype(BF16)
    owners = table_ref.shape[0]
    for owner in range(owners):
        out_ref[owner] = jnp.dot(table_ref[owner], scaled, preferred_element_type=F32).astype(BF16)


def spread_legendre(gathered_ref, pick_rows_ref, pick_lat_ref, keep_ref, out_ref):
    total = None
    for part in range(gathered_ref.shape[0]):
        term = jnp.dot(gathered_ref[part], pick_lat_ref[part], preferred_element_type=F32)
        total = term if total is None else total + term
    rows = jnp.dot(pick_rows_ref[...], total.astype(BF16), preferred_element_type=F32)
    out_ref[...] = (rows * keep_ref[...]).astype(BF16)


def mix(lat_devices, chan_count, scale, recv_ref, spread_ref, coeffs_ref, mixing_ref, send_ref, term_ref):
    chunk_rows, half = recv_ref.shape[1], recv_ref.shape[2]
    parts = []
    for h in range(chan_count):
        block = jnp.concatenate([recv_ref[j * chan_count + h] for j in range(lat_devices)], axis=0)
        parts.append(jnp.dot(spread_ref[...], block, preferred_element_type=F32).astype(BF16))
    coef = jnp.concatenate(parts, axis=1)
    mixed = lax.dot_general(
        coef, mixing_ref[...], (((1,), (1,)), ((), ())), preferred_element_type=F32
    ).astype(BF16)
    returned = lax.dot_general(
        spread_ref[...], mixed, (((0,), (0,)), ((), ())), preferred_element_type=F32
    ).astype(BF16)
    for j in range(lat_devices):
        for h in range(chan_count):
            send_ref[j * chan_count + h] = returned[
                j * chunk_rows : (j + 1) * chunk_rows, h * half : (h + 1) * half
            ]
    term = lax.dot_general(
        coeffs_ref[...], coef, (((0,), (0,)), ((), ())), preferred_element_type=F32
    )
    term_ref[...] = (term * scale).reshape(term_ref.shape).astype(term_ref.dtype)


def synthesise(recv_ref, table_ref, grad_ref, out_ref):
    received = recv_ref[...].reshape(-1, recv_ref.shape[2])
    spatial = jnp.dot(table_ref[...], received, preferred_element_type=F32)
    rows, lon_count, cols = grad_ref.shape
    result = grad_ref[...].astype(F32) + spatial.reshape(rows, lon_count, cols)
    out_ref[...] = result.astype(BF16)


def add_terms(terms_ref, out_ref):
    total = jnp.sum(terms_ref[...].astype(F32), axis=0)
    out_ref[...] = jnp.broadcast_to(total[None], out_ref.shape).astype(BF16)


def widen(blocks_ref, out_ref):
    out_ref[...] = blocks_ref[...].astype(F32).reshape(out_ref.shape)


def call(kernel, outs, *operands):
    return pl.pallas_call(
        kernel,
        out_shape=outs,
        in_specs=[VMEM] * len(operands),
        out_specs=jax.tree.map(lambda _: VMEM, outs),
        compiler_params=pltpu.CompilerParams(vmem_limit_bytes=56 * 1024 * 1024),
    )(*operands)


def on_device(grad_out, pre_act, coeffs, legendre, mixing):
    lat_rows, lon_count, chan_cols = grad_out.shape[1:]
    mode_count = lon_count // 2
    lat_devices = lax.axis_size("lat")
    chan_count = lax.axis_size("chan")
    members = lax.axis_size("ens")
    owners = lat_devices * chan_count
    terms = owners * members
    channels = chan_cols * chan_count
    local_modes = mode_count // owners
    degrees = legendre.shape[1]
    table = analysis_matrix(lat_rows, lon_count, mode_count, owners)
    chunk_rows = table.shape[1]
    pick_rows, pick_lat, keep = expansion_tables(
        local_modes, degrees, lat_rows, lat_devices, members
    )
    chunks = jax.ShapeDtypeStruct((owners, chunk_rows, chan_cols), BF16)

    spectral = call(analyse, chunks, grad_out[0], pre_act[0], jnp.asarray(table))
    spectral = lax.all_to_all(spectral, ("lat", "chan"), split_axis=0, concat_axis=0, tiled=True)

    flat_legendre = legendre.reshape(local_modes * degrees, -1)
    gathered = lax.all_gather(flat_legendre, "ens", axis=0)
    spread = call(
        spread_legendre,
        jax.ShapeDtypeStruct(keep.shape, BF16),
        gathered,
        jnp.asarray(pick_rows),
        jnp.asarray(pick_lat),
        jnp.asarray(keep),
    )

    even = channels % terms == 0
    if even:
        term_shape = jax.ShapeDtypeStruct((terms, channels // terms, channels), BF16)
    else:
        term_shape = jax.ShapeDtypeStruct((channels, channels), F32)
    scale = 1.0 / (members * mode_count)
    returned, term = call(
        lambda *refs: mix(lat_devices, chan_count, scale, *refs),
        (chunks, term_shape),
        spectral,
        spread,
        coeffs.reshape(-1, channels),
        mixing,
    )
    returned = lax.all_to_all(returned, ("lat", "chan"), split_axis=0, concat_axis=0, tiled=True)
    back = jnp.asarray(np.ascontiguousarray(table.reshape(-1, lat_rows * lon_count).T))
    result = call(
        synthesise, jax.ShapeDtypeStruct(grad_out.shape[1:], BF16), returned, back, grad_out[0]
    )

    axes = ("lat", "chan", "ens")
    if even:
        collected = lax.all_to_all(term, axes, split_axis=0, concat_axis=0, tiled=True)
        total = call(add_terms, term_shape, collected)
        total = lax.all_to_all(total, axes, split_axis=0, concat_axis=0, tiled=True)
        weight_grad = call(widen, jax.ShapeDtypeStruct((channels, channels), F32), total)
    else:
        weight_grad = lax.psum(term, axes)
    return (result[None], weight_grad)


def solution(mesh):
    placed = (
        P(("grp", "ens"), "lat", None, "chan"),
        P(("grp", "ens"), "lat", None, "chan"),
        P(("grp", "ens"), ("lat", "chan"), None, None, None),
        P(("lat", "chan"), None, "ens"),
        P(),
    )
    return jax.shard_map(
        on_device,
        mesh=mesh,
        in_specs=placed,
        out_specs=(P(("grp", "ens"), "lat", None, "chan"), P("grp", None)),
        check_vma=False,
    )
```

```python
import math

import jax
import jax.numpy as jnp
import numpy as np
from jax import lax
from jax.experimental import pallas as pl
from jax.experimental.pallas import tpu as pltpu
from jax.sharding import PartitionSpec as P

VMEM = pl.BlockSpec(memory_space=pltpu.VMEM)
BF16 = jnp.bfloat16
F32 = jnp.float32


def fourier_table(lon_count, mode_count):
    longitude = np.arange(lon_count, dtype=np.int32)[:, None]
    wavenumber = np.arange(mode_count, dtype=np.int32)[None, :]
    product_index = longitude * wavenumber % lon_count
    angles = np.float32(2.0 * math.pi / lon_count) * product_index.astype(np.float32)
    factor = np.float32(math.sqrt(2.0 / lon_count))
    stacked = np.stack([np.cos(angles), -np.sin(angles)], axis=2) * factor
    return stacked.reshape(lon_count, 2 * mode_count).astype(BF16)


def row_padding(rows):
    return -(-rows // 8) * 8


def analysis_matrix(lat_rows, lon_count, mode_count, owners):
    width = 2 * mode_count // owners
    table = np.asarray(fourier_table(lon_count, mode_count)).astype(np.float32)
    table = table.T.reshape(owners, width, lon_count)
    full = np.zeros((owners, lat_rows, width, lat_rows, lon_count), np.float32)
    for row in range(lat_rows):
        full[:, row, :, row, :] = table
    full = full.reshape(owners, lat_rows * width, lat_rows * lon_count)
    padded = np.zeros((owners, row_padding(lat_rows * width), lat_rows * lon_count), np.float32)
    padded[:, : lat_rows * width] = full
    return padded.astype(BF16)


def expansion_tables(local_modes, degrees, lat_rows, lat_devices, ens_devices):
    width = 2 * local_modes
    cols = row_padding(lat_rows * width)
    lat_count = lat_rows * lat_devices
    share = lat_count // ens_devices
    rows_of = np.arange(local_modes * degrees * 2)
    pick_rows = (rows_of[:, None] // 2 == np.arange(local_modes * degrees)[None, :])
    col = np.arange(lat_devices * cols)
    device, inner = col // cols, col % cols
    valid = inner < lat_rows * width
    lat = device * lat_rows + inner // width
    pick_lat = (np.arange(lat_count)[:, None] == lat[None, :]) & valid[None, :]
    mode_of_row, part_of_row = rows_of // (2 * degrees), rows_of % 2
    mode_of_col, part_of_col = inner % width // 2, inner % 2
    keep = (mode_of_row[:, None] == mode_of_col[None, :]) & (
        part_of_row[:, None] == part_of_col[None, :]
    )
    return (
        pick_rows.astype(BF16),
        pick_lat.reshape(ens_devices, share, lat_devices * cols).astype(BF16),
        keep.astype(np.float32),
    )


def partner(me, step, count):
    return me ^ step


def analyse(axes, refs):
    grad_ref, pre_ref, table_ref = refs[:3]
    out_refs, held_ref = refs[3:-1], refs[-1]
    rows = grad_ref.shape[0] * grad_ref.shape[1]
    values = pre_ref[...].reshape(rows, -1).astype(F32)
    gate = 1.0 / (1.0 + jnp.exp(-values))
    cotangent = grad_ref[...].reshape(rows, -1).astype(F32)
    scaled = (cotangent * gate * (1.0 + values * (1.0 - gate))).astype(BF16)
    owners, chunk_rows, _ = table_ref.shape
    table = table_ref[...].reshape(owners * chunk_rows, -1)
    spectral = jnp.dot(table, scaled, preferred_element_type=F32)
    held_ref[...] = spectral.reshape(held_ref.shape)
    me = lax.axis_index(axes)
    for step in range(owners):
        out_refs[step][...] = held_ref[partner(me, step, owners)].astype(BF16)


def spread_legendre(refs):
    own_refs = refs[:-4]
    pick_rows_ref, pick_lat_ref, keep_ref, out_ref = refs[-4:]
    me = lax.axis_index("ens")
    total = None
    for step, part_ref in enumerate(own_refs):
        pick = pick_lat_ref[partner(me, step, len(own_refs))]
        term = jnp.dot(part_ref[...], pick, preferred_element_type=F32)
        total = term if total is None else total + term
    rows = jnp.dot(pick_rows_ref[...], total.astype(BF16), preferred_element_type=F32)
    out_ref[...] = (rows * keep_ref[...]).astype(BF16)


def mix(lat_devices, chan_count, scale, terms, refs):
    owners = lat_devices * chan_count
    recv_refs, (spread_ref, coeffs_ref, mixing_ref) = refs[:owners], refs[owners : owners + 3]
    send_refs = refs[owners + 3 : 2 * owners + 3]
    term_refs = refs[2 * owners + 3 : 2 * owners + 3 + terms]
    held_ref, out_ref, term_ref = refs[2 * owners + 3 + terms :]
    chunk_rows, half = recv_refs[0].shape
    me = lax.axis_index(("lat", "chan"))
    for step in range(owners):
        held_ref[partner(me, step, owners)] = recv_refs[step][...].astype(F32)
    parts = []
    for h in range(chan_count):
        block = jnp.concatenate([held_ref[j * chan_count + h] for j in range(lat_devices)], axis=0)
        parts.append(
            jnp.dot(spread_ref[...], block.astype(BF16), preferred_element_type=F32).astype(BF16)
        )
    coef = jnp.concatenate(parts, axis=1)
    mixed = lax.dot_general(
        coef, mixing_ref[...], (((1,), (1,)), ((), ())), preferred_element_type=F32
    ).astype(BF16)
    returned = lax.dot_general(
        spread_ref[...], mixed, (((0,), (0,)), ((), ())), preferred_element_type=F32
    )
    for j in range(lat_devices):
        for h in range(chan_count):
            out_ref[j * chan_count + h] = returned[
                j * chunk_rows : (j + 1) * chunk_rows, h * half : (h + 1) * half
            ]
    for step in range(owners):
        send_refs[step][...] = out_ref[partner(me, step, owners)].astype(BF16)
    term = lax.dot_general(
        coeffs_ref[...], coef, (((0,), (0,)), ((), ())), preferred_element_type=F32
    )
    term_ref[...] = (term * scale).reshape(term_ref.shape)
    if terms == 1:
        term_refs[0][...] = term_ref[0]
    else:
        place = lax.axis_index(("lat", "chan", "ens"))
        for step in range(terms):
            term_refs[step][...] = term_ref[partner(place, step, terms)].astype(BF16)


def synthesise(axes, refs):
    recv_refs, (table_ref, grad_ref, out_ref, held_ref) = refs[:-4], refs[-4:]
    owners = len(recv_refs)
    me = lax.axis_index(axes)
    for step in range(owners):
        held_ref[partner(me, step, owners)] = recv_refs[step][...].astype(F32)
    received = held_ref[...].reshape(-1, held_ref.shape[2]).astype(BF16)
    if len(table_ref.shape) == 3:
        table, depth = table_ref[...].reshape(received.shape[0], -1), 0
    else:
        table, depth = table_ref[...], 1
    spatial = lax.dot_general(
        table, received, (((depth,), (0,)), ((), ())), preferred_element_type=F32
    )
    rows, lon_count, cols = grad_ref.shape
    result = grad_ref[...].astype(F32) + spatial.reshape(rows, lon_count, cols)
    out_ref[...] = result.astype(BF16)


def add_terms(refs):
    total = refs[0][...].astype(F32)
    for ref in refs[1:-1]:
        total = total + ref[...].astype(F32)
    refs[-1][...] = total.astype(BF16)


def widen(refs):
    block_refs, (out_ref, held_ref) = refs[:-2], refs[-2:]
    terms = len(block_refs)
    me = lax.axis_index(("lat", "chan", "ens"))
    for step in range(terms):
        held_ref[partner(me, step, terms)] = block_refs[step][...].astype(F32)
    out_ref[...] = held_ref[...].reshape(out_ref.shape)


def call(kernel, outs, operands, scratch=()):
    sizes = [math.prod(x.shape) * x.dtype.itemsize for x in (*operands, *outs)]
    sizes += [math.prod(x.shape) * 4 for x in scratch]
    return pl.pallas_call(
        lambda *refs: kernel(refs),
        out_shape=tuple(outs),
        in_specs=[VMEM] * len(operands),
        out_specs=(VMEM,) * len(outs),
        scratch_shapes=scratch,
        compiler_params=pltpu.CompilerParams(
            vmem_limit_bytes=min(56 << 20, (6 << 20) + 4 * sum(sizes))
        ),
        cost_estimate=pl.CostEstimate(
            flops=1000000, bytes_accessed=2 * sum(sizes), transcendentals=0
        ),
    )(*operands)


def swap(blocks, axes):
    count = len(blocks)
    received = [blocks[0]]
    for step in range(1, count):
        pairs = [(device, partner(device, step, count)) for device in range(count)]
        received.append(lax.ppermute(blocks[step], axes, pairs))
    return received


def repeat(block, axes, count):
    return swap([block] * count, axes)


def on_device(grad_out, pre_act, coeffs, legendre, mixing):
    lat_rows, lon_count, chan_cols = grad_out.shape[1:]
    mode_count = lon_count // 2
    lat_devices = lax.axis_size("lat")
    chan_count = lax.axis_size("chan")
    members = lax.axis_size("ens")
    owners = lat_devices * chan_count
    terms = owners * members
    channels = chan_cols * chan_count
    local_modes = mode_count // owners
    degrees = legendre.shape[1]
    table = analysis_matrix(lat_rows, lon_count, mode_count, owners)
    chunk_rows = table.shape[1]
    pick_rows, pick_lat, keep = expansion_tables(
        local_modes, degrees, lat_rows, lat_devices, members
    )
    rows_axes, axes = ("lat", "chan"), ("lat", "chan", "ens")
    chunk = jax.ShapeDtypeStruct((chunk_rows, chan_cols), BF16)
    held = pltpu.VMEM((owners, chunk_rows, chan_cols), F32)

    legendre_parts = repeat(legendre.reshape(local_modes * degrees, -1), "ens", members)
    spectral = call(
        lambda refs: analyse(rows_axes, refs),
        [chunk] * owners,
        (grad_out[0], pre_act[0], jnp.asarray(table)),
        (held,),
    )
    spectral = swap(spectral, rows_axes)
    (spread,) = call(
        spread_legendre,
        [jax.ShapeDtypeStruct(keep.shape, BF16)],
        (*legendre_parts, jnp.asarray(pick_rows), jnp.asarray(pick_lat), jnp.asarray(keep)),
    )

    small = terms <= 16 and channels % terms == 0
    blocks = terms if small else 1
    block = jax.ShapeDtypeStruct((channels // blocks, channels), BF16 if small else F32)
    scale = 1.0 / (members * mode_count)
    outs = call(
        lambda refs: mix(lat_devices, chan_count, scale, blocks, refs),
        [chunk] * owners + [block] * blocks,
        (*spectral, spread, coeffs.reshape(-1, channels), mixing),
        (held, held, pltpu.VMEM((blocks, *block.shape), F32)),
    )
    returned = swap(outs[:owners], rows_axes)
    if table.size < 1 << 20:
        back = jnp.asarray(np.ascontiguousarray(table.reshape(-1, lat_rows * lon_count).T))
    else:
        back = jnp.asarray(table)
    (result,) = call(
        lambda refs: synthesise(rows_axes, refs),
        [jax.ShapeDtypeStruct(grad_out.shape[1:], BF16)],
        (*returned, back, grad_out[0]),
        (held,),
    )
    if small:
        (total,) = call(add_terms, [block], swap(outs[owners:], axes))
        (weight_grad,) = call(
            widen,
            [jax.ShapeDtypeStruct((channels, channels), F32)],
            repeat(total, axes, terms),
            (pltpu.VMEM((blocks, *block.shape), F32),),
        )
    else:
        weight_grad = lax.psum(outs[owners], axes)
    return (result[None], weight_grad)


def solution(mesh):
    placed = (
        P(("grp", "ens"), "lat", None, "chan"),
        P(("grp", "ens"), "lat", None, "chan"),
        P(("grp", "ens"), ("lat", "chan"), None, None, None),
        P(("lat", "chan"), None, "ens"),
        P(),
    )
    return jax.shard_map(
        on_device,
        mesh=mesh,
        in_specs=placed,
        out_specs=(P(("grp", "ens"), "lat", None, "chan"), P("grp", None)),
        check_vma=False,
    )
```

```python
import math

import jax
import jax.numpy as jnp
import numpy as np
from jax import lax
from jax.experimental import pallas as pl
from jax.experimental.pallas import tpu as pltpu
from jax.sharding import PartitionSpec as P

VMEM = pl.BlockSpec(memory_space=pltpu.VMEM)
BF16 = jnp.bfloat16
F32 = jnp.float32


def fourier_table(lon_count, mode_count):
    longitude = np.arange(lon_count, dtype=np.int32)[:, None]
    wavenumber = np.arange(mode_count, dtype=np.int32)[None, :]
    product_index = longitude * wavenumber % lon_count
    angles = np.float32(2.0 * math.pi / lon_count) * product_index.astype(np.float32)
    factor = np.float32(math.sqrt(2.0 / lon_count))
    stacked = np.stack([np.cos(angles), -np.sin(angles)], axis=2) * factor
    return stacked.reshape(lon_count, 2 * mode_count).astype(BF16)


def padded(rows, tile):
    return -(-rows // tile) * tile


def analysis_matrix(lat_rows, lon_count, mode_count, groups):
    width = 2 * mode_count // groups
    table = np.asarray(fourier_table(lon_count, mode_count)).astype(np.float32)
    table = table.T.reshape(groups, width, lon_count)
    full = np.zeros((groups, lat_rows, width, lat_rows, lon_count), np.float32)
    for row in range(lat_rows):
        full[:, row, :, row, :] = table
    full = full.reshape(groups, lat_rows * width, lat_rows * lon_count)
    out = np.zeros((groups, padded(lat_rows * width, 8), lat_rows * lon_count), np.float32)
    out[:, : lat_rows * width] = full
    return out.astype(BF16)


def expansion_tables(local_modes, chan_count, degrees, lat_rows, groups, members):
    modes = local_modes * chan_count
    width = 2 * modes
    cols = padded(lat_rows * width, 8)
    lat_count = lat_rows * groups
    row = np.arange(local_modes * degrees * 2)
    pick_rows = row[:, None] // 2 == np.arange(local_modes * degrees)[None, :]
    col = np.arange(groups * cols)
    group, inner = col // cols, col % cols
    valid = inner < lat_rows * width
    lat = group * lat_rows + inner // width
    pick_lat = (np.arange(lat_count)[:, None] == lat[None, :]) & valid[None, :]
    kind_of_row = row // (2 * degrees) * 2 + row % 2
    kind_of_row = kind_of_row[None] + 2 * local_modes * np.arange(chan_count)[:, None]
    kind_of_col = inner % width
    kinds = np.arange(width)
    return (
        pick_rows.astype(BF16),
        pick_lat.reshape(members, lat_count // members, groups * cols).astype(BF16),
        (kind_of_row[:, :, None] == kinds).astype(BF16),
        (kinds[:, None] == kind_of_col[None, :]).astype(BF16),
    )


def partner(me, step):
    return me ^ step


def dot(left, right, left_dim=1, right_dim=0):
    return lax.dot_general(
        left, right, (((left_dim,), (right_dim,)), ((), ())), preferred_element_type=F32
    )


def analyse(grad_hbm, pre_hbm, table_hbm, *refs):
    groups = table_hbm.shape[0]
    out_refs, (grad_ref, pre_ref, table_ref, held_ref, sems) = refs[:groups], refs[groups:]
    copies = [
        pltpu.make_async_copy(source, target, sems.at[place])
        for place, (source, target) in enumerate(
            [(grad_hbm, grad_ref), (pre_hbm, pre_ref), (table_hbm, table_ref)]
        )
    ]
    for copy in copies:
        copy.start()
    for copy in copies:
        copy.wait()
    rows = grad_ref.shape[0] * grad_ref.shape[1]
    values = pre_ref[...].reshape(rows, -1).astype(F32)
    gate = 1.0 / (1.0 + jnp.exp(-values))
    cotangent = grad_ref[...].reshape(rows, -1).astype(F32)
    scaled = (cotangent * gate * (1.0 + values * (1.0 - gate))).astype(BF16)
    table = table_ref[...].reshape(groups * table_ref.shape[1], -1)
    held_ref[...] = dot(table, scaled).reshape(held_ref.shape)
    me = lax.axis_index("lat")
    for step in range(groups):
        out_refs[step][...] = held_ref[partner(me, step)].astype(BF16)


def prepare(*refs):
    legendre_refs = refs[:-7]
    pick_rows_ref, pick_lat_ref, row_kind_ref, col_kind_ref, mixing_ref = refs[-7:-2]
    spread_ref, mixing_out = refs[-2:]
    chan, ens = lax.axis_index("chan"), lax.axis_index("ens")
    members, pairs = pick_lat_ref.shape[0], pick_lat_ref.shape[0] * pick_rows_ref.shape[1]
    count = pairs // members
    for step, part_ref in enumerate(legendre_refs):
        core = partner(chan, step)
        total = None
        for place in range(members):
            term = dot(
                part_ref[place].astype(BF16), pick_lat_ref[partner(ens, place)]
            )
            total = term if total is None else total + term
        rows = dot(pick_rows_ref[...], total.astype(BF16))
        keep = dot(row_kind_ref[core], col_kind_ref[...])
        spread_ref[core] = (rows * keep).astype(BF16)
    halves, half, _ = mixing_out.shape
    rows = mixing_ref[pl.ds(pl.multiple_of(chan * half, half), half), :]
    for core in range(halves):
        mixing_out[core] = rows[:, core * half : (core + 1) * half]


def coefficients(groups, chan_count, members, scale, *refs):
    recv_refs = refs[:groups]
    spread_ref = refs[groups]
    coeffs_refs = refs[groups + 1 : groups + 1 + chan_count]
    coef_out, term_own, *term_refs = refs[groups + 1 + chan_count : -3]
    held_ref, coef_ref, term_ref = refs[-3:]
    lat, chan, ens = (lax.axis_index(axis) for axis in ("lat", "chan", "ens"))
    for step in range(groups):
        held_ref[partner(lat, step)] = recv_refs[step][...].astype(F32)
    block = held_ref[...].reshape(-1, held_ref.shape[2]).astype(BF16)
    for core in range(chan_count):
        coef = dot(spread_ref[core], block).astype(BF16)
        coef_ref[core] = coef
        coef_out[core] = coef
    term = None
    for step in range(chan_count):
        part = dot(coeffs_refs[step][...], coef_ref[partner(chan, step)], 0, 0)
        term = part if term is None else term + part
    term_ref[...] = (term * scale).reshape(term_ref.shape)
    term_own[...] = term_ref[ens]
    for step in range(1, members):
        term_refs[step - 1][...] = term_ref[partner(ens, step)].astype(BF16)


def mix(groups, chan_count, members, piece, *refs):
    coef_refs = refs[:chan_count]
    mixing_ref, spread_ref, term_own = refs[chan_count : chan_count + 3]
    term_refs = refs[chan_count + 3 : chan_count + 2 + members]
    piece_out, *send_refs = refs[chan_count + 2 + members : -2]
    back_ref, term_ref = refs[-2:]
    lat, chan = lax.axis_index("lat"), lax.axis_index("chan")
    rows = coef_refs[0].shape[0] * coef_refs[0].shape[1]
    mixed = None
    for step in range(chan_count):
        coef = coef_refs[step][...].reshape(rows, -1)
        part = dot(coef, mixing_ref[partner(chan, step)], 1, 1)
        mixed = part if mixed is None else mixed + part
    mixed = mixed.astype(BF16)
    spread = spread_ref[...].reshape(rows, -1)
    back_ref[...] = dot(spread, mixed, 0, 0).reshape(back_ref.shape)
    term = term_own[...]
    for ref in term_refs:
        term = term + ref[...].astype(F32)
    for group in range(groups):
        term_ref[group, :piece] = term[group * piece : (group + 1) * piece]
    if piece < term_ref.shape[1]:
        term_ref[:, piece:] = jnp.zeros_like(term_ref[:, piece:])
    head = term_ref.shape[1]
    piece_out[...] = term_ref[lat]
    for step in range(groups):
        target = partner(lat, step)
        send_refs[step][head:] = back_ref[target].astype(BF16)
        if step > 0:
            send_refs[step][:head] = term_ref[target].astype(BF16)
        else:
            send_refs[step][:head] = jnp.zeros((head, term_ref.shape[2]), BF16)


def add_pieces(piece_ref, *refs):
    total = piece_ref[...]
    for ref in refs[:-1]:
        total = total + ref[: total.shape[0]].astype(F32)
    refs[-1][...] = total.astype(BF16)


def synthesise(head, *refs):
    recv_refs, (table_ref, grad_ref, out_ref, held_ref) = refs[:-4], refs[-4:]
    lat = lax.axis_index("lat")
    for step, ref in enumerate(recv_refs):
        held_ref[partner(lat, step)] = ref[head:].astype(F32)
    received = held_ref[...].reshape(-1, held_ref.shape[2]).astype(BF16)
    if len(table_ref.shape) == 3:
        spatial = dot(table_ref[...].reshape(received.shape[0], -1), received, 0)
    else:
        spatial = dot(table_ref[...], received)
    rows, lon_count, cols = grad_ref.shape
    result = grad_ref[...].astype(F32) + spatial.reshape(rows, lon_count, cols)
    out_ref[...] = result.astype(BF16)


def gather(axis, piece, *refs):
    block_refs, (out_ref, held_ref) = refs[:-2], refs[-2:]
    me = lax.axis_index(axis)
    for step, ref in enumerate(block_refs):
        held_ref[partner(me, step)] = ref[...].astype(F32)
    for place in range(len(block_refs)):
        out_ref[place * piece : (place + 1) * piece] = held_ref[place, :piece].astype(BF16)


def finish(*refs):
    block_refs, (out_ref, held_ref) = refs[:-2], refs[-2:]
    chan = lax.axis_index("chan")
    for step, ref in enumerate(block_refs):
        held_ref[partner(chan, step)] = ref[...].astype(F32)
    half = held_ref.shape[2]
    for core in range(len(block_refs)):
        out_ref[:, core * half : (core + 1) * half] = held_ref[core]


def call(kernel, outs, operands, scratch=(), in_hbm=False):
    sizes = [math.prod(x.shape) * x.dtype.itemsize for x in (*operands, *outs)]
    sizes += [math.prod(x.shape) * 4 for x in scratch]
    space = pl.BlockSpec(memory_space=pltpu.HBM) if in_hbm else VMEM
    return pl.pallas_call(
        lambda *refs: kernel(*refs),
        out_shape=tuple(outs),
        in_specs=[space] * len(operands),
        out_specs=(VMEM,) * len(outs),
        scratch_shapes=scratch,
        compiler_params=pltpu.CompilerParams(
            vmem_limit_bytes=min(56 << 20, (6 << 20) + 4 * sum(sizes))
        ),
        cost_estimate=pl.CostEstimate(
            flops=1000000, bytes_accessed=2 * sum(sizes), transcendentals=0
        ),
    )(*operands)


def swap(blocks, axis):
    count = len(blocks)
    received = [blocks[0]]
    for step in range(1, count):
        pairs = [(device, partner(device, step)) for device in range(count)]
        received.append(lax.ppermute(blocks[step], axis, pairs))
    return received


def share(block, axis):
    return swap([block] * lax.axis_size(axis), axis)


def shape(*dims, dtype=BF16):
    return jax.ShapeDtypeStruct(dims, dtype)


def on_device(grad_out, pre_act, coeffs, legendre, mixing):
    lat_rows, lon_count, chan_cols = grad_out.shape[1:]
    mode_count = lon_count // 2
    groups = lax.axis_size("lat")
    chan_count = lax.axis_size("chan")
    members = lax.axis_size("ens")
    channels = chan_cols * chan_count
    local_modes, degrees, _ = legendre.shape
    table = analysis_matrix(lat_rows, lon_count, mode_count, groups)
    selections = expansion_tables(
        local_modes, chan_count, degrees, lat_rows, groups, members
    )
    chunk = table.shape[1]
    rows = local_modes * degrees * 2
    share_rows = channels // members
    piece = share_rows // groups
    head = padded(piece, 16)

    flat_legendre = legendre.reshape(local_modes * degrees, -1)
    own_legendre = jnp.stack(share(flat_legendre, "ens"))
    coeffs_parts = share(coeffs.reshape(rows, channels), "chan")

    spectral = call(
        analyse,
        [shape(chunk, chan_cols)] * groups,
        (grad_out[0], pre_act[0], jnp.asarray(table)),
        (
            pltpu.VMEM(grad_out.shape[1:], BF16),
            pltpu.VMEM(grad_out.shape[1:], BF16),
            pltpu.VMEM(table.shape, BF16),
            pltpu.VMEM((groups, chunk, chan_cols), F32),
            pltpu.SemaphoreType.DMA((3,)),
        ),
        in_hbm=True,
    )
    spectral = swap(spectral, "lat")
    spread, halves = call(
        prepare,
        [
            shape(chan_count, rows, groups * chunk),
            shape(chan_count, chan_cols, chan_cols),
        ],
        (*share(own_legendre, "chan"), *(jnp.asarray(x) for x in selections), mixing),
    )

    held = pltpu.VMEM((groups, chunk, chan_cols), F32)
    coef, term_own, *terms = call(
        lambda *refs: coefficients(
            groups, chan_count, members, 1.0 / (members * mode_count), *refs
        ),
        [
            shape(chan_count, rows, chan_cols),
            shape(share_rows, chan_cols, dtype=F32),
            *[shape(share_rows, chan_cols)] * (members - 1),
        ],
        (*spectral, spread, *coeffs_parts),
        (
            held,
            pltpu.VMEM((chan_count, rows, chan_cols), BF16),
            pltpu.VMEM((members, share_rows, chan_cols), F32),
        ),
    )
    terms = swap([term_own, *terms], "ens")
    piece_own, *blocks = call(
        lambda *refs: mix(groups, chan_count, members, piece, *refs),
        [shape(head, chan_cols, dtype=F32), *[shape(head + chunk, chan_cols)] * groups],
        (*share(coef, "chan"), halves, spread, *terms),
        (held, pltpu.VMEM((groups, head, chan_cols), F32)),
    )
    blocks = swap(blocks, "lat")
    (total,) = call(add_pieces, [shape(head, chan_cols)], (piece_own, *blocks[1:]))
    if table.size < 1 << 20:
        back = jnp.asarray(np.ascontiguousarray(table.reshape(-1, lat_rows * lon_count).T))
    else:
        back = jnp.asarray(table)
    (result,) = call(
        lambda *refs: synthesise(head, *refs),
        [shape(*grad_out.shape[1:])],
        (*blocks, back, grad_out[0]),
        (held,),
    )
    (total,) = call(
        lambda *refs: gather("lat", piece, *refs),
        [shape(share_rows, chan_cols)],
        share(total, "lat"),
        (pltpu.VMEM((groups, head, chan_cols), F32),),
    )
    (total,) = call(
        lambda *refs: gather("ens", share_rows, *refs),
        [shape(channels, chan_cols)],
        share(total, "ens"),
        (pltpu.VMEM((members, share_rows, chan_cols), F32),),
    )
    (weight_grad,) = call(
        finish,
        [shape(channels, channels, dtype=F32)],
        share(total, "chan"),
        (pltpu.VMEM((chan_count, channels, chan_cols), F32),),
    )
    return (result[None], weight_grad)


def solution(mesh):
    placed = (
        P(("grp", "ens"), "lat", None, "chan"),
        P(("grp", "ens"), "lat", None, "chan"),
        P(("grp", "ens"), ("lat", "chan"), None, None, None),
        P(("lat", "chan"), None, "ens"),
        P(),
    )
    return jax.shard_map(
        on_device,
        mesh=mesh,
        in_specs=placed,
        out_specs=(P(("grp", "ens"), "lat", None, "chan"), P("grp", None)),
        check_vma=False,
    )
```

```python
import math

import jax
import jax.numpy as jnp
import numpy as np
from jax import lax
from jax.experimental import pallas as pl
from jax.experimental.pallas import tpu as pltpu
from jax.sharding import PartitionSpec as P

VMEM = pl.BlockSpec(memory_space=pltpu.VMEM)
BF16 = jnp.bfloat16
F32 = jnp.float32


def fourier_table(lon_count, mode_count):
    longitude = np.arange(lon_count, dtype=np.int32)[:, None]
    wavenumber = np.arange(mode_count, dtype=np.int32)[None, :]
    product_index = longitude * wavenumber % lon_count
    angles = np.float32(2.0 * math.pi / lon_count) * product_index.astype(np.float32)
    factor = np.float32(math.sqrt(2.0 / lon_count))
    stacked = np.stack([np.cos(angles), -np.sin(angles)], axis=2) * factor
    return stacked.reshape(lon_count, 2 * mode_count).astype(BF16)


def padded(rows, tile):
    return -(-rows // tile) * tile


def analysis_matrix(lat_rows, lon_count, mode_count, groups):
    width = 2 * mode_count // groups
    table = np.asarray(fourier_table(lon_count, mode_count)).astype(np.float32)
    table = table.T.reshape(groups, width, lon_count)
    full = np.zeros((groups, lat_rows, width, lat_rows, lon_count), np.float32)
    for row in range(lat_rows):
        full[:, row, :, row, :] = table
    full = full.reshape(groups, lat_rows * width, lat_rows * lon_count)
    out = np.zeros((groups, padded(lat_rows * width, 8), lat_rows * lon_count), np.float32)
    out[:, : lat_rows * width] = full
    return out.astype(BF16)


def expansion_tables(local_modes, chan_count, degrees, lat_rows, groups, members):
    modes = local_modes * chan_count
    width = 2 * modes
    cols = padded(lat_rows * width, 8)
    lat_count = lat_rows * groups
    row = np.arange(local_modes * degrees * 2)
    pick_rows = row[:, None] // 2 == np.arange(local_modes * degrees)[None, :]
    col = np.arange(groups * cols)
    group, inner = col // cols, col % cols
    valid = inner < lat_rows * width
    lat = group * lat_rows + inner // width
    pick_lat = (np.arange(lat_count)[:, None] == lat[None, :]) & valid[None, :]
    kind_of_row = row // (2 * degrees) * 2 + row % 2
    kind_of_row = kind_of_row[None] + 2 * local_modes * np.arange(chan_count)[:, None]
    kind_of_col = inner % width
    kinds = np.arange(width)
    return (
        pick_rows.astype(BF16),
        pick_lat.reshape(members, lat_count // members, groups * cols).astype(BF16),
        (kind_of_row[:, :, None] == kinds).astype(BF16),
        (kinds[:, None] == kind_of_col[None, :]).astype(BF16),
    )


def partner(me, step):
    return me ^ step


def dot(left, right, left_dim=1, right_dim=0):
    return lax.dot_general(
        left, right, (((left_dim,), (right_dim,)), ((), ())), preferred_element_type=F32
    )


def fold_rows(rows, cols):
    return padded(rows - rows // 2, 8) if cols % 128 == 64 and rows >= 16 else 0


def fold(x):
    rows, cols = x.shape
    side = fold_rows(rows, cols)
    if side == 0:
        return x
    full = cols - 64
    right = x[side:, full:]
    if rows - side < side:
        right = jnp.concatenate([right, jnp.zeros((2 * side - rows, 64), x.dtype)], axis=0)
    tail = jnp.concatenate([x[:side, full:], right], axis=1)
    if full > 128:
        tail = jnp.concatenate([tail, jnp.zeros((side, full - 128), x.dtype)], axis=1)
    return jnp.concatenate([x[:, :full], tail], axis=0)


def unfold(x, rows, cols):
    side = fold_rows(rows, cols)
    if side == 0:
        return x
    tail = x[rows:]
    last = jnp.concatenate([tail[:, :64], tail[: rows - side, 64:128]], axis=0)
    return jnp.concatenate([x[:rows], last], axis=1)


def folded(rows, cols):
    side = fold_rows(rows, cols)
    return shape(rows + side, cols - 64) if side else shape(rows, cols)


def analyse(grad_ref, pre_ref, table_ref, legendre_ref, *refs):
    groups = table_ref.shape[0]
    out_refs, (legendre_out, held_ref) = refs[:groups], refs[groups:]
    legendre_out[...] = legendre_ref[...]
    rows = grad_ref.shape[0] * grad_ref.shape[1]
    values = pre_ref[...].reshape(rows, -1).astype(F32)
    gate = 1.0 / (1.0 + jnp.exp(-values))
    cotangent = grad_ref[...].reshape(rows, -1).astype(F32)
    scaled = (cotangent * gate * (1.0 + values * (1.0 - gate))).astype(BF16)
    table = table_ref[...].reshape(groups * table_ref.shape[1], -1)
    held_ref[...] = dot(table, scaled).reshape(held_ref.shape)
    me = lax.axis_index("lat")
    for step in range(groups):
        out_refs[step][...] = fold(held_ref[partner(me, step)]).astype(BF16)


def prepare(*refs):
    legendre_refs = refs[:-7]
    pick_rows_ref, pick_lat_ref, row_kind_ref, col_kind_ref, mixing_ref = refs[-7:-2]
    spread_ref, mixing_out = refs[-2:]
    chan, ens = lax.axis_index("chan"), lax.axis_index("ens")
    members, chan_count = pick_lat_ref.shape[0], row_kind_ref.shape[0]
    for step in range(chan_count):
        core = partner(chan, step)
        blocks = []
        for mode in range(legendre_refs[0].shape[0]):
            total = None
            for place in range(members):
                part = legendre_refs[step * members + place][mode]
                term = dot(part, pick_lat_ref[partner(ens, place)], 0, 0)
                total = term if total is None else total + term
            blocks.append(total)
        block = jnp.concatenate(blocks, axis=0).astype(BF16)
        keep = dot(row_kind_ref[core], col_kind_ref[...])
        spread_ref[core] = (dot(pick_rows_ref[...], block) * keep).astype(BF16)
    halves, half, _ = mixing_out.shape
    rows = mixing_ref[pl.ds(pl.multiple_of(chan * half, half), half), :]
    for core in range(halves):
        mixing_out[core] = rows[:, core * half : (core + 1) * half]


def coefficients(groups, chan_count, members, scale, *refs):
    recv_refs = refs[:groups]
    spread_ref = refs[groups]
    coeffs_refs = refs[groups + 1 : groups + 1 + chan_count]
    coef_out, term_own, *term_refs = refs[groups + 1 + chan_count : -3]
    held_ref, coef_ref, term_ref = refs[-3:]
    lat, chan, ens = (lax.axis_index(axis) for axis in ("lat", "chan", "ens"))
    _, chunk, cols = held_ref.shape
    for step in range(groups):
        held_ref[partner(lat, step)] = unfold(recv_refs[step][...].astype(F32), chunk, cols)
    block = held_ref[...].reshape(-1, cols).astype(BF16)
    for core in range(chan_count):
        coef = dot(spread_ref[core], block).astype(BF16)
        coef_ref[core] = coef
        coef_out[core] = coef
    term = None
    for step in range(chan_count):
        part = dot(coeffs_refs[step][...], coef_ref[partner(chan, step)], 0, 0)
        term = part if term is None else term + part
    term_ref[...] = (term * scale).reshape(term_ref.shape)
    term_own[...] = term_ref[ens]
    for step in range(1, members):
        term_refs[step - 1][...] = fold(term_ref[partner(ens, step)]).astype(BF16)


def mix(groups, chan_count, *refs):
    coef_refs = refs[:chan_count]
    mixing_ref, spread_ref = refs[chan_count : chan_count + 2]
    send_refs, back_ref = refs[chan_count + 2 : -1], refs[-1]
    lat, chan = lax.axis_index("lat"), lax.axis_index("chan")
    rows = coef_refs[0].shape[0] * coef_refs[0].shape[1]
    mixed = None
    for step in range(chan_count):
        coef = coef_refs[step][...].reshape(rows, -1)
        part = dot(coef, mixing_ref[partner(chan, step)], 1, 1)
        mixed = part if mixed is None else mixed + part
    spread = spread_ref[...].reshape(rows, -1)
    back_ref[...] = dot(spread, mixed.astype(BF16), 0, 0).reshape(back_ref.shape)
    for step in range(groups):
        send_refs[step][...] = fold(back_ref[partner(lat, step)]).astype(BF16)


def add_members(groups, piece, *refs):
    term_ref, recv_refs = refs[0], refs[1 : -1 - groups]
    own_ref, *piece_refs = refs[-1 - groups : -1]
    held_ref = refs[-1]
    lat = lax.axis_index("lat")
    total = term_ref[...]
    for ref in recv_refs:
        total = total + unfold(ref[...].astype(F32), *total.shape)
    for group in range(groups):
        held_ref[group, :piece] = total[group * piece : (group + 1) * piece]
    if piece < held_ref.shape[1]:
        held_ref[:, piece:] = jnp.zeros_like(held_ref[:, piece:])
    own_ref[...] = held_ref[lat]
    for step in range(1, groups):
        piece_refs[step - 1][...] = fold(held_ref[partner(lat, step)]).astype(BF16)


def add_groups(own_ref, *refs):
    total = fold(own_ref[...])
    for ref in refs[:-1]:
        total = total + ref[...].astype(F32)
    refs[-1][...] = total.astype(BF16)


def synthesise(*refs):
    recv_refs, (table_ref, grad_ref, out_ref, held_ref) = refs[:-4], refs[-4:]
    lat = lax.axis_index("lat")
    _, chunk, cols = held_ref.shape
    for step, ref in enumerate(recv_refs):
        held_ref[partner(lat, step)] = unfold(ref[...].astype(F32), chunk, cols)
    received = held_ref[...].reshape(-1, cols).astype(BF16)
    if len(table_ref.shape) == 3:
        spatial = dot(table_ref[...].reshape(received.shape[0], -1), received, 0)
    else:
        spatial = dot(table_ref[...], received)
    result = grad_ref[...].astype(F32) + spatial.reshape(grad_ref.shape)
    out_ref[...] = result.astype(BF16)


def assemble(groups, members, piece, *refs):
    block_refs, (out_ref, held_ref) = refs[: groups * members], refs[-2:]
    lat, ens = lax.axis_index("lat"), lax.axis_index("ens")
    _, head, cols = held_ref.shape
    for step in range(groups):
        for place in range(members):
            target = partner(ens, place) * groups + partner(lat, step)
            block = block_refs[step * members + place][...].astype(F32)
            held_ref[target] = unfold(block, head, cols)
    for place in range(groups * members):
        out_ref[place * piece : (place + 1) * piece] = held_ref[place, :piece].astype(BF16)


def finish(*refs):
    block_refs, (out_ref, held_ref) = refs[:-2], refs[-2:]
    chan = lax.axis_index("chan")
    for step, ref in enumerate(block_refs):
        held_ref[partner(chan, step)] = ref[...].astype(F32)
    half = held_ref.shape[2]
    for core in range(len(block_refs)):
        out_ref[:, core * half : (core + 1) * half] = held_ref[core]


def call(kernel, outs, operands, scratch=(), limit=None, unread=()):
    sizes = [math.prod(x.shape) * x.dtype.itemsize for x in (*operands, *outs)]
    sizes += [math.prod(x.shape) * 4 for x in scratch]
    count = len(operands)
    return pl.pallas_call(
        lambda *refs: kernel(*refs[:count], *refs[count + len(unread) :]),
        out_shape=tuple(outs),
        in_specs=[VMEM] * count + [pl.BlockSpec(memory_space=pl.ANY)] * len(unread),
        out_specs=(VMEM,) * len(outs),
        scratch_shapes=scratch,
        compiler_params=pltpu.CompilerParams(
            vmem_limit_bytes=limit or min(56 << 20, (6 << 20) + 4 * sum(sizes))
        ),
        cost_estimate=pl.CostEstimate(
            flops=1000000, bytes_accessed=2 * sum(sizes), transcendentals=0
        ),
    )(*operands, *unread)


def swap(blocks, axis):
    count = len(blocks)
    received = [blocks[0]]
    for step in range(1, count):
        pairs = [(device, partner(device, step)) for device in range(count)]
        received.append(lax.ppermute(blocks[step], axis, pairs))
    return received


def share(block, axis):
    return swap([block] * lax.axis_size(axis), axis)


def shape(*dims, dtype=BF16):
    return jax.ShapeDtypeStruct(dims, dtype)


def on_device(grad_out, pre_act, coeffs, legendre, mixing):
    lat_rows, lon_count, chan_cols = grad_out.shape[1:]
    mode_count = lon_count // 2
    groups = lax.axis_size("lat")
    chan_count = lax.axis_size("chan")
    members = lax.axis_size("ens")
    channels = chan_cols * chan_count
    local_modes, degrees, _ = legendre.shape
    table = analysis_matrix(lat_rows, lon_count, mode_count, groups)
    selections = expansion_tables(
        local_modes, chan_count, degrees, lat_rows, groups, members
    )
    chunk = table.shape[1]
    rows = local_modes * degrees * 2
    share_rows = channels // members
    piece = share_rows // groups
    head = padded(piece, 16)
    held = pltpu.VMEM((groups, chunk, chan_cols), F32)

    turned = legendre.transpose(0, 2, 1)
    *spectral, turned = call(
        analyse,
        [folded(chunk, chan_cols)] * groups + [shape(*turned.shape)],
        (grad_out[0], pre_act[0], jnp.asarray(table), turned),
        (held,),
        limit=60 << 20,
    )
    spectral = swap(spectral, "lat")
    coeffs_parts = [x.reshape(rows, channels) for x in share(coeffs[0], "chan")]
    own_parts = share(turned, "ens")
    other_parts = [share(part, "chan") for part in own_parts]
    parts = [part[step] for step in range(chan_count) for part in other_parts]
    spread, halves = call(
        prepare,
        [
            shape(chan_count, rows, groups * chunk),
            shape(chan_count, chan_cols, chan_cols),
        ],
        (*parts, *(jnp.asarray(x) for x in selections), mixing),
    )

    coef, term_own, *terms = call(
        lambda *refs: coefficients(
            groups, chan_count, members, 1.0 / (members * mode_count), *refs
        ),
        [
            shape(chan_count, rows, chan_cols),
            shape(share_rows, chan_cols, dtype=F32),
            *[folded(share_rows, chan_cols)] * (members - 1),
        ],
        (*spectral, spread, *coeffs_parts),
        (
            held,
            pltpu.VMEM((chan_count, rows, chan_cols), BF16),
            pltpu.VMEM((members, share_rows, chan_cols), F32),
        ),
    )
    terms = swap([term_own, *terms], "ens")
    blocks = call(
        lambda *refs: mix(groups, chan_count, *refs),
        [folded(chunk, chan_cols)] * groups,
        (*share(coef, "chan"), halves, spread),
        (held,),
    )
    blocks = swap(blocks, "lat")
    pieces = call(
        lambda *refs: add_members(groups, piece, *refs),
        [shape(head, chan_cols, dtype=F32), *[folded(head, chan_cols)] * (groups - 1)],
        terms,
        (pltpu.VMEM((groups, head, chan_cols), F32),),
    )
    pieces = swap(pieces, "lat")
    (total,) = call(add_groups, [folded(head, chan_cols)], pieces)
    if table.size < 1 << 20:
        back = jnp.asarray(np.ascontiguousarray(table.reshape(-1, lat_rows * lon_count).T))
    else:
        back = jnp.asarray(table)
    (result,) = call(
        synthesise,
        [shape(*grad_out.shape[1:])],
        (*blocks, back, grad_out[0]),
        (held,),
    )
    everywhere = [block for part in share(total, "lat") for block in share(part, "ens")]
    (total,) = call(
        lambda *refs: assemble(groups, members, piece, *refs),
        [shape(channels, chan_cols)],
        everywhere,
        (pltpu.VMEM((groups * members, head, chan_cols), F32),),
        unread=(result,),
    )
    (weight_grad,) = call(
        finish,
        [shape(channels, channels, dtype=F32)],
        share(total, "chan"),
        (pltpu.VMEM((chan_count, channels, chan_cols), F32),),
    )
    return (result[None], weight_grad)


def solution(mesh):
    placed = (
        P(("grp", "ens"), "lat", None, "chan"),
        P(("grp", "ens"), "lat", None, "chan"),
        P(("grp", "ens"), ("lat", "chan"), None, None, None),
        P(("lat", "chan"), None, "ens"),
        P(),
    )
    return jax.shard_map(
        on_device,
        mesh=mesh,
        in_specs=placed,
        out_specs=(P(("grp", "ens"), "lat", None, "chan"), P("grp", None)),
        check_vma=False,
    )
```

```python
import math

import jax
import jax.numpy as jnp
import numpy as np
from jax import lax
from jax.experimental import pallas as pl
from jax.experimental.pallas import tpu as pltpu
from jax.sharding import PartitionSpec as P

VMEM = pl.BlockSpec(memory_space=pltpu.VMEM)
BF16 = jnp.bfloat16
F32 = jnp.float32


def fourier_table(lon_count, mode_count):
    longitude = np.arange(lon_count, dtype=np.int32)[:, None]
    wavenumber = np.arange(mode_count, dtype=np.int32)[None, :]
    product_index = longitude * wavenumber % lon_count
    angles = np.float32(2.0 * math.pi / lon_count) * product_index.astype(np.float32)
    factor = np.float32(math.sqrt(2.0 / lon_count))
    stacked = np.stack([np.cos(angles), -np.sin(angles)], axis=2) * factor
    return stacked.reshape(lon_count, 2 * mode_count).astype(BF16)


def padded(rows, tile):
    return -(-rows // tile) * tile


def analysis_matrix(lat_rows, lon_count, mode_count, groups):
    width = 2 * mode_count // groups
    table = np.asarray(fourier_table(lon_count, mode_count)).astype(np.float32)
    table = table.T.reshape(groups, width, lon_count)
    full = np.zeros((groups, lat_rows, width, lat_rows, lon_count), np.float32)
    for row in range(lat_rows):
        full[:, row, :, row, :] = table
    full = full.reshape(groups, lat_rows * width, lat_rows * lon_count)
    out = np.zeros((groups, padded(lat_rows * width, 8), lat_rows * lon_count), np.float32)
    out[:, : lat_rows * width] = full
    return out.astype(BF16)


def expansion_tables(local_modes, chan_count, degrees, lat_rows, groups, members):
    modes = local_modes * chan_count
    width = 2 * modes
    cols = padded(lat_rows * width, 8)
    lat_count = lat_rows * groups
    row = np.arange(local_modes * degrees * 2)
    pick_rows = row[:, None] // 2 == np.arange(local_modes * degrees)[None, :]
    col = np.arange(groups * cols)
    group, inner = col // cols, col % cols
    valid = inner < lat_rows * width
    lat = group * lat_rows + inner // width
    pick_lat = (np.arange(lat_count)[:, None] == lat[None, :]) & valid[None, :]
    kind_of_row = row // (2 * degrees) * 2 + row % 2
    kind_of_row = kind_of_row[None] + 2 * local_modes * np.arange(chan_count)[:, None]
    kind_of_col = inner % width
    kinds = np.arange(width)
    return (
        pick_rows.astype(BF16),
        pick_lat.reshape(members, lat_count // members, groups * cols).astype(BF16),
        (kind_of_row[:, :, None] == kinds).astype(BF16),
        (kinds[:, None] == kind_of_col[None, :]).astype(BF16),
    )


def partner(me, step):
    return me ^ step


def dot(left, right, left_dim=1, right_dim=0):
    return lax.dot_general(
        left, right, (((left_dim,), (right_dim,)), ((), ())), preferred_element_type=F32
    )


def fold_rows(rows, cols):
    return padded(rows - rows // 2, 8) if cols % 128 == 64 and rows >= 16 else 0


def fold(x):
    rows, cols = x.shape
    side = fold_rows(rows, cols)
    if side == 0:
        return x
    full = cols - 64
    right = x[side:, full:]
    if rows - side < side:
        right = jnp.concatenate([right, jnp.zeros((2 * side - rows, 64), x.dtype)], axis=0)
    tail = jnp.concatenate([x[:side, full:], right], axis=1)
    if full > 128:
        tail = jnp.concatenate([tail, jnp.zeros((side, full - 128), x.dtype)], axis=1)
    return jnp.concatenate([x[:, :full], tail], axis=0)


def unfold(x, rows, cols):
    side = fold_rows(rows, cols)
    if side == 0:
        return x
    tail = x[rows:]
    last = jnp.concatenate([tail[:, :64], tail[: rows - side, 64:128]], axis=0)
    return jnp.concatenate([x[:rows], last], axis=1)


def folded(rows, cols):
    side = fold_rows(rows, cols)
    return shape(rows + side, cols - 64) if side else shape(rows, cols)


def analyse(grad_ref, pre_ref, table_ref, *refs):
    groups = table_ref.shape[0]
    out_refs, held_ref = refs[:groups], refs[groups]
    rows = grad_ref.shape[0] * grad_ref.shape[1]
    values = pre_ref[...].reshape(rows, -1).astype(F32)
    gate = 1.0 / (1.0 + jnp.exp(-values))
    cotangent = grad_ref[...].reshape(rows, -1).astype(F32)
    scaled = (cotangent * gate * (1.0 + values * (1.0 - gate))).astype(BF16)
    table = table_ref[...].reshape(groups * table_ref.shape[1], -1)
    held_ref[...] = dot(table, scaled).reshape(held_ref.shape)
    me = lax.axis_index("lat")
    for step in range(groups):
        out_refs[step][...] = fold(held_ref[partner(me, step)]).astype(BF16)


def prepare(*refs):
    legendre_refs = refs[:-7]
    pick_rows_ref, pick_lat_ref, row_kind_ref, col_kind_ref, mixing_ref = refs[-7:-2]
    spread_ref, mixing_out = refs[-2:]
    chan, ens = lax.axis_index("chan"), lax.axis_index("ens")
    members, chan_count = pick_lat_ref.shape[0], row_kind_ref.shape[0]
    for step in range(chan_count):
        core = partner(chan, step)
        blocks = []
        for mode in range(legendre_refs[0].shape[0]):
            total = None
            for place in range(members):
                part = legendre_refs[step * members + place][mode]
                term = dot(part, pick_lat_ref[partner(ens, place)], 0, 0)
                total = term if total is None else total + term
            blocks.append(total)
        block = jnp.concatenate(blocks, axis=0).astype(BF16)
        keep = dot(row_kind_ref[core], col_kind_ref[...])
        spread_ref[core] = (dot(pick_rows_ref[...], block) * keep).astype(BF16)
    halves, half, _ = mixing_out.shape
    rows = mixing_ref[pl.ds(pl.multiple_of(chan * half, half), half), :]
    for core in range(halves):
        mixing_out[core] = rows[:, core * half : (core + 1) * half]


def coefficients(groups, chan_count, piece, scale, *refs):
    recv_refs = refs[:groups]
    spread_ref = refs[groups]
    coeffs_refs = refs[groups + 1 : groups + 1 + chan_count]
    coef_out, term_out, held_ref, coef_ref = refs[groups + 1 + chan_count :]
    lat, chan = lax.axis_index("lat"), lax.axis_index("chan")
    _, chunk, cols = held_ref.shape
    for step in range(groups):
        held_ref[partner(lat, step)] = unfold(recv_refs[step][...].astype(F32), chunk, cols)
    block = held_ref[...].reshape(-1, cols).astype(BF16)
    for core in range(chan_count):
        coef = dot(spread_ref[core], block).astype(BF16)
        coef_ref[core] = coef
        coef_out[core] = coef
    term = None
    for step in range(chan_count):
        part = dot(coeffs_refs[step][...], coef_ref[partner(chan, step)], 0, 0)
        term = part if term is None else term + part
    term = term * scale
    if piece < term_out.shape[1]:
        term_out[:, piece:] = jnp.zeros_like(term_out[:, piece:])
    for group in range(groups):
        term_out[group, :piece] = term[group * piece : (group + 1) * piece]


def mix(groups, chan_count, *refs):
    coef_refs = refs[:chan_count]
    mixing_ref, spread_ref, term_ref = refs[chan_count : chan_count + 3]
    own_ref, *send_refs, back_ref = refs[chan_count + 3 :]
    lat, chan = lax.axis_index("lat"), lax.axis_index("chan")
    rows = coef_refs[0].shape[0] * coef_refs[0].shape[1]
    mixed = None
    for step in range(chan_count):
        coef = coef_refs[step][...].reshape(rows, -1)
        part = dot(coef, mixing_ref[partner(chan, step)], 1, 1)
        mixed = part if mixed is None else mixed + part
    spread = spread_ref[...].reshape(rows, -1)
    back_ref[...] = dot(spread, mixed.astype(BF16), 0, 0).reshape(back_ref.shape)
    own_ref[...] = fold(back_ref[lat]).astype(BF16)
    for step in range(1, groups):
        target = partner(lat, step)
        term = fold(term_ref[target]).astype(BF16)
        send_refs[step - 1][: term.shape[0]] = term
        send_refs[step - 1][term.shape[0] :] = fold(back_ref[target]).astype(BF16)


def add_groups(term_ref, *refs):
    total = fold(term_ref[lax.axis_index("lat")])
    for ref in refs[:-1]:
        total = total + ref[: total.shape[0]].astype(F32)
    refs[-1][...] = total.astype(BF16)


def add_members(*refs):
    term_refs, (out_ref, held_ref) = refs[:-2], refs[-2:]
    ens = lax.axis_index("ens")
    for step, ref in enumerate(term_refs):
        held_ref[partner(ens, step)] = ref[...].astype(F32)
    total = held_ref[0]
    for member in range(1, len(term_refs)):
        total = total + held_ref[member]
    out_ref[...] = total.astype(BF16)


def synthesise(*refs):
    recv_refs, (table_ref, grad_ref, out_ref, held_ref) = refs[:-4], refs[-4:]
    lat = lax.axis_index("lat")
    _, chunk, cols = held_ref.shape
    size = recv_refs[0].shape[0]
    for step, ref in enumerate(recv_refs):
        block = ref[ref.shape[0] - size :].astype(F32)
        held_ref[partner(lat, step)] = unfold(block, chunk, cols)
    received = held_ref[...].reshape(-1, cols).astype(BF16)
    if len(table_ref.shape) == 3:
        spatial = dot(table_ref[...].reshape(received.shape[0], -1), received, 0)
    else:
        spatial = dot(table_ref[...], received)
    result = grad_ref[...].astype(F32) + spatial.reshape(grad_ref.shape)
    out_ref[...] = result.astype(BF16)


def assemble(piece, *refs):
    block_refs, (out_ref, held_ref) = refs[:-2], refs[-2:]
    lat = lax.axis_index("lat")
    _, head, cols = held_ref.shape
    for step, ref in enumerate(block_refs):
        held_ref[partner(lat, step)] = unfold(ref[...].astype(F32), head, cols)
    for group in range(len(block_refs)):
        out_ref[group * piece : (group + 1) * piece] = held_ref[group, :piece].astype(BF16)


def finish(*refs):
    block_refs, (out_ref, held_ref) = refs[:-2], refs[-2:]
    chan = lax.axis_index("chan")
    for step, ref in enumerate(block_refs):
        held_ref[partner(chan, step)] = ref[...].astype(F32)
    half = held_ref.shape[2]
    for core in range(len(block_refs)):
        out_ref[:, core * half : (core + 1) * half] = held_ref[core]


def call(kernel, outs, operands, scratch=(), limit=None):
    sizes = [math.prod(x.shape) * x.dtype.itemsize for x in (*operands, *outs)]
    sizes += [math.prod(x.shape) * 4 for x in scratch]
    return pl.pallas_call(
        lambda *refs: kernel(*refs),
        out_shape=tuple(outs),
        in_specs=[VMEM] * len(operands),
        out_specs=(VMEM,) * len(outs),
        scratch_shapes=scratch,
        compiler_params=pltpu.CompilerParams(
            vmem_limit_bytes=limit or min(56 << 20, (6 << 20) + 4 * sum(sizes))
        ),
        cost_estimate=pl.CostEstimate(
            flops=1000000, bytes_accessed=2 * sum(sizes), transcendentals=0
        ),
    )(*operands)


def swap(blocks, axis):
    count = len(blocks)
    received = [blocks[0]]
    for step in range(1, count):
        pairs = [(device, partner(device, step)) for device in range(count)]
        received.append(lax.ppermute(blocks[step], axis, pairs))
    return received


def share(block, axis):
    return swap([block] * lax.axis_size(axis), axis)


def shape(*dims, dtype=BF16):
    return jax.ShapeDtypeStruct(dims, dtype)


def on_device(grad_out, pre_act, coeffs, legendre, mixing):
    lat_rows, lon_count, chan_cols = grad_out.shape[1:]
    mode_count = lon_count // 2
    groups = lax.axis_size("lat")
    chan_count = lax.axis_size("chan")
    members = lax.axis_size("ens")
    channels = chan_cols * chan_count
    local_modes, degrees, _ = legendre.shape
    table = analysis_matrix(lat_rows, lon_count, mode_count, groups)
    selections = expansion_tables(
        local_modes, chan_count, degrees, lat_rows, groups, members
    )
    chunk = table.shape[1]
    rows = local_modes * degrees * 2
    piece = channels // groups
    head = padded(piece, 32)
    held = pltpu.VMEM((groups, chunk, chan_cols), F32)
    part = folded(head, chan_cols)
    side = folded(chunk, chan_cols)
    both = shape(part.shape[0] + side.shape[0], side.shape[1])

    own_parts = share(legendre.transpose(0, 2, 1), "ens")
    spectral = call(
        analyse,
        [side] * groups,
        (grad_out[0], pre_act[0], jnp.asarray(table)),
        (held,),
        limit=60 << 20,
    )
    spectral = swap(spectral, "lat")
    coeffs_parts = [x.reshape(rows, channels) for x in share(coeffs[0], "chan")]
    other_parts = [share(own, "chan") for own in own_parts]
    parts = [other[step] for step in range(chan_count) for other in other_parts]
    spread, halves = call(
        prepare,
        [
            shape(chan_count, rows, groups * chunk),
            shape(chan_count, chan_cols, chan_cols),
        ],
        (*parts, *(jnp.asarray(x) for x in selections), mixing),
    )

    coef, term = call(
        lambda *refs: coefficients(
            groups, chan_count, piece, 1.0 / (members * mode_count), *refs
        ),
        [shape(chan_count, rows, chan_cols), shape(groups, head, chan_cols, dtype=F32)],
        (*spectral, spread, *coeffs_parts),
        (held, pltpu.VMEM((chan_count, rows, chan_cols), BF16)),
    )
    blocks = call(
        lambda *refs: mix(groups, chan_count, *refs),
        [side, *[both] * (groups - 1)],
        (*share(coef, "chan"), halves, spread, term),
        (held,),
    )
    blocks = swap(blocks, "lat")
    (total,) = call(add_groups, [part], (term, *blocks[1:]))
    (total,) = call(
        add_members,
        [part],
        share(total, "ens"),
        (pltpu.VMEM((members, *part.shape), F32),),
    )
    if table.size < 1 << 20:
        back = jnp.asarray(np.ascontiguousarray(table.reshape(-1, lat_rows * lon_count).T))
    else:
        back = jnp.asarray(table)
    (result,) = call(
        synthesise,
        [shape(*grad_out.shape[1:])],
        (*blocks, back, grad_out[0]),
        (held,),
    )
    (total,) = call(
        lambda *refs: assemble(piece, *refs),
        [shape(channels, chan_cols)],
        share(total, "lat"),
        (pltpu.VMEM((groups, head, chan_cols), F32),),
    )
    (weight_grad,) = call(
        finish,
        [shape(channels, channels, dtype=F32)],
        share(total, "chan"),
        (pltpu.VMEM((chan_count, channels, chan_cols), F32),),
    )
    return (result[None], weight_grad)


def solution(mesh):
    placed = (
        P(("grp", "ens"), "lat", None, "chan"),
        P(("grp", "ens"), "lat", None, "chan"),
        P(("grp", "ens"), ("lat", "chan"), None, None, None),
        P(("lat", "chan"), None, "ens"),
        P(),
    )
    return jax.shard_map(
        on_device,
        mesh=mesh,
        in_specs=placed,
        out_specs=(P(("grp", "ens"), "lat", None, "chan"), P("grp", None)),
        check_vma=False,
    )
```

```python
import math

import jax
import jax.numpy as jnp
import numpy as np
from jax import lax
from jax.experimental import pallas as pl
from jax.experimental.pallas import tpu as pltpu
from jax.sharding import PartitionSpec as P

VMEM = pl.BlockSpec(memory_space=pltpu.VMEM)
BF16 = jnp.bfloat16
F32 = jnp.float32


def fourier_table(lon_count, mode_count):
    longitude = np.arange(lon_count, dtype=np.int32)[:, None]
    wavenumber = np.arange(mode_count, dtype=np.int32)[None, :]
    product_index = longitude * wavenumber % lon_count
    angles = np.float32(2.0 * math.pi / lon_count) * product_index.astype(np.float32)
    factor = np.float32(math.sqrt(2.0 / lon_count))
    stacked = np.stack([np.cos(angles), -np.sin(angles)], axis=2) * factor
    return stacked.reshape(lon_count, 2 * mode_count).astype(BF16)


def padded(rows, tile):
    return -(-rows // tile) * tile


def analysis_matrix(lat_rows, lon_count, mode_count, groups):
    width = 2 * mode_count // groups
    table = np.asarray(fourier_table(lon_count, mode_count)).astype(np.float32)
    table = table.T.reshape(groups, width, lon_count)
    full = np.zeros((groups, lat_rows, width, lat_rows, lon_count), np.float32)
    for row in range(lat_rows):
        full[:, row, :, row, :] = table
    full = full.reshape(groups, lat_rows * width, lat_rows * lon_count)
    out = np.zeros((groups, padded(lat_rows * width, 8), lat_rows * lon_count), np.float32)
    out[:, : lat_rows * width] = full
    return out.astype(BF16)


def expansion_tables(local_modes, chan_count, degrees, lat_rows, groups, members):
    modes = local_modes * chan_count
    width = 2 * modes
    cols = padded(lat_rows * width, 8)
    lat_count = lat_rows * groups
    row = np.arange(local_modes * degrees * 2)
    pick_rows = row[:, None] // 2 == np.arange(local_modes * degrees)[None, :]
    col = np.arange(groups * cols)
    group, inner = col // cols, col % cols
    valid = inner < lat_rows * width
    lat = group * lat_rows + inner // width
    pick_lat = (np.arange(lat_count)[:, None] == lat[None, :]) & valid[None, :]
    kind_of_row = row // (2 * degrees) * 2 + row % 2
    kind_of_row = kind_of_row[None] + 2 * local_modes * np.arange(chan_count)[:, None]
    kind_of_col = inner % width
    kinds = np.arange(width)
    return (
        pick_rows.astype(BF16),
        pick_lat.reshape(members, lat_count // members, groups * cols).astype(BF16),
        (kind_of_row[:, :, None] == kinds).astype(BF16),
        (kinds[:, None] == kind_of_col[None, :]).astype(BF16),
    )


def partner(me, step):
    return me ^ step


def dot(left, right, left_dim=1, right_dim=0):
    return lax.dot_general(
        left, right, (((left_dim,), (right_dim,)), ((), ())), preferred_element_type=F32
    )


def fold_rows(rows, cols):
    return padded(rows - rows // 2, 8) if cols % 128 == 64 and rows >= 16 else 0


def fold(x):
    rows, cols = x.shape
    side = fold_rows(rows, cols)
    if side == 0:
        return x
    full = cols - 64
    right = x[side:, full:]
    if rows - side < side:
        right = jnp.concatenate([right, jnp.zeros((2 * side - rows, 64), x.dtype)], axis=0)
    tail = jnp.concatenate([x[:side, full:], right], axis=1)
    if full > 128:
        tail = jnp.concatenate([tail, jnp.zeros((side, full - 128), x.dtype)], axis=1)
    return jnp.concatenate([x[:, :full], tail], axis=0)


def unfold(x, rows, cols):
    side = fold_rows(rows, cols)
    if side == 0:
        return x
    tail = x[rows:]
    last = jnp.concatenate([tail[:, :64], tail[: rows - side, 64:128]], axis=0)
    return jnp.concatenate([x[:rows], last], axis=1)


def folded(rows, cols):
    side = fold_rows(rows, cols)
    return shape(rows + side, cols - 64) if side else shape(rows, cols)


def analyse(grad_ref, pre_ref, table_ref, *refs):
    groups = table_ref.shape[0]
    out_refs, held_ref = refs[:groups], refs[groups]
    rows = grad_ref.shape[0] * grad_ref.shape[1]
    values = pre_ref[...].reshape(rows, -1).astype(F32)
    gate = 1.0 / (1.0 + jnp.exp(-values))
    cotangent = grad_ref[...].reshape(rows, -1).astype(F32)
    scaled = (cotangent * gate * (1.0 + values * (1.0 - gate))).astype(BF16)
    table = table_ref[...].reshape(groups * table_ref.shape[1], -1)
    held_ref[...] = dot(table, scaled).reshape(held_ref.shape)
    me = lax.axis_index("lat")
    for step in range(groups):
        out_refs[step][...] = fold(held_ref[partner(me, step)]).astype(BF16)


def prepare(*refs):
    legendre_refs = refs[:-7]
    pick_rows_ref, pick_lat_ref, row_kind_ref, col_kind_ref, mixing_ref = refs[-7:-2]
    spread_ref, mixing_out = refs[-2:]
    chan, ens = lax.axis_index("chan"), lax.axis_index("ens")
    for step, legendre_ref in enumerate(legendre_refs):
        core = partner(chan, step)
        blocks = []
        for mode in range(legendre_ref.shape[1]):
            total = None
            for place in range(legendre_ref.shape[0]):
                pick = pick_lat_ref[partner(ens, place)]
                term = dot(legendre_ref[place, mode], pick, 0, 0)
                total = term if total is None else total + term
            blocks.append(total)
        block = jnp.concatenate(blocks, axis=0).astype(BF16)
        keep = dot(row_kind_ref[core], col_kind_ref[...])
        spread_ref[core] = (dot(pick_rows_ref[...], block) * keep).astype(BF16)
    cores, _, half = mixing_out.shape
    for core in range(cores):
        mixing_out[core] = mixing_ref[:, core * half : (core + 1) * half]


def coefficients(groups, chan_count, scale, *refs):
    recv_refs = refs[:groups]
    spread_ref = refs[groups]
    coeffs_refs = refs[groups + 1 : groups + 1 + chan_count]
    coef_out, term_out, swap_out, held_ref, coef_ref = refs[groups + 1 + chan_count :]
    lat, chan = lax.axis_index("lat"), lax.axis_index("chan")
    _, chunk, cols = held_ref.shape
    for step in range(groups):
        held_ref[partner(lat, step)] = unfold(recv_refs[step][...].astype(F32), chunk, cols)
    block = held_ref[...].reshape(-1, cols).astype(BF16)
    rows = spread_ref.shape[1]
    for core in range(chan_count):
        coef_ref[core] = dot(spread_ref[core], block).astype(BF16)
    coef_out[...] = coef_ref[...].reshape(coef_out.shape)
    term = None
    for step in range(chan_count):
        part = dot(coeffs_refs[step][...], coef_ref[partner(chan, step)], 0, 0)
        term = part if term is None else term + part
    term_out[...] = term * scale

    @pl.when(chan == 0)
    def _():
        swap_out[: term_out.shape[0]] = term_out[...].astype(BF16)

    @pl.when(chan != 0)
    def _():
        swap_out[: coef_out.shape[0]] = coef_out[...]


def mix(groups, piece, *refs):
    coef_ref, term_ref, swap_ref, mixing_ref, spread_ref = refs[:5]
    back_out, piece_out, *send_refs = refs[5:-2]
    back_ref, pieces_ref = refs[-2:]
    lat, chan = lax.axis_index("lat"), lax.axis_index("chan")
    rows, half = coef_ref.shape
    chunk, head = back_ref.shape[1], pieces_ref.shape[1]

    @pl.when(chan == 0)
    def _():
        mixed = dot(coef_ref[...], mixing_ref[0], 1, 1)
        mixed = mixed + dot(swap_ref[:rows], mixing_ref[1], 1, 1)
        spread = spread_ref[...].reshape(rows, -1)
        back_ref[...] = dot(spread, mixed.astype(BF16), 0, 0).reshape(back_ref.shape)
        back_out[...] = back_ref[lat].astype(BF16)
        for step in range(1, groups):
            send_refs[step - 1][:chunk] = back_ref[partner(lat, step)].astype(BF16)

    @pl.when(chan != 0)
    def _():
        if piece < head:
            pieces_ref[...] = jnp.zeros_like(pieces_ref)
        for group in range(groups):
            part = slice(group * piece, (group + 1) * piece)
            pieces_ref[group, :piece, :half] = swap_ref[: term_ref.shape[0]].astype(F32)[part]
            pieces_ref[group, :piece, half:] = term_ref[part]
        piece_out[...] = pieces_ref[lat]
        for step in range(1, groups):
            send_refs[step - 1][:head] = pieces_ref[partner(lat, step)].astype(BF16)


def add_groups(piece_ref, *refs):
    total = piece_ref[...]
    for ref in refs[:-1]:
        total = total + ref[: total.shape[0]].astype(F32)
    refs[-1][...] = total.astype(BF16)


def add_members(*refs):
    term_refs, (out_ref, held_ref) = refs[:-2], refs[-2:]
    ens = lax.axis_index("ens")
    for step, ref in enumerate(term_refs):
        held_ref[partner(ens, step)] = ref[...].astype(F32)
    total = held_ref[0]
    for member in range(1, len(term_refs)):
        total = total + held_ref[member]
    out_ref[...] = total.astype(BF16)


def collect(*refs):
    own_ref, *recv_refs = refs[:-3]
    first_out, last_out, held_ref = refs[-3:]
    lat = lax.axis_index("lat")
    _, chunk, cols = held_ref.shape
    held_ref[lat] = own_ref[...].astype(F32)
    for step, ref in enumerate(recv_refs):
        held_ref[partner(lat, step + 1)] = ref[...].astype(F32)[:chunk]
    received = held_ref[...].reshape(-1, cols)
    first_out[...] = received[:, : cols // 2].astype(BF16)
    last_out[...] = received[:, cols // 2 :].astype(BF16)


def synthesise(own_ref, swap_ref, table_ref, grad_ref, out_ref, held_ref):
    chan = lax.axis_index("chan")

    @pl.when(chan == 0)
    def _():
        held_ref[...] = own_ref[...]

    @pl.when(chan != 0)
    def _():
        held_ref[...] = swap_ref[...]

    received = held_ref[...]
    if len(table_ref.shape) == 3:
        spatial = dot(table_ref[...].reshape(received.shape[0], -1), received, 0)
    else:
        spatial = dot(table_ref[...], received)
    result = grad_ref[...].astype(F32) + spatial.reshape(grad_ref.shape)
    out_ref[...] = result.astype(BF16)


def assemble(piece, *refs):
    block_refs, (out_ref, held_ref) = refs[:-2], refs[-2:]
    lat = lax.axis_index("lat")
    for step, ref in enumerate(block_refs):
        held_ref[partner(lat, step)] = ref[...].astype(F32)
    for group in range(len(block_refs)):
        out_ref[group * piece : (group + 1) * piece] = held_ref[group, :piece].astype(BF16)


def finish(own_ref, swap_ref, out_ref):
    chan = lax.axis_index("chan")

    @pl.when(chan == 0)
    def _():
        out_ref[...] = swap_ref[...].astype(F32)

    @pl.when(chan != 0)
    def _():
        out_ref[...] = own_ref[...].astype(F32)


def call(kernel, outs, operands, scratch=(), limit=None):
    sizes = [math.prod(x.shape) * x.dtype.itemsize for x in (*operands, *outs)]
    sizes += [math.prod(x.shape) * 4 for x in scratch]
    return pl.pallas_call(
        lambda *refs: kernel(*refs),
        out_shape=tuple(outs),
        in_specs=[VMEM] * len(operands),
        out_specs=(VMEM,) * len(outs),
        scratch_shapes=scratch,
        compiler_params=pltpu.CompilerParams(
            vmem_limit_bytes=limit or min(56 << 20, (6 << 20) + 4 * sum(sizes))
        ),
        cost_estimate=pl.CostEstimate(
            flops=1000000, bytes_accessed=2 * sum(sizes), transcendentals=0
        ),
    )(*operands)


def swap(blocks, axis):
    count = len(blocks)
    received = [blocks[0]]
    for step in range(1, count):
        pairs = [(device, partner(device, step)) for device in range(count)]
        received.append(lax.ppermute(blocks[step], axis, pairs))
    return received


def share(block, axis):
    return swap([block] * lax.axis_size(axis), axis)


def share_last(block, axis):
    count, cores = lax.axis_size(axis), lax.axis_size("chan")
    if axis == "lat":
        axes, place = ("lat", "chan"), lambda device: device * cores + cores - 1
    else:
        axes, place = ("chan", axis), lambda device: (cores - 1) * count + device
    received = [block]
    for step in range(1, count):
        pairs = [(place(device), place(partner(device, step))) for device in range(count)]
        received.append(lax.ppermute(block, axes, pairs))
    return received


def shape(*dims, dtype=BF16):
    return jax.ShapeDtypeStruct(dims, dtype)


def on_device(grad_out, pre_act, coeffs, legendre, mixing):
    lat_rows, lon_count, chan_cols = grad_out.shape[1:]
    mode_count = lon_count // 2
    groups = lax.axis_size("lat")
    chan_count = lax.axis_size("chan")
    members = lax.axis_size("ens")
    channels = chan_cols * chan_count
    local_modes, degrees, _ = legendre.shape
    table = analysis_matrix(lat_rows, lon_count, mode_count, groups)
    selections = expansion_tables(
        local_modes, chan_count, degrees, lat_rows, groups, members
    )
    chunk = table.shape[1]
    rows = local_modes * degrees * 2
    piece = channels // groups
    head = padded(piece, 16)
    side = folded(chunk, chan_cols)
    both = shape(padded(max(chunk, head), 16), channels)

    own_legendre = jnp.stack(share(legendre.transpose(0, 2, 1), "ens"))
    spectral = call(
        analyse,
        [side] * groups,
        (grad_out[0], pre_act[0], jnp.asarray(table)),
        (pltpu.VMEM((groups, chunk, chan_cols), F32),),
        limit=60 << 20,
    )
    spectral = swap(spectral, "lat")
    coeffs_parts = [x.reshape(rows, channels) for x in share(coeffs[0], "chan")]
    spread, mixing_parts = call(
        prepare,
        [
            shape(chan_count, rows, groups * chunk),
            shape(chan_count, channels, chan_cols),
        ],
        (*share(own_legendre, "chan"), *(jnp.asarray(x) for x in selections), mixing),
    )

    coef_rows = chan_count * rows
    coef, term, handed = call(
        lambda *refs: coefficients(groups, chan_count, 1.0 / (members * mode_count), *refs),
        [
            shape(coef_rows, chan_cols),
            shape(channels, chan_cols, dtype=F32),
            shape(max(coef_rows, channels), chan_cols),
        ],
        (*spectral, spread, *coeffs_parts),
        (
            pltpu.VMEM((groups, chunk, chan_cols), F32),
            pltpu.VMEM((chan_count, rows, chan_cols), BF16),
        ),
    )
    handed = lax.ppermute(handed, "chan", [(0, 1), (1, 0)])
    returned, own_piece, *blocks = call(
        lambda *refs: mix(groups, piece, *refs),
        [
            shape(chunk, channels),
            shape(head, channels, dtype=F32),
            *[both] * (groups - 1),
        ],
        (coef, term, handed, mixing_parts, spread),
        (
            pltpu.VMEM((groups, chunk, channels), F32),
            pltpu.VMEM((groups, head, channels), F32),
        ),
    )
    blocks = swap([returned, *blocks], "lat")[1:]
    (total,) = call(add_groups, [shape(head, channels)], (own_piece, *blocks))
    (total,) = call(
        add_members,
        [shape(head, channels)],
        share_last(total, "ens"),
        (pltpu.VMEM((members, head, channels), F32),),
    )
    if table.size < 1 << 20:
        back = jnp.asarray(np.ascontiguousarray(table.reshape(-1, lat_rows * lon_count).T))
    else:
        back = jnp.asarray(table)
    half = shape(groups * chunk, chan_cols)
    first, last = call(
        collect,
        [half, half],
        (returned, *blocks),
        (pltpu.VMEM((groups, chunk, channels), F32),),
    )
    (result,) = call(
        synthesise,
        [shape(*grad_out.shape[1:])],
        (first, lax.ppermute(last, "chan", [(0, 1)]), back, grad_out[0]),
        (pltpu.VMEM(half.shape, BF16),),
    )
    (total,) = call(
        lambda *refs: assemble(piece, *refs),
        [shape(channels, channels)],
        share_last(total, "lat"),
        (pltpu.VMEM((groups, head, channels), F32),),
    )
    (weight_grad,) = call(
        finish,
        [shape(channels, channels, dtype=F32)],
        (total, lax.ppermute(total, "chan", [(1, 0)])),
    )
    return (result[None], weight_grad)


def solution(mesh):
    placed = (
        P(("grp", "ens"), "lat", None, "chan"),
        P(("grp", "ens"), "lat", None, "chan"),
        P(("grp", "ens"), ("lat", "chan"), None, None, None),
        P(("lat", "chan"), None, "ens"),
        P(),
    )
    return jax.shard_map(
        on_device,
        mesh=mesh,
        in_specs=placed,
        out_specs=(P(("grp", "ens"), "lat", None, "chan"), P("grp", None)),
        check_vma=False,
    )
```

```python
import math

import jax
import jax.numpy as jnp
import numpy as np
from jax import lax
from jax.experimental import pallas as pl
from jax.experimental.pallas import tpu as pltpu
from jax.sharding import PartitionSpec as P

VMEM = pl.BlockSpec(memory_space=pltpu.VMEM)
BF16 = jnp.bfloat16
F32 = jnp.float32


def fourier_table(lon_count, mode_count):
    longitude = np.arange(lon_count, dtype=np.int32)[:, None]
    wavenumber = np.arange(mode_count, dtype=np.int32)[None, :]
    product_index = longitude * wavenumber % lon_count
    angles = np.float32(2.0 * math.pi / lon_count) * product_index.astype(np.float32)
    factor = np.float32(math.sqrt(2.0 / lon_count))
    stacked = np.stack([np.cos(angles), -np.sin(angles)], axis=2) * factor
    return stacked.reshape(lon_count, 2 * mode_count).astype(BF16)


def padded(rows, tile):
    return -(-rows // tile) * tile


def analysis_matrix(lat_rows, lon_count, mode_count, groups):
    width = 2 * mode_count // groups
    table = np.asarray(fourier_table(lon_count, mode_count)).astype(np.float32)
    table = table.T.reshape(groups, width, lon_count)
    full = np.zeros((groups, lat_rows, width, lat_rows, lon_count), np.float32)
    for row in range(lat_rows):
        full[:, row, :, row, :] = table
    full = full.reshape(groups, lat_rows * width, lat_rows * lon_count)
    out = np.zeros((groups, padded(lat_rows * width, 8), lat_rows * lon_count), np.float32)
    out[:, : lat_rows * width] = full
    return out.astype(BF16)


def expansion_tables(local_modes, chan_count, degrees, lat_rows, groups, members):
    modes = local_modes * chan_count
    width = 2 * modes
    cols = padded(lat_rows * width, 8)
    lat_count = lat_rows * groups
    row = np.arange(local_modes * degrees * 2)
    pick_rows = row[:, None] // 2 == np.arange(local_modes * degrees)[None, :]
    col = np.arange(groups * cols)
    group, inner = col // cols, col % cols
    valid = inner < lat_rows * width
    lat = group * lat_rows + inner // width
    pick_lat = (np.arange(lat_count)[:, None] == lat[None, :]) & valid[None, :]
    kind_of_row = row // (2 * degrees) * 2 + row % 2
    kind_of_row = kind_of_row[None] + 2 * local_modes * np.arange(chan_count)[:, None]
    kind_of_col = inner % width
    kinds = np.arange(width)
    return (
        pick_rows.astype(BF16),
        pick_lat.reshape(members, lat_count // members, groups * cols).astype(BF16),
        (kind_of_row[:, :, None] == kinds).astype(BF16),
        (kinds[:, None] == kind_of_col[None, :]).astype(BF16),
    )


def partner(me, step):
    return me ^ step


def dot(left, right, left_dim=1, right_dim=0):
    return lax.dot_general(
        left, right, (((left_dim,), (right_dim,)), ((), ())), preferred_element_type=F32
    )


def fold_rows(rows, cols):
    return padded(rows - rows // 2, 8) if cols % 128 == 64 and rows >= 16 else 0


def fold(x):
    rows, cols = x.shape
    side = fold_rows(rows, cols)
    if side == 0:
        return x
    full = cols - 64
    right = x[side:, full:]
    if rows - side < side:
        right = jnp.concatenate([right, jnp.zeros((2 * side - rows, 64), x.dtype)], axis=0)
    tail = jnp.concatenate([x[:side, full:], right], axis=1)
    if full > 128:
        tail = jnp.concatenate([tail, jnp.zeros((side, full - 128), x.dtype)], axis=1)
    return jnp.concatenate([x[:, :full], tail], axis=0)


def unfold(x, rows, cols):
    side = fold_rows(rows, cols)
    if side == 0:
        return x
    tail = x[rows:]
    last = jnp.concatenate([tail[:, :64], tail[: rows - side, 64:128]], axis=0)
    return jnp.concatenate([x[:rows], last], axis=1)


def folded(rows, cols):
    side = fold_rows(rows, cols)
    return shape(rows + side, cols - 64) if side else shape(rows, cols)


def analyse(grad_ref, pre_ref, table_ref, *refs):
    groups = table_ref.shape[0]
    out_refs, held_ref = refs[:groups], refs[groups]
    rows = grad_ref.shape[0] * grad_ref.shape[1]
    values = pre_ref[...].reshape(rows, -1).astype(F32)
    gate = 1.0 / (1.0 + jnp.exp(-values))
    cotangent = grad_ref[...].reshape(rows, -1).astype(F32)
    scaled = (cotangent * gate * (1.0 + values * (1.0 - gate))).astype(BF16)
    table = table_ref[...].reshape(groups * table_ref.shape[1], -1)
    held_ref[...] = dot(table, scaled).reshape(held_ref.shape)
    me = lax.axis_index("lat")
    for step in range(groups):
        out_refs[step][...] = fold(held_ref[partner(me, step)]).astype(BF16)


def prepare(*refs):
    legendre_refs = refs[:-7]
    pick_rows_ref, pick_lat_ref, row_kind_ref, col_kind_ref, mixing_ref = refs[-7:-2]
    spread_ref, mixing_out = refs[-2:]
    chan, ens = lax.axis_index("chan"), lax.axis_index("ens")
    for step, legendre_ref in enumerate(legendre_refs):
        core = partner(chan, step)
        blocks = []
        for mode in range(legendre_ref.shape[1]):
            total = None
            for place in range(legendre_ref.shape[0]):
                pick = pick_lat_ref[partner(ens, place)]
                term = dot(legendre_ref[place, mode], pick, 0, 0)
                total = term if total is None else total + term
            blocks.append(total)
        block = jnp.concatenate(blocks, axis=0).astype(BF16)
        keep = dot(row_kind_ref[core], col_kind_ref[...])
        spread_ref[core] = (dot(pick_rows_ref[...], block) * keep).astype(BF16)
    cores, _, half = mixing_out.shape
    for core in range(cores):
        mixing_out[core] = mixing_ref[:, core * half : (core + 1) * half]


def coefficients(groups, chan_count, scale, *refs):
    recv_refs = refs[:groups]
    spread_ref = refs[groups]
    coeffs_refs = refs[groups + 1 : groups + 1 + chan_count]
    coef_out, term_out, swap_out, held_ref, coef_ref = refs[groups + 1 + chan_count :]
    lat, chan = lax.axis_index("lat"), lax.axis_index("chan")
    _, chunk, cols = held_ref.shape
    for step in range(groups):
        held_ref[partner(lat, step)] = unfold(recv_refs[step][...].astype(F32), chunk, cols)
    block = held_ref[...].reshape(-1, cols).astype(BF16)
    rows = spread_ref.shape[1]
    for core in range(chan_count):
        coef_ref[core] = dot(spread_ref[core], block).astype(BF16)
    coef_out[...] = coef_ref[...].reshape(coef_out.shape)
    term = None
    for step in range(chan_count):
        part = dot(coeffs_refs[step][...], coef_ref[partner(chan, step)], 0, 0)
        term = part if term is None else term + part
    term_out[...] = term * scale

    @pl.when(chan == 0)
    def _():
        swap_out[: term_out.shape[0]] = term_out[...].astype(BF16)

    @pl.when(chan != 0)
    def _():
        swap_out[: coef_out.shape[0]] = coef_out[...]


def mix(groups, piece, *refs):
    coef_ref, term_ref, swap_ref, mixing_ref, spread_ref = refs[:5]
    back_out, piece_out, *send_refs = refs[5:-2]
    back_ref, pieces_ref = refs[-2:]
    lat, chan = lax.axis_index("lat"), lax.axis_index("chan")
    rows, half = coef_ref.shape
    chunk, head = back_ref.shape[1], pieces_ref.shape[1]

    @pl.when(chan == 0)
    def _():
        mixed = dot(coef_ref[...], mixing_ref[0], 1, 1)
        mixed = mixed + dot(swap_ref[:rows], mixing_ref[1], 1, 1)
        spread = spread_ref[...].reshape(rows, -1)
        back_ref[...] = dot(spread, mixed.astype(BF16), 0, 0).reshape(back_ref.shape)
        back_out[...] = back_ref[lat].astype(BF16)
        for step in range(1, groups):
            send_refs[step - 1][:chunk] = back_ref[partner(lat, step)].astype(BF16)

    @pl.when(chan != 0)
    def _():
        if piece < head:
            pieces_ref[...] = jnp.zeros_like(pieces_ref)
        for group in range(groups):
            part = slice(group * piece, (group + 1) * piece)
            pieces_ref[group, :piece, :half] = swap_ref[: term_ref.shape[0]].astype(F32)[part]
            pieces_ref[group, :piece, half:] = term_ref[part]
        piece_out[...] = pieces_ref[lat]
        for step in range(1, groups):
            send_refs[step - 1][:head] = pieces_ref[partner(lat, step)].astype(BF16)


def add_groups(piece_ref, own_ref, *refs):
    recv_refs, (piece_out, first_out, last_out, held_ref) = refs[:-4], refs[-4:]
    lat, chan = lax.axis_index("lat"), lax.axis_index("chan")
    _, chunk, cols = held_ref.shape

    @pl.when(chan == 0)
    def _():
        held_ref[lat] = own_ref[...].astype(F32)
        for step, ref in enumerate(recv_refs):
            held_ref[partner(lat, step + 1)] = ref[...].astype(F32)[:chunk]
        received = held_ref[...].reshape(-1, cols)
        first_out[...] = received[:, : cols // 2].astype(BF16)
        last_out[...] = received[:, cols // 2 :].astype(BF16)

    @pl.when(chan != 0)
    def _():
        total = piece_ref[...]
        for ref in recv_refs:
            total = total + ref[: total.shape[0]].astype(F32)
        piece_out[...] = total.astype(BF16)


def add_members(*refs):
    term_refs, (out_ref, held_ref) = refs[:-2], refs[-2:]
    ens = lax.axis_index("ens")
    for step, ref in enumerate(term_refs):
        held_ref[partner(ens, step)] = ref[...].astype(F32)
    total = held_ref[0]
    for member in range(1, len(term_refs)):
        total = total + held_ref[member]
    out_ref[...] = total.astype(BF16)


def synthesise(own_ref, swap_ref, table_ref, grad_ref, out_ref, held_ref):
    chan = lax.axis_index("chan")

    @pl.when(chan == 0)
    def _():
        held_ref[...] = own_ref[...]

    @pl.when(chan != 0)
    def _():
        held_ref[...] = swap_ref[...]

    received = held_ref[...]
    if len(table_ref.shape) == 3:
        spatial = dot(table_ref[...].reshape(received.shape[0], -1), received, 0)
    else:
        spatial = dot(table_ref[...], received)
    result = grad_ref[...].astype(F32) + spatial.reshape(grad_ref.shape)
    out_ref[...] = result.astype(BF16)


def assemble(piece, *refs):
    block_refs, (out_ref, held_ref) = refs[:-2], refs[-2:]
    lat = lax.axis_index("lat")
    for step, ref in enumerate(block_refs):
        held_ref[partner(lat, step)] = ref[...].astype(F32)
    for group in range(len(block_refs)):
        out_ref[group * piece : (group + 1) * piece] = held_ref[group, :piece].astype(BF16)


def finish(own_ref, swap_ref, out_ref):
    chan = lax.axis_index("chan")

    @pl.when(chan == 0)
    def _():
        out_ref[...] = swap_ref[...].astype(F32)

    @pl.when(chan != 0)
    def _():
        out_ref[...] = own_ref[...].astype(F32)


def call(kernel, outs, operands, scratch=(), limit=None):
    sizes = [math.prod(x.shape) * x.dtype.itemsize for x in (*operands, *outs)]
    sizes += [math.prod(x.shape) * 4 for x in scratch]
    return pl.pallas_call(
        lambda *refs: kernel(*refs),
        out_shape=tuple(outs),
        in_specs=[VMEM] * len(operands),
        out_specs=(VMEM,) * len(outs),
        scratch_shapes=scratch,
        compiler_params=pltpu.CompilerParams(
            vmem_limit_bytes=limit or min(56 << 20, (6 << 20) + 4 * sum(sizes))
        ),
        cost_estimate=pl.CostEstimate(
            flops=1000000, bytes_accessed=2 * sum(sizes), transcendentals=0
        ),
    )(*operands)


def swap(blocks, axis):
    count = len(blocks)
    received = [blocks[0]]
    for step in range(1, count):
        pairs = [(device, partner(device, step)) for device in range(count)]
        received.append(lax.ppermute(blocks[step], axis, pairs))
    return received


def share(block, axis):
    return swap([block] * lax.axis_size(axis), axis)


def share_last(block, axis):
    count, cores = lax.axis_size(axis), lax.axis_size("chan")
    if axis == "lat":
        axes, place = ("lat", "chan"), lambda device: device * cores + cores - 1
    else:
        axes, place = ("chan", axis), lambda device: (cores - 1) * count + device
    received = [block]
    for step in range(1, count):
        pairs = {device: device for device in range(count * cores)}
        pairs.update((place(device), place(partner(device, step))) for device in range(count))
        received.append(lax.ppermute(block, axes, sorted(pairs.items())))
    return received


def shape(*dims, dtype=BF16):
    return jax.ShapeDtypeStruct(dims, dtype)


def on_device(grad_out, pre_act, coeffs, legendre, mixing):
    lat_rows, lon_count, chan_cols = grad_out.shape[1:]
    mode_count = lon_count // 2
    groups = lax.axis_size("lat")
    chan_count = lax.axis_size("chan")
    members = lax.axis_size("ens")
    channels = chan_cols * chan_count
    local_modes, degrees, _ = legendre.shape
    table = analysis_matrix(lat_rows, lon_count, mode_count, groups)
    selections = expansion_tables(
        local_modes, chan_count, degrees, lat_rows, groups, members
    )
    chunk = table.shape[1]
    rows = local_modes * degrees * 2
    piece = channels // groups
    head = padded(piece, 16)
    side = folded(chunk, chan_cols)
    both = shape(padded(max(chunk, head), 16), channels)

    own_legendre = jnp.stack(share(legendre.transpose(0, 2, 1), "ens"))
    spectral = call(
        analyse,
        [side] * groups,
        (grad_out[0], pre_act[0], jnp.asarray(table)),
        (pltpu.VMEM((groups, chunk, chan_cols), F32),),
        limit=60 << 20,
    )
    spectral = swap(spectral, "lat")
    coeffs_parts = [x.reshape(rows, channels) for x in share(coeffs[0], "chan")]
    spread, mixing_parts = call(
        prepare,
        [
            shape(chan_count, rows, groups * chunk),
            shape(chan_count, channels, chan_cols),
        ],
        (*share(own_legendre, "chan"), *(jnp.asarray(x) for x in selections), mixing),
    )

    coef_rows = chan_count * rows
    coef, term, handed = call(
        lambda *refs: coefficients(groups, chan_count, 1.0 / (members * mode_count), *refs),
        [
            shape(coef_rows, chan_cols),
            shape(channels, chan_cols, dtype=F32),
            shape(max(coef_rows, channels), chan_cols),
        ],
        (*spectral, spread, *coeffs_parts),
        (
            pltpu.VMEM((groups, chunk, chan_cols), F32),
            pltpu.VMEM((chan_count, rows, chan_cols), BF16),
        ),
    )
    handed = lax.ppermute(handed, "chan", [(0, 1), (1, 0)])
    returned, own_piece, *blocks = call(
        lambda *refs: mix(groups, piece, *refs),
        [
            shape(chunk, channels),
            shape(head, channels, dtype=F32),
            *[both] * (groups - 1),
        ],
        (coef, term, handed, mixing_parts, spread),
        (
            pltpu.VMEM((groups, chunk, channels), F32),
            pltpu.VMEM((groups, head, channels), F32),
        ),
    )
    blocks = swap([returned, *blocks], "lat")[1:]
    half = shape(groups * chunk, chan_cols)
    total, first, last = call(
        add_groups,
        [shape(head, channels), half, half],
        (own_piece, returned, *blocks),
        (pltpu.VMEM((groups, chunk, channels), F32),),
    )
    (total,) = call(
        add_members,
        [shape(head, channels)],
        share_last(total, "ens"),
        (pltpu.VMEM((members, head, channels), F32),),
    )
    if table.size < 1 << 20:
        back = jnp.asarray(np.ascontiguousarray(table.reshape(-1, lat_rows * lon_count).T))
    else:
        back = jnp.asarray(table)
    (result,) = call(
        synthesise,
        [shape(*grad_out.shape[1:])],
        (first, lax.ppermute(last, "chan", [(0, 1), (1, 0)]), back, grad_out[0]),
        (pltpu.VMEM(half.shape, BF16),),
    )
    (total,) = call(
        lambda *refs: assemble(piece, *refs),
        [shape(channels, channels)],
        share_last(total, "lat"),
        (pltpu.VMEM((groups, head, channels), F32),),
    )
    (weight_grad,) = call(
        finish,
        [shape(channels, channels, dtype=F32)],
        (total, lax.ppermute(total, "chan", [(0, 1), (1, 0)])),
    )
    return (result[None], weight_grad)


def solution(mesh):
    placed = (
        P(("grp", "ens"), "lat", None, "chan"),
        P(("grp", "ens"), "lat", None, "chan"),
        P(("grp", "ens"), ("lat", "chan"), None, None, None),
        P(("lat", "chan"), None, "ens"),
        P(),
    )
    return jax.shard_map(
        on_device,
        mesh=mesh,
        in_specs=placed,
        out_specs=(P(("grp", "ens"), "lat", None, "chan"), P("grp", None)),
        check_vma=False,
    )
```

```python
import math

import jax
import jax.numpy as jnp
import numpy as np
from jax import lax
from jax.experimental import pallas as pl
from jax.experimental.pallas import tpu as pltpu
from jax.sharding import PartitionSpec as P

VMEM = pl.BlockSpec(memory_space=pltpu.VMEM)
BF16 = jnp.bfloat16
F32 = jnp.float32


def fourier_table(lon_count, mode_count):
    longitude = np.arange(lon_count, dtype=np.int32)[:, None]
    wavenumber = np.arange(mode_count, dtype=np.int32)[None, :]
    product_index = longitude * wavenumber % lon_count
    angles = np.float32(2.0 * math.pi / lon_count) * product_index.astype(np.float32)
    factor = np.float32(math.sqrt(2.0 / lon_count))
    stacked = np.stack([np.cos(angles), -np.sin(angles)], axis=2) * factor
    return stacked.reshape(lon_count, 2 * mode_count).astype(BF16)


def padded(rows, tile):
    return -(-rows // tile) * tile


def analysis_matrix(lat_rows, lon_count, mode_count, groups):
    width = 2 * mode_count // groups
    table = np.asarray(fourier_table(lon_count, mode_count)).astype(np.float32)
    table = table.T.reshape(groups, width, lon_count)
    full = np.zeros((groups, lat_rows, width, lat_rows, lon_count), np.float32)
    for row in range(lat_rows):
        full[:, row, :, row, :] = table
    full = full.reshape(groups, lat_rows * width, lat_rows * lon_count)
    out = np.zeros((groups, padded(lat_rows * width, 8), lat_rows * lon_count), np.float32)
    out[:, : lat_rows * width] = full
    return out.astype(BF16)


def expansion_tables(local_modes, chan_count, degrees, lat_rows, groups, members):
    modes = local_modes * chan_count
    width = 2 * modes
    cols = padded(lat_rows * width, 8)
    lat_count = lat_rows * groups
    row = np.arange(local_modes * degrees * 2)
    pick_rows = row[:, None] // 2 == np.arange(local_modes * degrees)[None, :]
    col = np.arange(groups * cols)
    group, inner = col // cols, col % cols
    valid = inner < lat_rows * width
    lat = group * lat_rows + inner // width
    pick_lat = (np.arange(lat_count)[:, None] == lat[None, :]) & valid[None, :]
    kind_of_row = row // (2 * degrees) * 2 + row % 2
    kind_of_row = kind_of_row[None] + 2 * local_modes * np.arange(chan_count)[:, None]
    kind_of_col = inner % width
    kinds = np.arange(width)
    return (
        pick_rows.astype(BF16),
        pick_lat.reshape(members, lat_count // members, groups * cols).astype(BF16),
        (kind_of_row[:, :, None] == kinds).astype(BF16),
        (kinds[:, None] == kind_of_col[None, :]).astype(BF16),
    )


def partner(me, step):
    return me ^ step


def dot(left, right, left_dim=1, right_dim=0):
    return lax.dot_general(
        left, right, (((left_dim,), (right_dim,)), ((), ())), preferred_element_type=F32
    )


def fold_rows(rows, cols):
    return padded(rows - rows // 2, 8) if cols % 128 == 64 and rows >= 16 else 0


def fold(x):
    rows, cols = x.shape
    side = fold_rows(rows, cols)
    if side == 0:
        return x
    full = cols - 64
    right = x[side:, full:]
    if rows - side < side:
        right = jnp.concatenate([right, jnp.zeros((2 * side - rows, 64), x.dtype)], axis=0)
    tail = jnp.concatenate([x[:side, full:], right], axis=1)
    if full > 128:
        tail = jnp.concatenate([tail, jnp.zeros((side, full - 128), x.dtype)], axis=1)
    return jnp.concatenate([x[:, :full], tail], axis=0)


def unfold(x, rows, cols):
    side = fold_rows(rows, cols)
    if side == 0:
        return x
    tail = x[rows:]
    last = jnp.concatenate([tail[:, :64], tail[: rows - side, 64:128]], axis=0)
    return jnp.concatenate([x[:rows], last], axis=1)


def folded(rows, cols):
    side = fold_rows(rows, cols)
    return shape(rows + side, cols - 64) if side else shape(rows, cols)


def silu_backward(cotangent, preact):
    values = preact.astype(F32)
    gate = 1.0 / (1.0 + jnp.exp(-values))
    return (cotangent.astype(F32) * gate * (1.0 + values * (1.0 - gate))).astype(BF16)


def analyse(scaled_ref, table_ref, *refs):
    groups = table_ref.shape[0]
    out_refs, held_ref = refs[:groups], refs[groups]
    scaled = scaled_ref[...].reshape(-1, scaled_ref.shape[2])
    table = table_ref[...].reshape(groups * table_ref.shape[1], -1)
    held_ref[...] = dot(table, scaled).reshape(held_ref.shape)
    me = lax.axis_index("lat")
    for step in range(groups):
        out_refs[step][...] = fold(held_ref[partner(me, step)]).astype(BF16)


def prepare(*refs):
    legendre_refs = refs[:-7]
    pick_rows_ref, pick_lat_ref, row_kind_ref, col_kind_ref, mixing_ref = refs[-7:-2]
    spread_ref, mixing_out = refs[-2:]
    chan, ens = lax.axis_index("chan"), lax.axis_index("ens")
    for step in range(row_kind_ref.shape[0]):
        core = partner(chan, step)
        blocks = []
        for mode in range(legendre_refs[0].shape[1]):
            total = None
            for place, legendre_ref in enumerate(legendre_refs):
                pick = pick_lat_ref[partner(ens, place)]
                term = dot(legendre_ref[step, mode], pick, 0, 0)
                total = term if total is None else total + term
            blocks.append(total)
        block = jnp.concatenate(blocks, axis=0).astype(BF16)
        keep = dot(row_kind_ref[core], col_kind_ref[...])
        spread_ref[core] = (dot(pick_rows_ref[...], block) * keep).astype(BF16)
    halves, half, _ = mixing_out.shape
    rows = mixing_ref[pl.ds(pl.multiple_of(chan * half, half), half), :]
    for core in range(halves):
        mixing_out[core] = rows[:, core * half : (core + 1) * half]


def coefficients(groups, chan_count, piece, scale, *refs):
    recv_refs = refs[:groups]
    spread_ref = refs[groups]
    coeffs_refs = refs[groups + 1 : groups + 1 + chan_count]
    coef_out, term_out, held_ref, coef_ref = refs[groups + 1 + chan_count :]
    lat, chan = lax.axis_index("lat"), lax.axis_index("chan")
    _, chunk, cols = held_ref.shape
    for step in range(groups):
        held_ref[partner(lat, step)] = unfold(recv_refs[step][...].astype(F32), chunk, cols)
    block = held_ref[...].reshape(-1, cols).astype(BF16)
    for core in range(chan_count):
        coef = dot(spread_ref[core], block).astype(BF16)
        coef_ref[core] = coef
        coef_out[core] = coef
    term = None
    for step in range(chan_count):
        part = dot(coeffs_refs[step][...], coef_ref[partner(chan, step)], 0, 0)
        term = part if term is None else term + part
    term = term * scale
    if piece < term_out.shape[1]:
        term_out[:, piece:] = jnp.zeros_like(term_out[:, piece:])
    for group in range(groups):
        term_out[group, :piece] = term[group * piece : (group + 1) * piece]


def mix(groups, chan_count, *refs):
    coef_refs = refs[:chan_count]
    mixing_ref, spread_ref, term_ref = refs[chan_count : chan_count + 3]
    own_ref, *send_refs, back_ref = refs[chan_count + 3 :]
    lat, chan = lax.axis_index("lat"), lax.axis_index("chan")
    rows = coef_refs[0].shape[0] * coef_refs[0].shape[1]
    mixed = None
    for step in range(chan_count):
        coef = coef_refs[step][...].reshape(rows, -1)
        part = dot(coef, mixing_ref[partner(chan, step)], 1, 1)
        mixed = part if mixed is None else mixed + part
    spread = spread_ref[...].reshape(rows, -1)
    back_ref[...] = dot(spread, mixed.astype(BF16), 0, 0).reshape(back_ref.shape)
    own_ref[...] = fold(back_ref[lat]).astype(BF16)
    for step in range(1, groups):
        target = partner(lat, step)
        term = fold(term_ref[target]).astype(BF16)
        send_refs[step - 1][: term.shape[0]] = term
        send_refs[step - 1][term.shape[0] :] = fold(back_ref[target]).astype(BF16)


def add_groups(term_ref, *refs):
    total = fold(term_ref[lax.axis_index("lat")])
    for ref in refs[:-1]:
        total = total + ref[: total.shape[0]].astype(F32)
    refs[-1][...] = total.astype(BF16)


def add_members(*refs):
    term_refs, (out_ref, held_ref) = refs[:-2], refs[-2:]
    ens = lax.axis_index("ens")
    for step, ref in enumerate(term_refs):
        held_ref[partner(ens, step)] = ref[...].astype(F32)
    total = held_ref[0]
    for member in range(1, len(term_refs)):
        total = total + held_ref[member]
    out_ref[...] = total.astype(BF16)


def synthesise(*refs):
    recv_refs, (table_ref, grad_ref, out_ref, held_ref) = refs[:-4], refs[-4:]
    lat = lax.axis_index("lat")
    _, chunk, cols = held_ref.shape
    size = recv_refs[0].shape[0]
    for step, ref in enumerate(recv_refs):
        block = ref[ref.shape[0] - size :].astype(F32)
        held_ref[partner(lat, step)] = unfold(block, chunk, cols)
    received = held_ref[...].reshape(-1, cols).astype(BF16)
    if len(table_ref.shape) == 3:
        spatial = dot(table_ref[...].reshape(received.shape[0], -1), received, 0)
    else:
        spatial = dot(table_ref[...], received)
    result = grad_ref[...].astype(F32) + spatial.reshape(grad_ref.shape)
    out_ref[...] = result.astype(BF16)


def assemble(piece, *refs):
    block_refs, (out_ref, held_ref) = refs[:-2], refs[-2:]
    lat = lax.axis_index("lat")
    _, head, cols = held_ref.shape
    for step, ref in enumerate(block_refs):
        held_ref[partner(lat, step)] = unfold(ref[...].astype(F32), head, cols)
    for group in range(len(block_refs)):
        out_ref[group * piece : (group + 1) * piece] = held_ref[group, :piece].astype(BF16)


def finish(*refs):
    block_refs, (out_ref, held_ref) = refs[:-2], refs[-2:]
    chan = lax.axis_index("chan")
    for step, ref in enumerate(block_refs):
        held_ref[partner(chan, step)] = ref[...].astype(F32)
    half = held_ref.shape[2]
    for core in range(len(block_refs)):
        out_ref[:, core * half : (core + 1) * half] = held_ref[core]


def call(kernel, outs, operands, scratch=(), limit=None):
    sizes = [math.prod(x.shape) * x.dtype.itemsize for x in (*operands, *outs)]
    sizes += [math.prod(x.shape) * 4 for x in scratch]
    return pl.pallas_call(
        lambda *refs: kernel(*refs),
        out_shape=tuple(outs),
        in_specs=[VMEM] * len(operands),
        out_specs=(VMEM,) * len(outs),
        scratch_shapes=scratch,
        compiler_params=pltpu.CompilerParams(
            vmem_limit_bytes=limit or min(56 << 20, (6 << 20) + 4 * sum(sizes))
        ),
        cost_estimate=pl.CostEstimate(
            flops=1000000, bytes_accessed=2 * sum(sizes), transcendentals=0
        ),
    )(*operands)


def swap(blocks, axis):
    count = len(blocks)
    received = {0: blocks[0]}
    for step in reversed(range(1, count)):
        pairs = [(device, partner(device, step)) for device in range(count)]
        received[step] = lax.ppermute(blocks[step], axis, pairs)
    return [received[step] for step in range(count)]


def share(block, axis):
    return swap([block] * lax.axis_size(axis), axis)


def shape(*dims, dtype=BF16):
    return jax.ShapeDtypeStruct(dims, dtype)


def on_device(grad_out, pre_act, coeffs, legendre, mixing):
    lat_rows, lon_count, chan_cols = grad_out.shape[1:]
    mode_count = lon_count // 2
    groups = lax.axis_size("lat")
    chan_count = lax.axis_size("chan")
    members = lax.axis_size("ens")
    channels = chan_cols * chan_count
    local_modes, degrees, _ = legendre.shape
    table = analysis_matrix(lat_rows, lon_count, mode_count, groups)
    selections = expansion_tables(
        local_modes, chan_count, degrees, lat_rows, groups, members
    )
    chunk = table.shape[1]
    rows = local_modes * degrees * 2
    piece = channels // groups
    head = padded(piece, 32)
    held = pltpu.VMEM((groups, chunk, chan_cols), F32)
    part = folded(head, chan_cols)
    side = folded(chunk, chan_cols)
    both = shape(part.shape[0] + side.shape[0], side.shape[1])

    legendre_parts = share(jnp.stack(share(legendre.transpose(0, 2, 1), "chan")), "ens")
    spectral = call(
        analyse,
        [side] * groups,
        (silu_backward(grad_out[0], pre_act[0]), jnp.asarray(table)),
        (held,),
    )
    spectral = swap(spectral, "lat")
    coeffs_parts = [x.reshape(rows, channels) for x in share(coeffs[0], "chan")]
    spread, halves = call(
        prepare,
        [
            shape(chan_count, rows, groups * chunk),
            shape(chan_count, chan_cols, chan_cols),
        ],
        (*legendre_parts, *(jnp.asarray(x) for x in selections), mixing),
    )

    coef, term = call(
        lambda *refs: coefficients(
            groups, chan_count, piece, 1.0 / (members * mode_count), *refs
        ),
        [shape(chan_count, rows, chan_cols), shape(groups, head, chan_cols, dtype=F32)],
        (*spectral, spread, *coeffs_parts),
        (held, pltpu.VMEM((chan_count, rows, chan_cols), BF16)),
    )
    blocks = call(
        lambda *refs: mix(groups, chan_count, *refs),
        [side, *[both] * (groups - 1)],
        (*share(coef, "chan"), halves, spread, term),
        (held,),
    )
    blocks = swap(blocks, "lat")
    (total,) = call(add_groups, [part], (term, *blocks[1:]))
    (total,) = call(
        add_members,
        [part],
        share(total, "ens"),
        (pltpu.VMEM((members, *part.shape), F32),),
    )
    if table.size < 1 << 20:
        back = jnp.asarray(np.ascontiguousarray(table.reshape(-1, lat_rows * lon_count).T))
    else:
        back = jnp.asarray(table)
    (result,) = call(
        synthesise,
        [shape(*grad_out.shape[1:])],
        (*blocks, back, grad_out[0]),
        (held,),
    )
    (total,) = call(
        lambda *refs: assemble(piece, *refs),
        [shape(channels, chan_cols)],
        share(total, "lat"),
        (pltpu.VMEM((groups, head, chan_cols), F32),),
    )
    (weight_grad,) = call(
        finish,
        [shape(channels, channels, dtype=F32)],
        share(total, "chan"),
        (pltpu.VMEM((chan_count, channels, chan_cols), F32),),
    )
    return (result[None], weight_grad)


def solution(mesh):
    placed = (
        P(("grp", "ens"), "lat", None, "chan"),
        P(("grp", "ens"), "lat", None, "chan"),
        P(("grp", "ens"), ("lat", "chan"), None, None, None),
        P(("lat", "chan"), None, "ens"),
        P(),
    )
    return jax.shard_map(
        on_device,
        mesh=mesh,
        in_specs=placed,
        out_specs=(P(("grp", "ens"), "lat", None, "chan"), P("grp", None)),
        check_vma=False,
    )
```

```python
import math

import jax
import jax.numpy as jnp
import numpy as np
from jax import lax
from jax.experimental import pallas as pl
from jax.experimental.pallas import tpu as pltpu
from jax.sharding import PartitionSpec as P

VMEM = pl.BlockSpec(memory_space=pltpu.VMEM)
BF16 = jnp.bfloat16
F32 = jnp.float32


def fourier_table(lon_count, mode_count):
    longitude = np.arange(lon_count, dtype=np.int32)[:, None]
    wavenumber = np.arange(mode_count, dtype=np.int32)[None, :]
    product_index = longitude * wavenumber % lon_count
    angles = np.float32(2.0 * math.pi / lon_count) * product_index.astype(np.float32)
    factor = np.float32(math.sqrt(2.0 / lon_count))
    stacked = np.stack([np.cos(angles), -np.sin(angles)], axis=2) * factor
    return stacked.reshape(lon_count, 2 * mode_count).astype(BF16)


def padded(rows, tile):
    return -(-rows // tile) * tile


def analysis_matrix(lat_rows, lon_count, mode_count, groups):
    width = 2 * mode_count // groups
    table = np.asarray(fourier_table(lon_count, mode_count)).astype(np.float32)
    table = table.T.reshape(groups, width, lon_count)
    full = np.zeros((groups, lat_rows, width, lat_rows, lon_count), np.float32)
    for row in range(lat_rows):
        full[:, row, :, row, :] = table
    full = full.reshape(groups, lat_rows * width, lat_rows * lon_count)
    out = np.zeros((groups, padded(lat_rows * width, 8), lat_rows * lon_count), np.float32)
    out[:, : lat_rows * width] = full
    return out.astype(BF16)


def expansion_tables(local_modes, chan_count, degrees, lat_rows, groups, members):
    modes = local_modes * chan_count
    width = 2 * modes
    cols = padded(lat_rows * width, 8)
    lat_count = lat_rows * groups
    row = np.arange(local_modes * degrees * 2)
    pick_rows = row[:, None] // 2 == np.arange(local_modes * degrees)[None, :]
    col = np.arange(groups * cols)
    group, inner = col // cols, col % cols
    valid = inner < lat_rows * width
    lat = group * lat_rows + inner // width
    pick_lat = (np.arange(lat_count)[:, None] == lat[None, :]) & valid[None, :]
    kind_of_row = row // (2 * degrees) * 2 + row % 2
    kind_of_row = kind_of_row[None] + 2 * local_modes * np.arange(chan_count)[:, None]
    kind_of_col = inner % width
    kinds = np.arange(width)
    return (
        pick_rows.astype(BF16),
        pick_lat.reshape(members, lat_count // members, groups * cols).astype(BF16),
        (kind_of_row[:, :, None] == kinds).astype(BF16),
        (kinds[:, None] == kind_of_col[None, :]).astype(BF16),
    )


def partner(me, step, count=0):
    return me ^ (count - step if step > 0 and count > 0 else step)


def dot(left, right, left_dim=1, right_dim=0):
    return lax.dot_general(
        left, right, (((left_dim,), (right_dim,)), ((), ())), preferred_element_type=F32
    )


def fold_rows(rows, cols):
    return padded(rows - rows // 2, 8) if cols % 128 == 64 and rows >= 16 else 0


def fold(x):
    rows, cols = x.shape
    side = fold_rows(rows, cols)
    if side == 0:
        return x
    full = cols - 64
    right = x[side:, full:]
    if rows - side < side:
        right = jnp.concatenate([right, jnp.zeros((2 * side - rows, 64), x.dtype)], axis=0)
    tail = jnp.concatenate([x[:side, full:], right], axis=1)
    if full > 128:
        tail = jnp.concatenate([tail, jnp.zeros((side, full - 128), x.dtype)], axis=1)
    return jnp.concatenate([x[:, :full], tail], axis=0)


def unfold(x, rows, cols):
    side = fold_rows(rows, cols)
    if side == 0:
        return x
    tail = x[rows:]
    last = jnp.concatenate([tail[:, :64], tail[: rows - side, 64:128]], axis=0)
    return jnp.concatenate([x[:rows], last], axis=1)


def folded(rows, cols):
    side = fold_rows(rows, cols)
    return shape(rows + side, cols - 64) if side else shape(rows, cols)


def silu_backward(cotangent, preact):
    values = preact.astype(F32)
    gate = 1.0 / (1.0 + jnp.exp(-values))
    return (cotangent.astype(F32) * gate * (1.0 + values * (1.0 - gate))).astype(BF16)


def analyse(scaled_ref, table_ref, *refs):
    groups = table_ref.shape[0]
    out_refs, held_ref = refs[:groups], refs[groups]
    scaled = scaled_ref[...].reshape(-1, scaled_ref.shape[2])
    table = table_ref[...].reshape(groups * table_ref.shape[1], -1)
    held_ref[...] = dot(table, scaled).reshape(held_ref.shape)
    me = lax.axis_index("lat")
    for step in range(groups):
        out_refs[step][...] = fold(held_ref[partner(me, step, groups)]).astype(BF16)


def prepare(*refs):
    legendre_refs = refs[:-7]
    pick_rows_ref, pick_lat_ref, row_kind_ref, col_kind_ref, mixing_ref = refs[-7:-2]
    spread_ref, mixing_out = refs[-2:]
    chan, ens = lax.axis_index("chan"), lax.axis_index("ens")
    for step in range(row_kind_ref.shape[0]):
        core = partner(chan, step)
        blocks = []
        for mode in range(legendre_refs[0].shape[1]):
            total = None
            for place in range(pick_lat_ref.shape[0]):
                pick = pick_lat_ref[partner(ens, place)]
                term = dot(legendre_refs[step][place, mode], pick, 0, 0)
                total = term if total is None else total + term
            blocks.append(total)
        block = jnp.concatenate(blocks, axis=0).astype(BF16)
        keep = dot(row_kind_ref[core], col_kind_ref[...])
        spread_ref[core] = (dot(pick_rows_ref[...], block) * keep).astype(BF16)
    halves, half, _ = mixing_out.shape
    rows = mixing_ref[pl.ds(pl.multiple_of(chan * half, half), half), :]
    for core in range(halves):
        mixing_out[core] = rows[:, core * half : (core + 1) * half]


def coefficients(groups, chan_count, piece, scale, *refs):
    recv_refs = refs[:groups]
    spread_ref = refs[groups]
    coeffs_refs = refs[groups + 1 : groups + 1 + chan_count]
    coef_out, term_out, held_ref, coef_ref = refs[groups + 1 + chan_count :]
    lat, chan = lax.axis_index("lat"), lax.axis_index("chan")
    _, chunk, cols = held_ref.shape
    for step in range(groups):
        block = unfold(recv_refs[step][...].astype(F32), chunk, cols)
        held_ref[partner(lat, step, groups)] = block
    block = held_ref[...].reshape(-1, cols).astype(BF16)
    for core in range(chan_count):
        coef = dot(spread_ref[core], block).astype(BF16)
        coef_ref[core] = coef
        coef_out[core] = coef
    term = None
    for step in range(chan_count):
        part = dot(coeffs_refs[step][...], coef_ref[partner(chan, step)], 0, 0)
        term = part if term is None else term + part
    term = term * scale
    if piece < term_out.shape[1]:
        term_out[:, piece:] = jnp.zeros_like(term_out[:, piece:])
    for group in range(groups):
        term_out[group, :piece] = term[group * piece : (group + 1) * piece]


def mix(groups, chan_count, *refs):
    coef_refs = refs[:chan_count]
    mixing_ref, spread_ref, term_ref = refs[chan_count : chan_count + 3]
    own_ref, *send_refs, back_ref = refs[chan_count + 3 :]
    lat, chan = lax.axis_index("lat"), lax.axis_index("chan")
    rows = coef_refs[0].shape[0] * coef_refs[0].shape[1]
    mixed = None
    for step in range(chan_count):
        coef = coef_refs[step][...].reshape(rows, -1)
        part = dot(coef, mixing_ref[partner(chan, step)], 1, 1)
        mixed = part if mixed is None else mixed + part
    spread = spread_ref[...].reshape(rows, -1)
    back_ref[...] = dot(spread, mixed.astype(BF16), 0, 0).reshape(back_ref.shape)
    own_ref[...] = fold(back_ref[lat]).astype(BF16)
    for step in range(1, groups):
        target = partner(lat, step, groups)
        term = fold(term_ref[target]).astype(BF16)
        send_refs[step - 1][: term.shape[0]] = term
        send_refs[step - 1][term.shape[0] :] = fold(back_ref[target]).astype(BF16)


def add_groups(term_ref, *refs):
    total = fold(term_ref[lax.axis_index("lat")])
    for ref in refs[:-1]:
        total = total + ref[: total.shape[0]].astype(F32)
    refs[-1][...] = total.astype(BF16)


def add_members(*refs):
    term_refs, (out_ref, held_ref) = refs[:-2], refs[-2:]
    ens = lax.axis_index("ens")
    for step, ref in enumerate(term_refs):
        held_ref[partner(ens, step)] = ref[...].astype(F32)
    total = held_ref[0]
    for member in range(1, len(term_refs)):
        total = total + held_ref[member]
    out_ref[...] = total.astype(BF16)


def synthesise(*refs):
    recv_refs, (table_ref, grad_ref, out_ref, held_ref) = refs[:-4], refs[-4:]
    lat = lax.axis_index("lat")
    _, chunk, cols = held_ref.shape
    size = recv_refs[0].shape[0]
    for step, ref in enumerate(recv_refs):
        block = ref[ref.shape[0] - size :].astype(F32)
        held_ref[partner(lat, step, len(recv_refs))] = unfold(block, chunk, cols)
    received = held_ref[...].reshape(-1, cols).astype(BF16)
    if len(table_ref.shape) == 3:
        spatial = dot(table_ref[...].reshape(received.shape[0], -1), received, 0)
    else:
        spatial = dot(table_ref[...], received)
    result = grad_ref[...].astype(F32) + spatial.reshape(grad_ref.shape)
    out_ref[...] = result.astype(BF16)


def assemble(piece, *refs):
    block_refs, (out_ref, held_ref) = refs[:-2], refs[-2:]
    lat = lax.axis_index("lat")
    _, head, cols = held_ref.shape
    for step, ref in enumerate(block_refs):
        held_ref[partner(lat, step)] = unfold(ref[...].astype(F32), head, cols)
    for group in range(len(block_refs)):
        out_ref[group * piece : (group + 1) * piece] = held_ref[group, :piece].astype(BF16)


def finish(*refs):
    block_refs, (out_ref, held_ref) = refs[:-2], refs[-2:]
    chan = lax.axis_index("chan")
    for step, ref in enumerate(block_refs):
        held_ref[partner(chan, step)] = ref[...].astype(F32)
    half = held_ref.shape[2]
    for core in range(len(block_refs)):
        out_ref[:, core * half : (core + 1) * half] = held_ref[core]


def call(kernel, outs, operands, scratch=(), limit=None):
    sizes = [math.prod(x.shape) * x.dtype.itemsize for x in (*operands, *outs)]
    sizes += [math.prod(x.shape) * 4 for x in scratch]
    return pl.pallas_call(
        lambda *refs: kernel(*refs),
        out_shape=tuple(outs),
        in_specs=[VMEM] * len(operands),
        out_specs=(VMEM,) * len(outs),
        scratch_shapes=scratch,
        compiler_params=pltpu.CompilerParams(
            vmem_limit_bytes=limit or min(56 << 20, (6 << 20) + 4 * sum(sizes))
        ),
        cost_estimate=pl.CostEstimate(
            flops=1000000, bytes_accessed=2 * sum(sizes), transcendentals=0
        ),
    )(*operands)


def swap(blocks, axis, far=False):
    count = len(blocks)
    received = [blocks[0]]
    for step in range(1, count):
        pairs = [
            (device, partner(device, step, count if far else 0)) for device in range(count)
        ]
        received.append(lax.ppermute(blocks[step], axis, pairs))
    return received


def share(block, axis):
    return swap([block] * lax.axis_size(axis), axis)


def shape(*dims, dtype=BF16):
    return jax.ShapeDtypeStruct(dims, dtype)


def on_device(grad_out, pre_act, coeffs, legendre, mixing):
    lat_rows, lon_count, chan_cols = grad_out.shape[1:]
    mode_count = lon_count // 2
    groups = lax.axis_size("lat")
    chan_count = lax.axis_size("chan")
    members = lax.axis_size("ens")
    channels = chan_cols * chan_count
    local_modes, degrees, _ = legendre.shape
    table = analysis_matrix(lat_rows, lon_count, mode_count, groups)
    selections = expansion_tables(
        local_modes, chan_count, degrees, lat_rows, groups, members
    )
    chunk = table.shape[1]
    rows = local_modes * degrees * 2
    piece = channels // groups
    head = padded(piece, 32)
    held = pltpu.VMEM((groups, chunk, chan_cols), F32)
    part = folded(head, chan_cols)
    side = folded(chunk, chan_cols)
    both = shape(part.shape[0] + side.shape[0], side.shape[1])

    legendre_parts = share(jnp.stack(share(legendre.transpose(0, 2, 1), "ens")), "chan")
    spectral = call(
        analyse,
        [side] * groups,
        (silu_backward(grad_out[0], pre_act[0]), jnp.asarray(table)),
        (held,),
    )
    spectral = swap(spectral, "lat", far=True)
    coeffs_parts = [x.reshape(rows, channels) for x in share(coeffs[0], "chan")]
    spread, halves = call(
        prepare,
        [
            shape(chan_count, rows, groups * chunk),
            shape(chan_count, chan_cols, chan_cols),
        ],
        (*legendre_parts, *(jnp.asarray(x) for x in selections), mixing),
    )

    coef, term = call(
        lambda *refs: coefficients(
            groups, chan_count, piece, 1.0 / (members * mode_count), *refs
        ),
        [shape(chan_count, rows, chan_cols), shape(groups, head, chan_cols, dtype=F32)],
        (*spectral, spread, *coeffs_parts),
        (held, pltpu.VMEM((chan_count, rows, chan_cols), BF16)),
    )
    blocks = call(
        lambda *refs: mix(groups, chan_count, *refs),
        [side, *[both] * (groups - 1)],
        (*share(coef, "chan"), halves, spread, term),
        (held,),
    )
    blocks = swap(blocks, "lat", far=True)
    (total,) = call(add_groups, [part], (term, *blocks[1:]))
    (total,) = call(
        add_members,
        [part],
        share(total, "ens"),
        (pltpu.VMEM((members, *part.shape), F32),),
    )
    if table.size < 1 << 20:
        back = jnp.asarray(np.ascontiguousarray(table.reshape(-1, lat_rows * lon_count).T))
    else:
        back = jnp.asarray(table)
    (result,) = call(
        synthesise,
        [shape(*grad_out.shape[1:])],
        (*blocks, back, grad_out[0]),
        (held,),
    )
    (total,) = call(
        lambda *refs: assemble(piece, *refs),
        [shape(channels, chan_cols)],
        share(total, "lat"),
        (pltpu.VMEM((groups, head, chan_cols), F32),),
    )
    (weight_grad,) = call(
        finish,
        [shape(channels, channels, dtype=F32)],
        share(total, "chan"),
        (pltpu.VMEM((chan_count, channels, chan_cols), F32),),
    )
    return (result[None], weight_grad)


def solution(mesh):
    placed = (
        P(("grp", "ens"), "lat", None, "chan"),
        P(("grp", "ens"), "lat", None, "chan"),
        P(("grp", "ens"), ("lat", "chan"), None, None, None),
        P(("lat", "chan"), None, "ens"),
        P(),
    )
    return jax.shard_map(
        on_device,
        mesh=mesh,
        in_specs=placed,
        out_specs=(P(("grp", "ens"), "lat", None, "chan"), P("grp", None)),
        check_vma=False,
    )
```

```python
import math

import jax
import jax.numpy as jnp
import numpy as np
from jax import lax
from jax.experimental import pallas as pl
from jax.experimental.pallas import tpu as pltpu
from jax.sharding import PartitionSpec as P

VMEM = pl.BlockSpec(memory_space=pltpu.VMEM)
BF16 = jnp.bfloat16
F32 = jnp.float32


def fourier_table(lon_count, mode_count):
    longitude = np.arange(lon_count, dtype=np.int32)[:, None]
    wavenumber = np.arange(mode_count, dtype=np.int32)[None, :]
    product_index = longitude * wavenumber % lon_count
    angles = np.float32(2.0 * math.pi / lon_count) * product_index.astype(np.float32)
    factor = np.float32(math.sqrt(2.0 / lon_count))
    stacked = np.stack([np.cos(angles), -np.sin(angles)], axis=2) * factor
    return stacked.reshape(lon_count, 2 * mode_count).astype(BF16)


def padded(rows, tile):
    return -(-rows // tile) * tile


def analysis_matrix(lat_rows, lon_count, mode_count, groups):
    width = 2 * mode_count // groups
    table = np.asarray(fourier_table(lon_count, mode_count)).astype(np.float32)
    table = table.T.reshape(groups, width, lon_count)
    full = np.zeros((groups, lat_rows, width, lat_rows, lon_count), np.float32)
    for row in range(lat_rows):
        full[:, row, :, row, :] = table
    full = full.reshape(groups, lat_rows * width, lat_rows * lon_count)
    out = np.zeros((groups, padded(lat_rows * width, 8), lat_rows * lon_count), np.float32)
    out[:, : lat_rows * width] = full
    return out.astype(BF16)


def expansion_tables(local_modes, chan_count, degrees, lat_rows, groups, members):
    modes = local_modes * chan_count
    width = 2 * modes
    cols = padded(lat_rows * width, 8)
    lat_count = lat_rows * groups
    row = np.arange(local_modes * degrees * 2)
    pick_rows = row[:, None] // 2 == np.arange(local_modes * degrees)[None, :]
    col = np.arange(groups * cols)
    group, inner = col // cols, col % cols
    valid = inner < lat_rows * width
    lat = group * lat_rows + inner // width
    pick_lat = (np.arange(lat_count)[:, None] == lat[None, :]) & valid[None, :]
    kind_of_row = row // (2 * degrees) * 2 + row % 2
    kind_of_row = kind_of_row[None] + 2 * local_modes * np.arange(chan_count)[:, None]
    kind_of_col = inner % width
    kinds = np.arange(width)
    return (
        pick_rows.astype(BF16),
        pick_lat.reshape(members, lat_count // members, groups * cols).astype(BF16),
        (kind_of_row[:, :, None] == kinds).astype(BF16),
        (kinds[:, None] == kind_of_col[None, :]).astype(BF16),
    )


def partner(me, step, count=0):
    return me ^ (count - step if step > 0 and count > 0 else step)


def dot(left, right, left_dim=1, right_dim=0):
    return lax.dot_general(
        left, right, (((left_dim,), (right_dim,)), ((), ())), preferred_element_type=F32
    )


def fold_rows(rows, cols):
    return padded(rows - rows // 2, 8) if cols % 128 == 64 and rows >= 16 else 0


def fold(x):
    rows, cols = x.shape
    side = fold_rows(rows, cols)
    if side == 0:
        return x
    full = cols - 64
    right = x[side:, full:]
    if rows - side < side:
        right = jnp.concatenate([right, jnp.zeros((2 * side - rows, 64), x.dtype)], axis=0)
    tail = jnp.concatenate([x[:side, full:], right], axis=1)
    if full > 128:
        tail = jnp.concatenate([tail, jnp.zeros((side, full - 128), x.dtype)], axis=1)
    return jnp.concatenate([x[:, :full], tail], axis=0)


def unfold(x, rows, cols):
    side = fold_rows(rows, cols)
    if side == 0:
        return x
    tail = x[rows:]
    last = jnp.concatenate([tail[:, :64], tail[: rows - side, 64:128]], axis=0)
    return jnp.concatenate([x[:rows], last], axis=1)


def folded(rows, cols):
    side = fold_rows(rows, cols)
    return shape(rows + side, cols - 64) if side else shape(rows, cols)


def silu_backward(cotangent, preact):
    values = preact.astype(F32)
    gate = 1.0 / (1.0 + jnp.exp(-values))
    return (cotangent.astype(F32) * gate * (1.0 + values * (1.0 - gate))).astype(BF16)


def analyse(scaled_ref, table_ref, *refs):
    groups = table_ref.shape[0]
    out_refs, held_ref = refs[:groups], refs[groups]
    scaled = scaled_ref[...].reshape(-1, scaled_ref.shape[2])
    table = table_ref[...].reshape(groups * table_ref.shape[1], -1)
    held_ref[...] = dot(table, scaled).reshape(held_ref.shape)
    me = lax.axis_index("lat")
    for step in range(groups):
        out_refs[step][...] = fold(held_ref[partner(me, step, groups)]).astype(BF16)


def prepare(*refs):
    legendre_refs = refs[:-7]
    pick_rows_ref, pick_lat_ref, row_kind_ref, col_kind_ref, mixing_ref = refs[-7:-2]
    spread_ref, mixing_out = refs[-2:]
    chan, ens = lax.axis_index("chan"), lax.axis_index("ens")
    for step in range(row_kind_ref.shape[0]):
        core = partner(chan, step)
        blocks = []
        for mode in range(legendre_refs[0].shape[1]):
            total = None
            for place in range(pick_lat_ref.shape[0]):
                pick = pick_lat_ref[partner(ens, place)]
                term = dot(legendre_refs[step][place, mode], pick, 0, 0)
                total = term if total is None else total + term
            blocks.append(total)
        block = jnp.concatenate(blocks, axis=0).astype(BF16)
        keep = dot(row_kind_ref[core], col_kind_ref[...])
        spread_ref[core] = (dot(pick_rows_ref[...], block) * keep).astype(BF16)
    halves, half, _ = mixing_out.shape
    rows = mixing_ref[pl.ds(pl.multiple_of(chan * half, half), half), :]
    for core in range(halves):
        mixing_out[core] = rows[:, core * half : (core + 1) * half]


def coefficients(groups, chan_count, piece, scale, *refs):
    recv_refs = refs[:groups]
    spread_ref = refs[groups]
    coeffs_refs = refs[groups + 1 : groups + 1 + chan_count]
    coef_out, piece_out, *term_refs = refs[groups + 1 + chan_count : -3]
    held_ref, coef_ref, term_ref = refs[-3:]
    lat, chan = lax.axis_index("lat"), lax.axis_index("chan")
    _, chunk, cols = held_ref.shape
    for step in range(groups):
        block = unfold(recv_refs[step][...].astype(F32), chunk, cols)
        held_ref[partner(lat, step, groups)] = block
    block = held_ref[...].reshape(-1, cols).astype(BF16)
    for core in range(chan_count):
        coef = dot(spread_ref[core], block).astype(BF16)
        coef_ref[core] = coef
        coef_out[core] = coef
    term = None
    for step in range(chan_count):
        part = dot(coeffs_refs[step][...], coef_ref[partner(chan, step)], 0, 0)
        term = part if term is None else term + part
    term = term * scale
    if piece < term_ref.shape[1]:
        term_ref[:, piece:] = jnp.zeros_like(term_ref[:, piece:])
    for group in range(groups):
        term_ref[group, :piece] = term[group * piece : (group + 1) * piece]
    piece_out[...] = term_ref[lat]
    for step in range(1, groups):
        term_refs[step - 1][...] = fold(term_ref[partner(lat, step, groups)]).astype(BF16)


def mix(groups, chan_count, *refs):
    coef_refs = refs[:chan_count]
    mixing_ref, spread_ref = refs[chan_count : chan_count + 2]
    *send_refs, back_ref = refs[chan_count + 2 :]
    lat, chan = lax.axis_index("lat"), lax.axis_index("chan")
    rows = coef_refs[0].shape[0] * coef_refs[0].shape[1]
    mixed = None
    for step in range(chan_count):
        coef = coef_refs[step][...].reshape(rows, -1)
        part = dot(coef, mixing_ref[partner(chan, step)], 1, 1)
        mixed = part if mixed is None else mixed + part
    spread = spread_ref[...].reshape(rows, -1)
    back_ref[...] = dot(spread, mixed.astype(BF16), 0, 0).reshape(back_ref.shape)
    for step in range(groups):
        send_refs[step][...] = fold(back_ref[partner(lat, step, groups)]).astype(BF16)


def add_groups(piece_ref, *refs):
    total = fold(piece_ref[...])
    for ref in refs[:-1]:
        total = total + ref[...].astype(F32)
    refs[-1][...] = total.astype(BF16)


def add_members(members, *refs):
    term_refs, recv_refs = refs[:members], refs[members:-4]
    out_ref, rows_out, term_ref, held_ref = refs[-4:]
    lat, ens = lax.axis_index("lat"), lax.axis_index("ens")
    for step, ref in enumerate(term_refs):
        term_ref[partner(ens, step)] = ref[...].astype(F32)
    total = term_ref[0]
    for member in range(1, members):
        total = total + term_ref[member]
    out_ref[...] = total.astype(BF16)
    groups, chunk, cols = held_ref.shape
    for step, ref in enumerate(recv_refs):
        block = unfold(ref[...].astype(F32), chunk, cols)
        held_ref[partner(lat, step, groups)] = block
    rows_out[...] = held_ref[...].reshape(rows_out.shape).astype(BF16)


def synthesise(rows_ref, table_ref, grad_ref, out_ref):
    received = rows_ref[...]
    if len(table_ref.shape) == 3:
        spatial = dot(table_ref[...].reshape(received.shape[0], -1), received, 0)
    else:
        spatial = dot(table_ref[...], received)
    result = grad_ref[...].astype(F32) + spatial.reshape(grad_ref.shape)
    out_ref[...] = result.astype(BF16)


def assemble(piece, *refs):
    block_refs, (out_ref, held_ref) = refs[:-2], refs[-2:]
    lat = lax.axis_index("lat")
    _, head, cols = held_ref.shape
    for step, ref in enumerate(block_refs):
        held_ref[partner(lat, step)] = unfold(ref[...].astype(F32), head, cols)
    for group in range(len(block_refs)):
        out_ref[group * piece : (group + 1) * piece] = held_ref[group, :piece].astype(BF16)


def finish(own_ref, other_ref, out_ref):
    chan, half = lax.axis_index("chan"), own_ref.shape[1]

    @pl.when(chan == 0)
    def _():
        out_ref[:, :half] = own_ref[...].astype(F32)
        out_ref[:, half:] = other_ref[...].astype(F32)

    @pl.when(chan != 0)
    def _():
        out_ref[:, :half] = other_ref[...].astype(F32)
        out_ref[:, half:] = own_ref[...].astype(F32)


def call(kernel, outs, operands, scratch=(), limit=None):
    sizes = [math.prod(x.shape) * x.dtype.itemsize for x in (*operands, *outs)]
    sizes += [math.prod(x.shape) * 4 for x in scratch]
    return pl.pallas_call(
        lambda *refs: kernel(*refs),
        out_shape=tuple(outs),
        in_specs=[VMEM] * len(operands),
        out_specs=(VMEM,) * len(outs),
        scratch_shapes=scratch,
        compiler_params=pltpu.CompilerParams(
            vmem_limit_bytes=limit or min(56 << 20, (6 << 20) + 4 * sum(sizes))
        ),
        cost_estimate=pl.CostEstimate(
            flops=1000000, bytes_accessed=2 * sum(sizes), transcendentals=0
        ),
    )(*operands)


def swap(blocks, axis, far=False):
    count = len(blocks)
    received = [blocks[0]]
    for step in range(1, count):
        pairs = [
            (device, partner(device, step, count if far else 0)) for device in range(count)
        ]
        received.append(lax.ppermute(blocks[step], axis, pairs))
    return received


def share(block, axis):
    return swap([block] * lax.axis_size(axis), axis)


def shape(*dims, dtype=BF16):
    return jax.ShapeDtypeStruct(dims, dtype)


def on_device(grad_out, pre_act, coeffs, legendre, mixing):
    lat_rows, lon_count, chan_cols = grad_out.shape[1:]
    mode_count = lon_count // 2
    groups = lax.axis_size("lat")
    chan_count = lax.axis_size("chan")
    members = lax.axis_size("ens")
    channels = chan_cols * chan_count
    local_modes, degrees, _ = legendre.shape
    table = analysis_matrix(lat_rows, lon_count, mode_count, groups)
    selections = expansion_tables(
        local_modes, chan_count, degrees, lat_rows, groups, members
    )
    chunk = table.shape[1]
    rows = local_modes * degrees * 2
    piece = channels // groups
    head = padded(piece, 32)
    held = pltpu.VMEM((groups, chunk, chan_cols), F32)
    part = folded(head, chan_cols)
    side = folded(chunk, chan_cols)

    legendre_parts = share(jnp.stack(share(legendre.transpose(0, 2, 1), "ens")), "chan")
    spectral = call(
        analyse,
        [side] * groups,
        (silu_backward(grad_out[0], pre_act[0]), jnp.asarray(table)),
        (held,),
    )
    spectral = swap(spectral, "lat", far=True)
    coeffs_parts = [x.reshape(rows, channels) for x in share(coeffs[0], "chan")]
    spread, halves = call(
        prepare,
        [
            shape(chan_count, rows, groups * chunk),
            shape(chan_count, chan_cols, chan_cols),
        ],
        (*legendre_parts, *(jnp.asarray(x) for x in selections), mixing),
    )

    coef, *pieces = call(
        lambda *refs: coefficients(
            groups, chan_count, piece, 1.0 / (members * mode_count), *refs
        ),
        [
            shape(chan_count, rows, chan_cols),
            shape(head, chan_cols, dtype=F32),
            *[part] * (groups - 1),
        ],
        (*spectral, spread, *coeffs_parts),
        (
            held,
            pltpu.VMEM((chan_count, rows, chan_cols), BF16),
            pltpu.VMEM((groups, head, chan_cols), F32),
        ),
    )
    pieces = swap(pieces, "lat", far=True)
    blocks = call(
        lambda *refs: mix(groups, chan_count, *refs),
        [side] * groups,
        (*share(coef, "chan"), halves, spread),
        (held,),
    )
    blocks = swap(blocks, "lat", far=True)
    (total,) = call(add_groups, [part], pieces)
    total, received = call(
        lambda *refs: add_members(members, *refs),
        [part, shape(groups * chunk, chan_cols)],
        (*share(total, "ens"), *blocks),
        (pltpu.VMEM((members, *part.shape), F32), held),
    )
    if table.size < 1 << 20:
        back = jnp.asarray(np.ascontiguousarray(table.reshape(-1, lat_rows * lon_count).T))
    else:
        back = jnp.asarray(table)
    (result,) = call(
        synthesise, [shape(*grad_out.shape[1:])], (received, back, grad_out[0])
    )
    (total,) = call(
        lambda *refs: assemble(piece, *refs),
        [shape(channels, chan_cols)],
        share(total, "lat"),
        (pltpu.VMEM((groups, head, chan_cols), F32),),
    )
    (weight_grad,) = call(
        finish, [shape(channels, channels, dtype=F32)], share(total, "chan")
    )
    return (result[None], weight_grad)


def solution(mesh):
    placed = (
        P(("grp", "ens"), "lat", None, "chan"),
        P(("grp", "ens"), "lat", None, "chan"),
        P(("grp", "ens"), ("lat", "chan"), None, None, None),
        P(("lat", "chan"), None, "ens"),
        P(),
    )
    return jax.shard_map(
        on_device,
        mesh=mesh,
        in_specs=placed,
        out_specs=(P(("grp", "ens"), "lat", None, "chan"), P("grp", None)),
        check_vma=False,
    )
```

```python
import math

import jax
import jax.numpy as jnp
import numpy as np
from jax import lax
from jax.experimental import pallas as pl
from jax.experimental.pallas import tpu as pltpu
from jax.sharding import PartitionSpec as P

VMEM = pl.BlockSpec(memory_space=pltpu.VMEM)
BF16 = jnp.bfloat16
F32 = jnp.float32


def fourier_table(lon_count, mode_count):
    longitude = np.arange(lon_count, dtype=np.int32)[:, None]
    wavenumber = np.arange(mode_count, dtype=np.int32)[None, :]
    product_index = longitude * wavenumber % lon_count
    angles = np.float32(2.0 * math.pi / lon_count) * product_index.astype(np.float32)
    factor = np.float32(math.sqrt(2.0 / lon_count))
    stacked = np.stack([np.cos(angles), -np.sin(angles)], axis=2) * factor
    return stacked.reshape(lon_count, 2 * mode_count).astype(BF16)


def padded(rows, tile):
    return -(-rows // tile) * tile


def analysis_matrix(lat_rows, lon_count, mode_count, groups):
    width = 2 * mode_count // groups
    table = np.asarray(fourier_table(lon_count, mode_count)).astype(np.float32)
    table = table.T.reshape(groups, width, lon_count)
    full = np.zeros((groups, lat_rows, width, lat_rows, lon_count), np.float32)
    for row in range(lat_rows):
        full[:, row, :, row, :] = table
    full = full.reshape(groups, lat_rows * width, lat_rows * lon_count)
    out = np.zeros((groups, padded(lat_rows * width, 8), lat_rows * lon_count), np.float32)
    out[:, : lat_rows * width] = full
    return out.astype(BF16)


def expansion_tables(local_modes, chan_count, degrees, lat_rows, groups, members):
    modes = local_modes * chan_count
    width = 2 * modes
    cols = padded(lat_rows * width, 8)
    lat_count = lat_rows * groups
    row = np.arange(local_modes * degrees * 2)
    pick_rows = row[:, None] // 2 == np.arange(local_modes * degrees)[None, :]
    col = np.arange(groups * cols)
    group, inner = col // cols, col % cols
    valid = inner < lat_rows * width
    lat = group * lat_rows + inner // width
    pick_lat = (np.arange(lat_count)[:, None] == lat[None, :]) & valid[None, :]
    kind_of_row = row // (2 * degrees) * 2 + row % 2
    kind_of_row = kind_of_row[None] + 2 * local_modes * np.arange(chan_count)[:, None]
    kind_of_col = inner % width
    kinds = np.arange(width)
    return (
        pick_rows.astype(BF16),
        pick_lat.reshape(members, lat_count // members, groups * cols).astype(BF16),
        (kind_of_row[:, :, None] == kinds).astype(BF16),
        (kinds[:, None] == kind_of_col[None, :]).astype(BF16),
    )


def partner(me, step, count=0):
    return me ^ (count - step if step > 0 and count > 0 else step)


def dot(left, right, left_dim=1, right_dim=0):
    return lax.dot_general(
        left, right, (((left_dim,), (right_dim,)), ((), ())), preferred_element_type=F32
    )


def fold_rows(rows, cols):
    return padded(rows - rows // 2, 8) if cols % 128 == 64 and rows >= 16 else 0


def fold(x):
    rows, cols = x.shape
    side = fold_rows(rows, cols)
    if side == 0:
        return x
    full = cols - 64
    right = x[side:, full:]
    if rows - side < side:
        right = jnp.concatenate([right, jnp.zeros((2 * side - rows, 64), x.dtype)], axis=0)
    tail = jnp.concatenate([x[:side, full:], right], axis=1)
    if full > 128:
        tail = jnp.concatenate([tail, jnp.zeros((side, full - 128), x.dtype)], axis=1)
    return jnp.concatenate([x[:, :full], tail], axis=0)


def unfold(x, rows, cols):
    side = fold_rows(rows, cols)
    if side == 0:
        return x
    tail = x[rows:]
    last = jnp.concatenate([tail[:, :64], tail[: rows - side, 64:128]], axis=0)
    return jnp.concatenate([x[:rows], last], axis=1)


def folded(rows, cols):
    side = fold_rows(rows, cols)
    return shape(rows + side, cols - 64) if side else shape(rows, cols)


def silu_backward(cotangent, preact):
    values = preact.astype(F32)
    gate = 1.0 / (1.0 + jnp.exp(-values))
    return (cotangent.astype(F32) * gate * (1.0 + values * (1.0 - gate))).astype(BF16)


def analyse(scaled_ref, table_ref, *refs):
    groups = table_ref.shape[0]
    out_refs, held_ref = refs[:groups], refs[groups]
    scaled = scaled_ref[...].reshape(-1, scaled_ref.shape[2])
    table = table_ref[...].reshape(groups * table_ref.shape[1], -1)
    held_ref[...] = dot(table, scaled).reshape(held_ref.shape)
    me = lax.axis_index("lat")
    for step in range(groups):
        out_refs[step][...] = fold(held_ref[partner(me, step, groups)]).astype(BF16)


def prepare(*refs):
    legendre_refs = refs[:-7]
    pick_rows_ref, pick_lat_ref, row_kind_ref, col_kind_ref, mixing_ref = refs[-7:-2]
    spread_ref, mixing_out = refs[-2:]
    chan, ens = lax.axis_index("chan"), lax.axis_index("ens")
    for step in range(row_kind_ref.shape[0]):
        core = partner(chan, step)
        blocks = []
        for mode in range(legendre_refs[0].shape[1]):
            total = None
            for place in range(pick_lat_ref.shape[0]):
                pick = pick_lat_ref[partner(ens, place)]
                term = dot(legendre_refs[step][place, mode], pick, 0, 0)
                total = term if total is None else total + term
            blocks.append(total)
        block = jnp.concatenate(blocks, axis=0).astype(BF16)
        keep = dot(row_kind_ref[core], col_kind_ref[...])
        spread_ref[core] = (dot(pick_rows_ref[...], block) * keep).astype(BF16)
    halves, half, _ = mixing_out.shape
    rows = mixing_ref[pl.ds(pl.multiple_of(chan * half, half), half), :]
    for core in range(halves):
        mixing_out[core] = rows[:, core * half : (core + 1) * half]


def coefficients(groups, chan_count, piece, scale, *refs):
    recv_refs = refs[:groups]
    spread_ref = refs[groups]
    coeffs_refs = refs[groups + 1 : groups + 1 + chan_count]
    coef_out, piece_out, *term_refs = refs[groups + 1 + chan_count : -3]
    held_ref, coef_ref, term_ref = refs[-3:]
    lat, chan = lax.axis_index("lat"), lax.axis_index("chan")
    _, chunk, cols = held_ref.shape
    for step in range(groups):
        block = unfold(recv_refs[step][...].astype(F32), chunk, cols)
        held_ref[partner(lat, step, groups)] = block
    block = held_ref[...].reshape(-1, cols).astype(BF16)
    for core in range(chan_count):
        coef = dot(spread_ref[core], block).astype(BF16)
        coef_ref[core] = coef
        coef_out[core] = coef
    term = None
    for step in range(chan_count):
        part = dot(coeffs_refs[step][...], coef_ref[partner(chan, step)], 0, 0)
        term = part if term is None else term + part
    term = term * scale
    if piece < term_ref.shape[1]:
        term_ref[:, piece:] = jnp.zeros_like(term_ref[:, piece:])
    for group in range(groups):
        term_ref[group, :piece] = term[group * piece : (group + 1) * piece]
    piece_out[...] = term_ref[lat]
    for step in range(1, groups):
        term_refs[step - 1][...] = fold(term_ref[partner(lat, step, groups)]).astype(BF16)


def mix(groups, chan_count, *refs):
    coef_refs = refs[:chan_count]
    mixing_ref, spread_ref = refs[chan_count : chan_count + 2]
    *send_refs, back_ref = refs[chan_count + 2 :]
    lat, chan = lax.axis_index("lat"), lax.axis_index("chan")
    rows = coef_refs[0].shape[0] * coef_refs[0].shape[1]
    mixed = None
    for step in range(chan_count):
        coef = coef_refs[step][...].reshape(rows, -1)
        part = dot(coef, mixing_ref[partner(chan, step)], 1, 1)
        mixed = part if mixed is None else mixed + part
    spread = spread_ref[...].reshape(rows, -1)
    back_ref[...] = dot(spread, mixed.astype(BF16), 0, 0).reshape(back_ref.shape)
    for step in range(groups):
        send_refs[step][...] = fold(back_ref[partner(lat, step, groups)]).astype(BF16)


def add_groups(piece_ref, *refs):
    total = fold(piece_ref[...])
    for ref in refs[:-1]:
        total = total + ref[...].astype(F32)
    refs[-1][...] = total.astype(BF16)


def add_members(rows_ref, *refs):
    del rows_ref
    term_refs, (out_ref, held_ref) = refs[:-2], refs[-2:]
    ens = lax.axis_index("ens")
    for step, ref in enumerate(term_refs):
        held_ref[partner(ens, step)] = ref[...].astype(F32)
    total = held_ref[0]
    for member in range(1, len(term_refs)):
        total = total + held_ref[member]
    out_ref[...] = total.astype(BF16)


def collect(*refs):
    recv_refs, (out_ref, held_ref) = refs[:-2], refs[-2:]
    lat = lax.axis_index("lat")
    groups, chunk, cols = held_ref.shape
    for step, ref in enumerate(recv_refs):
        block = unfold(ref[...].astype(F32), chunk, cols)
        held_ref[partner(lat, step, groups)] = block
    out_ref[...] = held_ref[...].reshape(out_ref.shape).astype(BF16)


def synthesise(rows_ref, table_ref, grad_ref, out_ref):
    received = rows_ref[...]
    if len(table_ref.shape) == 3:
        spatial = dot(table_ref[...].reshape(received.shape[0], -1), received, 0)
    else:
        spatial = dot(table_ref[...], received)
    result = grad_ref[...].astype(F32) + spatial.reshape(grad_ref.shape)
    out_ref[...] = result.astype(BF16)


def assemble(piece, *refs):
    block_refs, (out_ref, held_ref) = refs[:-2], refs[-2:]
    lat = lax.axis_index("lat")
    _, head, cols = held_ref.shape
    for step, ref in enumerate(block_refs):
        held_ref[partner(lat, step)] = unfold(ref[...].astype(F32), head, cols)
    for group in range(len(block_refs)):
        out_ref[group * piece : (group + 1) * piece] = held_ref[group, :piece].astype(BF16)


def finish(own_ref, other_ref, out_ref):
    chan, half = lax.axis_index("chan"), own_ref.shape[1]

    @pl.when(chan == 0)
    def _():
        out_ref[:, :half] = own_ref[...].astype(F32)
        out_ref[:, half:] = other_ref[...].astype(F32)

    @pl.when(chan != 0)
    def _():
        out_ref[:, :half] = other_ref[...].astype(F32)
        out_ref[:, half:] = own_ref[...].astype(F32)


def call(kernel, outs, operands, scratch=(), cost=0):
    sizes = [math.prod(x.shape) * x.dtype.itemsize for x in (*operands, *outs)]
    sizes += [math.prod(x.shape) * 4 for x in scratch]
    return pl.pallas_call(
        lambda *refs: kernel(*refs),
        out_shape=tuple(outs),
        in_specs=[VMEM] * len(operands),
        out_specs=(VMEM,) * len(outs),
        scratch_shapes=scratch,
        compiler_params=pltpu.CompilerParams(
            vmem_limit_bytes=min(56 << 20, (6 << 20) + 4 * sum(sizes))
        ),
        cost_estimate=pl.CostEstimate(
            flops=1000000, bytes_accessed=cost or 2 * sum(sizes), transcendentals=0
        ),
    )(*operands)


def swap(blocks, axis, far=False):
    count = len(blocks)
    received = [blocks[0]]
    for step in range(1, count):
        pairs = [
            (device, partner(device, step, count if far else 0)) for device in range(count)
        ]
        received.append(lax.ppermute(blocks[step], axis, pairs))
    return received


def share(block, axis):
    return swap([block] * lax.axis_size(axis), axis)


def shape(*dims, dtype=BF16):
    return jax.ShapeDtypeStruct(dims, dtype)


def on_device(grad_out, pre_act, coeffs, legendre, mixing):
    lat_rows, lon_count, chan_cols = grad_out.shape[1:]
    mode_count = lon_count // 2
    groups = lax.axis_size("lat")
    chan_count = lax.axis_size("chan")
    members = lax.axis_size("ens")
    channels = chan_cols * chan_count
    local_modes, degrees, _ = legendre.shape
    table = analysis_matrix(lat_rows, lon_count, mode_count, groups)
    selections = expansion_tables(
        local_modes, chan_count, degrees, lat_rows, groups, members
    )
    chunk = table.shape[1]
    rows = local_modes * degrees * 2
    piece = channels // groups
    head = padded(piece, 32)
    held = pltpu.VMEM((groups, chunk, chan_cols), F32)
    part = folded(head, chan_cols)
    side = folded(chunk, chan_cols)

    legendre_parts = share(jnp.stack(share(legendre.transpose(0, 2, 1), "ens")), "chan")
    spectral = call(
        analyse,
        [side] * groups,
        (silu_backward(grad_out[0], pre_act[0]), jnp.asarray(table)),
        (held,),
    )
    spectral = swap(spectral, "lat", far=True)
    coeffs_parts = [x.reshape(rows, channels) for x in share(coeffs[0], "chan")]
    spread, halves = call(
        prepare,
        [
            shape(chan_count, rows, groups * chunk),
            shape(chan_count, chan_cols, chan_cols),
        ],
        (*legendre_parts, *(jnp.asarray(x) for x in selections), mixing),
    )

    coef, *pieces = call(
        lambda *refs: coefficients(
            groups, chan_count, piece, 1.0 / (members * mode_count), *refs
        ),
        [
            shape(chan_count, rows, chan_cols),
            shape(head, chan_cols, dtype=F32),
            *[part] * (groups - 1),
        ],
        (*spectral, spread, *coeffs_parts),
        (
            held,
            pltpu.VMEM((chan_count, rows, chan_cols), BF16),
            pltpu.VMEM((groups, head, chan_cols), F32),
        ),
    )
    pieces = swap(pieces, "lat", far=True)
    blocks = call(
        lambda *refs: mix(groups, chan_count, *refs),
        [side] * groups,
        (*share(coef, "chan"), halves, spread),
        (held,),
    )
    blocks = swap(blocks, "lat", far=True)
    (total,) = call(add_groups, [part], pieces)
    (received,) = call(
        collect, [shape(groups * chunk, chan_cols)], blocks, (held,), cost=32 << 20
    )
    (total,) = call(
        add_members,
        [part],
        (received, *share(total, "ens")),
        (pltpu.VMEM((members, *part.shape), F32),),
    )
    if table.size < 1 << 20:
        back = jnp.asarray(np.ascontiguousarray(table.reshape(-1, lat_rows * lon_count).T))
    else:
        back = jnp.asarray(table)
    (result,) = call(
        synthesise, [shape(*grad_out.shape[1:])], (received, back, grad_out[0])
    )
    (total,) = call(
        lambda *refs: assemble(piece, *refs),
        [shape(channels, chan_cols)],
        share(total, "lat"),
        (pltpu.VMEM((groups, head, chan_cols), F32),),
    )
    (weight_grad,) = call(
        finish, [shape(channels, channels, dtype=F32)], share(total, "chan")
    )
    return (result[None], weight_grad)


def solution(mesh):
    placed = (
        P(("grp", "ens"), "lat", None, "chan"),
        P(("grp", "ens"), "lat", None, "chan"),
        P(("grp", "ens"), ("lat", "chan"), None, None, None),
        P(("lat", "chan"), None, "ens"),
        P(),
    )
    return jax.shard_map(
        on_device,
        mesh=mesh,
        in_specs=placed,
        out_specs=(P(("grp", "ens"), "lat", None, "chan"), P("grp", None)),
        check_vma=False,
    )
```

```python
import math

import jax
import jax.numpy as jnp
import numpy as np
from jax import lax
from jax.experimental import pallas as pl
from jax.experimental.pallas import tpu as pltpu
from jax.sharding import PartitionSpec as P

VMEM = pl.BlockSpec(memory_space=pltpu.VMEM)
BF16 = jnp.bfloat16
F32 = jnp.float32


def fourier_table(lon_count, mode_count):
    longitude = np.arange(lon_count, dtype=np.int32)[:, None]
    wavenumber = np.arange(mode_count, dtype=np.int32)[None, :]
    product_index = longitude * wavenumber % lon_count
    angles = np.float32(2.0 * math.pi / lon_count) * product_index.astype(np.float32)
    factor = np.float32(math.sqrt(2.0 / lon_count))
    stacked = np.stack([np.cos(angles), -np.sin(angles)], axis=2) * factor
    return stacked.reshape(lon_count, 2 * mode_count).astype(BF16)


def padded(rows, tile):
    return -(-rows // tile) * tile


def analysis_matrix(lat_rows, lon_count, mode_count, groups):
    width = 2 * mode_count // groups
    table = np.asarray(fourier_table(lon_count, mode_count)).astype(np.float32)
    table = table.T.reshape(groups, width, lon_count)
    full = np.zeros((groups, lat_rows, width, lat_rows, lon_count), np.float32)
    for row in range(lat_rows):
        full[:, row, :, row, :] = table
    full = full.reshape(groups, lat_rows * width, lat_rows * lon_count)
    out = np.zeros((groups, padded(lat_rows * width, 8), lat_rows * lon_count), np.float32)
    out[:, : lat_rows * width] = full
    return out.astype(BF16)


def expansion_tables(local_modes, chan_count, degrees, lat_rows, groups, members):
    modes = local_modes * chan_count
    width = 2 * modes
    cols = padded(lat_rows * width, 8)
    lat_count = lat_rows * groups
    row = np.arange(local_modes * degrees * 2)
    pick_rows = row[:, None] // 2 == np.arange(local_modes * degrees)[None, :]
    col = np.arange(groups * cols)
    group, inner = col // cols, col % cols
    valid = inner < lat_rows * width
    lat = group * lat_rows + inner // width
    pick_lat = (np.arange(lat_count)[:, None] == lat[None, :]) & valid[None, :]
    kind_of_row = row // (2 * degrees) * 2 + row % 2
    kind_of_row = kind_of_row[None] + 2 * local_modes * np.arange(chan_count)[:, None]
    kind_of_col = inner % width
    kinds = np.arange(width)
    return (
        pick_rows.astype(BF16),
        pick_lat.reshape(members, lat_count // members, groups * cols).astype(BF16),
        (kind_of_row[:, :, None] == kinds).astype(BF16),
        (kinds[:, None] == kind_of_col[None, :]).astype(BF16),
    )


def partner(me, step, count=0):
    return me ^ (count - step if step > 0 and count > 0 else step)


def dot(left, right, left_dim=1, right_dim=0):
    return lax.dot_general(
        left, right, (((left_dim,), (right_dim,)), ((), ())), preferred_element_type=F32
    )


def fold_rows(rows, cols):
    return padded(rows - rows // 2, 8) if cols % 128 == 64 and rows >= 16 else 0


def fold(x):
    rows, cols = x.shape
    side = fold_rows(rows, cols)
    if side == 0:
        return x
    full = cols - 64
    right = x[side:, full:]
    if rows - side < side:
        right = jnp.concatenate([right, jnp.zeros((2 * side - rows, 64), x.dtype)], axis=0)
    tail = jnp.concatenate([x[:side, full:], right], axis=1)
    if full > 128:
        tail = jnp.concatenate([tail, jnp.zeros((side, full - 128), x.dtype)], axis=1)
    return jnp.concatenate([x[:, :full], tail], axis=0)


def unfold(x, rows, cols):
    side = fold_rows(rows, cols)
    if side == 0:
        return x
    tail = x[rows:]
    last = jnp.concatenate([tail[:, :64], tail[: rows - side, 64:128]], axis=0)
    return jnp.concatenate([x[:rows], last], axis=1)


def folded(rows, cols):
    side = fold_rows(rows, cols)
    return shape(rows + side, cols - 64) if side else shape(rows, cols)


def silu_backward(cotangent, preact):
    values = preact.astype(F32)
    gate = 1.0 / (1.0 + jnp.exp(-values))
    return (cotangent.astype(F32) * gate * (1.0 + values * (1.0 - gate))).astype(BF16)


def analyse(scaled_ref, table_ref, *refs):
    groups = table_ref.shape[0]
    out_refs, held_ref = refs[:groups], refs[groups]
    scaled = scaled_ref[...].reshape(-1, scaled_ref.shape[2])
    table = table_ref[...].reshape(groups * table_ref.shape[1], -1)
    held_ref[...] = dot(table, scaled).reshape(held_ref.shape)
    me = lax.axis_index("lat")
    for step in range(groups):
        out_refs[step][...] = fold(held_ref[partner(me, step, groups)]).astype(BF16)


def prepare(*refs):
    legendre_refs = refs[:-7]
    pick_rows_ref, pick_lat_ref, row_kind_ref, col_kind_ref, mixing_ref = refs[-7:-2]
    spread_ref, mixing_out = refs[-2:]
    chan, ens = lax.axis_index("chan"), lax.axis_index("ens")
    for step in range(row_kind_ref.shape[0]):
        core = partner(chan, step)
        blocks = []
        for mode in range(legendre_refs[0].shape[1]):
            total = None
            for place in range(pick_lat_ref.shape[0]):
                pick = pick_lat_ref[partner(ens, place)]
                term = dot(legendre_refs[step][place, mode], pick, 0, 0)
                total = term if total is None else total + term
            blocks.append(total)
        block = jnp.concatenate(blocks, axis=0).astype(BF16)
        keep = dot(row_kind_ref[core], col_kind_ref[...])
        spread_ref[core] = (dot(pick_rows_ref[...], block) * keep).astype(BF16)
    halves, half, _ = mixing_out.shape
    rows = mixing_ref[pl.ds(pl.multiple_of(chan * half, half), half), :]
    for core in range(halves):
        mixing_out[core] = rows[:, core * half : (core + 1) * half]


def coefficients(groups, chan_count, piece, scale, *refs):
    recv_refs = refs[:groups]
    spread_ref = refs[groups]
    coeffs_refs = refs[groups + 1 : groups + 1 + chan_count]
    rows_out, piece_out, *send_refs = refs[groups + 1 + chan_count : -3]
    held_ref, coef_ref, term_ref = refs[-3:]
    lat, chan = lax.axis_index("lat"), lax.axis_index("chan")
    _, chunk, cols = held_ref.shape
    for step in range(groups):
        block = unfold(recv_refs[step][...].astype(F32), chunk, cols)
        held_ref[partner(lat, step, groups)] = block
    block = held_ref[...].reshape(-1, cols).astype(BF16)
    back = None
    for core in range(chan_count):
        coef = dot(spread_ref[core], block).astype(BF16)
        coef_ref[core] = coef
        part = dot(spread_ref[core], coef, 0, 0)
        back = part if back is None else back + part
    held_ref[...] = back.reshape(held_ref.shape)
    term = None
    for step in range(chan_count):
        part = dot(coeffs_refs[step][...], coef_ref[partner(chan, step)], 0, 0)
        term = part if term is None else term + part
    term = term * scale
    if piece < term_ref.shape[1]:
        term_ref[:, piece:] = jnp.zeros_like(term_ref[:, piece:])
    for group in range(groups):
        term_ref[group, :piece] = term[group * piece : (group + 1) * piece]
    rows_out[...] = held_ref[lat].astype(BF16)
    piece_out[...] = term_ref[lat]
    for step in range(1, groups):
        target = partner(lat, step, groups)
        part = fold(term_ref[target]).astype(BF16)
        send_refs[step - 1][: part.shape[0]] = part
        send_refs[step - 1][part.shape[0] :] = fold(held_ref[target]).astype(BF16)


def add_groups(rows_ref, piece_ref, *refs):
    recv_refs, (piece_out, rows_out, held_ref) = refs[:-3], refs[-3:]
    lat = lax.axis_index("lat")
    groups, chunk, cols = held_ref.shape
    total = fold(piece_ref[...])
    held_ref[lat] = rows_ref[...].astype(F32)
    for step, ref in enumerate(recv_refs):
        total = total + ref[: total.shape[0]].astype(F32)
        block = unfold(ref[total.shape[0] :].astype(F32), chunk, cols)
        held_ref[partner(lat, step + 1, groups)] = block
    piece_out[...] = total.astype(BF16)
    rows_out[...] = held_ref[...].reshape(rows_out.shape).astype(BF16)


def mix(*refs):
    rows_refs, (mixing_ref, out_ref) = refs[:-2], refs[-2:]
    chan = lax.axis_index("chan")
    mixed = None
    for step, ref in enumerate(rows_refs):
        part = dot(ref[...], mixing_ref[partner(chan, step)], 1, 1)
        mixed = part if mixed is None else mixed + part
    out_ref[...] = mixed.astype(BF16)


def add_members(*refs):
    term_refs, (out_ref, held_ref) = refs[:-2], refs[-2:]
    ens = lax.axis_index("ens")
    for step, ref in enumerate(term_refs):
        held_ref[partner(ens, step)] = ref[...].astype(F32)
    total = held_ref[0]
    for member in range(1, len(term_refs)):
        total = total + held_ref[member]
    out_ref[...] = total.astype(BF16)


def synthesise(rows_ref, table_ref, grad_ref, out_ref):
    received = rows_ref[...]
    if len(table_ref.shape) == 3:
        spatial = dot(table_ref[...].reshape(received.shape[0], -1), received, 0)
    else:
        spatial = dot(table_ref[...], received)
    result = grad_ref[...].astype(F32) + spatial.reshape(grad_ref.shape)
    out_ref[...] = result.astype(BF16)


def assemble(piece, mixed_ref, *refs):
    del mixed_ref
    block_refs, (out_ref, held_ref) = refs[:-2], refs[-2:]
    lat = lax.axis_index("lat")
    _, head, cols = held_ref.shape
    for step, ref in enumerate(block_refs):
        held_ref[partner(lat, step)] = unfold(ref[...].astype(F32), head, cols)
    for group in range(len(block_refs)):
        out_ref[group * piece : (group + 1) * piece] = held_ref[group, :piece].astype(BF16)


def finish(own_ref, other_ref, out_ref):
    chan, half = lax.axis_index("chan"), own_ref.shape[1]

    @pl.when(chan == 0)
    def _():
        out_ref[:, :half] = own_ref[...].astype(F32)
        out_ref[:, half:] = other_ref[...].astype(F32)

    @pl.when(chan != 0)
    def _():
        out_ref[:, :half] = other_ref[...].astype(F32)
        out_ref[:, half:] = own_ref[...].astype(F32)


def call(kernel, outs, operands, scratch=(), limit=None):
    sizes = [math.prod(x.shape) * x.dtype.itemsize for x in (*operands, *outs)]
    sizes += [math.prod(x.shape) * 4 for x in scratch]
    return pl.pallas_call(
        lambda *refs: kernel(*refs),
        out_shape=tuple(outs),
        in_specs=[VMEM] * len(operands),
        out_specs=(VMEM,) * len(outs),
        scratch_shapes=scratch,
        compiler_params=pltpu.CompilerParams(
            vmem_limit_bytes=limit or min(56 << 20, (6 << 20) + 4 * sum(sizes))
        ),
        cost_estimate=pl.CostEstimate(
            flops=1000000, bytes_accessed=2 * sum(sizes), transcendentals=0
        ),
    )(*operands)


def swap(blocks, axis, far=False):
    count = len(blocks)
    received = [blocks[0]]
    for step in range(1, count):
        pairs = [
            (device, partner(device, step, count if far else 0)) for device in range(count)
        ]
        received.append(lax.ppermute(blocks[step], axis, pairs))
    return received


def share(block, axis):
    return swap([block] * lax.axis_size(axis), axis)


def shape(*dims, dtype=BF16):
    return jax.ShapeDtypeStruct(dims, dtype)


def on_device(grad_out, pre_act, coeffs, legendre, mixing):
    lat_rows, lon_count, chan_cols = grad_out.shape[1:]
    mode_count = lon_count // 2
    groups = lax.axis_size("lat")
    chan_count = lax.axis_size("chan")
    members = lax.axis_size("ens")
    channels = chan_cols * chan_count
    local_modes, degrees, _ = legendre.shape
    table = analysis_matrix(lat_rows, lon_count, mode_count, groups)
    selections = expansion_tables(
        local_modes, chan_count, degrees, lat_rows, groups, members
    )
    chunk = table.shape[1]
    rows = local_modes * degrees * 2
    piece = channels // groups
    head = padded(piece, 32)
    held = pltpu.VMEM((groups, chunk, chan_cols), F32)
    part = folded(head, chan_cols)
    side = folded(chunk, chan_cols)
    both = shape(part.shape[0] + side.shape[0], side.shape[1])

    legendre_parts = share(jnp.stack(share(legendre.transpose(0, 2, 1), "ens")), "chan")
    spectral = call(
        analyse,
        [side] * groups,
        (silu_backward(grad_out[0], pre_act[0]), jnp.asarray(table)),
        (held,),
    )
    spectral = swap(spectral, "lat", far=True)
    coeffs_parts = [x.reshape(rows, channels) for x in share(coeffs[0], "chan")]
    spread, halves = call(
        prepare,
        [
            shape(chan_count, rows, groups * chunk),
            shape(chan_count, chan_cols, chan_cols),
        ],
        (*legendre_parts, *(jnp.asarray(x) for x in selections), mixing),
    )

    rows_own, piece_own, *blocks = call(
        lambda *refs: coefficients(
            groups, chan_count, piece, 1.0 / (members * mode_count), *refs
        ),
        [
            shape(chunk, chan_cols),
            shape(head, chan_cols, dtype=F32),
            *[both] * (groups - 1),
        ],
        (*spectral, spread, *coeffs_parts),
        (
            held,
            pltpu.VMEM((chan_count, rows, chan_cols), BF16),
            pltpu.VMEM((groups, head, chan_cols), F32),
        ),
    )
    blocks = swap([rows_own, *blocks], "lat", far=True)[1:]
    returned = shape(groups * chunk, chan_cols)
    total, received = call(
        add_groups, [part, returned], (rows_own, piece_own, *blocks), (held,)
    )
    (mixed,) = call(mix, [returned], (*share(received, "chan"), halves))
    (total,) = call(
        add_members,
        [part],
        share(total, "ens"),
        (pltpu.VMEM((members, *part.shape), F32),),
    )
    if table.size < 1 << 20:
        back = jnp.asarray(np.ascontiguousarray(table.reshape(-1, lat_rows * lon_count).T))
    else:
        back = jnp.asarray(table)
    (result,) = call(
        synthesise, [shape(*grad_out.shape[1:])], (mixed, back, grad_out[0])
    )
    (total,) = call(
        lambda *refs: assemble(piece, *refs),
        [shape(channels, chan_cols)],
        (mixed, *share(total, "lat")),
        (pltpu.VMEM((groups, head, chan_cols), F32),),
    )
    (weight_grad,) = call(
        finish, [shape(channels, channels, dtype=F32)], share(total, "chan")
    )
    return (result[None], weight_grad)


def solution(mesh):
    placed = (
        P(("grp", "ens"), "lat", None, "chan"),
        P(("grp", "ens"), "lat", None, "chan"),
        P(("grp", "ens"), ("lat", "chan"), None, None, None),
        P(("lat", "chan"), None, "ens"),
        P(),
    )
    return jax.shard_map(
        on_device,
        mesh=mesh,
        in_specs=placed,
        out_specs=(P(("grp", "ens"), "lat", None, "chan"), P("grp", None)),
        check_vma=False,
    )
```

```python
import math

import jax
import jax.numpy as jnp
import numpy as np
from jax import lax
from jax.experimental import pallas as pl
from jax.experimental.pallas import tpu as pltpu
from jax.sharding import PartitionSpec as P

VMEM = pl.BlockSpec(memory_space=pltpu.VMEM)
BF16 = jnp.bfloat16
F32 = jnp.float32


def fourier_table(lon_count, mode_count):
    longitude = np.arange(lon_count, dtype=np.int32)[:, None]
    wavenumber = np.arange(mode_count, dtype=np.int32)[None, :]
    product_index = longitude * wavenumber % lon_count
    angles = np.float32(2.0 * math.pi / lon_count) * product_index.astype(np.float32)
    factor = np.float32(math.sqrt(2.0 / lon_count))
    stacked = np.stack([np.cos(angles), -np.sin(angles)], axis=2) * factor
    return stacked.reshape(lon_count, 2 * mode_count).astype(BF16)


def padded(rows, tile):
    return -(-rows // tile) * tile


def analysis_matrix(lat_rows, lon_count, mode_count, groups):
    width = 2 * mode_count // groups
    table = np.asarray(fourier_table(lon_count, mode_count)).astype(np.float32)
    table = table.T.reshape(groups, width, lon_count)
    full = np.zeros((groups, lat_rows, width, lat_rows, lon_count), np.float32)
    for row in range(lat_rows):
        full[:, row, :, row, :] = table
    full = full.reshape(groups, lat_rows * width, lat_rows * lon_count)
    out = np.zeros((groups, padded(lat_rows * width, 8), lat_rows * lon_count), np.float32)
    out[:, : lat_rows * width] = full
    return out.astype(BF16)


def expansion_tables(local_modes, chan_count, degrees, lat_rows, groups, members):
    modes = local_modes * chan_count
    width = 2 * modes
    cols = padded(lat_rows * width, 8)
    lat_count = lat_rows * groups
    row = np.arange(local_modes * degrees * 2)
    pick_rows = row[:, None] // 2 == np.arange(local_modes * degrees)[None, :]
    col = np.arange(groups * cols)
    group, inner = col // cols, col % cols
    valid = inner < lat_rows * width
    lat = group * lat_rows + inner // width
    pick_lat = (np.arange(lat_count)[:, None] == lat[None, :]) & valid[None, :]
    kind_of_row = row // (2 * degrees) * 2 + row % 2
    kind_of_row = kind_of_row[None] + 2 * local_modes * np.arange(chan_count)[:, None]
    kind_of_col = inner % width
    kinds = np.arange(width)
    return (
        pick_rows.astype(BF16),
        pick_lat.reshape(members, lat_count // members, groups * cols).astype(BF16),
        (kind_of_row[:, :, None] == kinds).astype(BF16),
        (kinds[:, None] == kind_of_col[None, :]).astype(BF16),
    )


def partner(me, step, count=0):
    return me ^ (count - step if step > 0 and count > 0 else step)


def dot(left, right, left_dim=1, right_dim=0):
    return lax.dot_general(
        left, right, (((left_dim,), (right_dim,)), ((), ())), preferred_element_type=F32
    )


def fold_rows(rows, cols):
    return padded(rows - rows // 2, 8) if cols % 128 == 64 and rows >= 16 else 0


def fold(x):
    rows, cols = x.shape
    side = fold_rows(rows, cols)
    if side == 0:
        return x
    full = cols - 64
    right = x[side:, full:]
    if rows - side < side:
        right = jnp.concatenate([right, jnp.zeros((2 * side - rows, 64), x.dtype)], axis=0)
    tail = jnp.concatenate([x[:side, full:], right], axis=1)
    if full > 128:
        tail = jnp.concatenate([tail, jnp.zeros((side, full - 128), x.dtype)], axis=1)
    return jnp.concatenate([x[:, :full], tail], axis=0)


def unfold(x, rows, cols):
    side = fold_rows(rows, cols)
    if side == 0:
        return x
    tail = x[rows:]
    last = jnp.concatenate([tail[:, :64], tail[: rows - side, 64:128]], axis=0)
    return jnp.concatenate([x[:rows], last], axis=1)


def folded(rows, cols):
    side = fold_rows(rows, cols)
    return shape(rows + side, cols - 64) if side else shape(rows, cols)


def silu_backward(cotangent, preact):
    values = preact.astype(F32)
    gate = 1.0 / (1.0 + jnp.exp(-values))
    return (cotangent.astype(F32) * gate * (1.0 + values * (1.0 - gate))).astype(BF16)


def analyse(scaled_ref, table_ref, *refs):
    groups = table_ref.shape[0]
    out_refs, held_ref = refs[:groups], refs[groups]
    scaled = scaled_ref[...].reshape(-1, scaled_ref.shape[2])
    table = table_ref[...].reshape(groups * table_ref.shape[1], -1)
    held_ref[...] = dot(table, scaled).reshape(held_ref.shape)
    me = lax.axis_index("lat")
    for step in range(groups):
        out_refs[step][...] = fold(held_ref[partner(me, step, groups)]).astype(BF16)


def prepare(*refs):
    legendre_refs = refs[:-7]
    pick_rows_ref, pick_lat_ref, row_kind_ref, col_kind_ref, mixing_ref = refs[-7:-2]
    spread_ref, mixing_out = refs[-2:]
    chan, ens = lax.axis_index("chan"), lax.axis_index("ens")
    for step in range(row_kind_ref.shape[0]):
        core = partner(chan, step)
        blocks = []
        for mode in range(legendre_refs[0].shape[1]):
            total = None
            for place in range(pick_lat_ref.shape[0]):
                pick = pick_lat_ref[partner(ens, place)]
                term = dot(legendre_refs[step][place, mode], pick, 0, 0)
                total = term if total is None else total + term
            blocks.append(total)
        block = jnp.concatenate(blocks, axis=0).astype(BF16)
        keep = dot(row_kind_ref[core], col_kind_ref[...])
        spread_ref[core] = (dot(pick_rows_ref[...], block) * keep).astype(BF16)
    halves, half, _ = mixing_out.shape
    rows = mixing_ref[pl.ds(pl.multiple_of(chan * half, half), half), :]
    for core in range(halves):
        mixing_out[core] = rows[:, core * half : (core + 1) * half]


def coefficients(groups, chan_count, piece, scale, *refs):
    recv_refs = refs[:groups]
    spread_ref = refs[groups]
    coeffs_refs = refs[groups + 1 : groups + 1 + chan_count]
    rows_out, piece_out, *send_refs = refs[groups + 1 + chan_count : -3]
    held_ref, coef_ref, term_ref = refs[-3:]
    lat, chan = lax.axis_index("lat"), lax.axis_index("chan")
    _, chunk, cols = held_ref.shape
    for step in range(groups):
        block = unfold(recv_refs[step][...].astype(F32), chunk, cols)
        held_ref[partner(lat, step, groups)] = block
    block = held_ref[...].reshape(-1, cols).astype(BF16)
    back = None
    for core in range(chan_count):
        coef = dot(spread_ref[core], block).astype(BF16)
        coef_ref[core] = coef
        part = dot(spread_ref[core], coef, 0, 0)
        back = part if back is None else back + part
    held_ref[...] = back.reshape(held_ref.shape)
    term = None
    for step in range(chan_count):
        part = dot(coeffs_refs[step][...], coef_ref[partner(chan, step)], 0, 0)
        term = part if term is None else term + part
    term = term * scale
    if piece < term_ref.shape[1]:
        term_ref[:, piece:] = jnp.zeros_like(term_ref[:, piece:])
    for group in range(groups):
        term_ref[group, :piece] = term[group * piece : (group + 1) * piece]
    rows_out[...] = held_ref[lat].astype(BF16)
    piece_out[...] = term_ref[lat]
    for step in range(1, groups):
        target = partner(lat, step, groups)
        part = fold(term_ref[target]).astype(BF16)
        send_refs[step - 1][: part.shape[0]] = part
        send_refs[step - 1][part.shape[0] :] = fold(held_ref[target]).astype(BF16)


def add_groups(rows_ref, piece_ref, *refs):
    recv_refs, (piece_out, rows_out, held_ref) = refs[:-3], refs[-3:]
    lat = lax.axis_index("lat")
    groups, chunk, cols = held_ref.shape
    total = fold(piece_ref[...])
    held_ref[lat] = rows_ref[...].astype(F32)
    for step, ref in enumerate(recv_refs):
        total = total + ref[: total.shape[0]].astype(F32)
        block = unfold(ref[total.shape[0] :].astype(F32), chunk, cols)
        held_ref[partner(lat, step + 1, groups)] = block
    piece_out[...] = total.astype(BF16)
    rows_out[...] = held_ref[...].reshape(rows_out.shape).astype(BF16)


def mix(*refs):
    rows_refs, (mixing_ref, out_ref) = refs[:-2], refs[-2:]
    chan = lax.axis_index("chan")
    mixed = None
    for step, ref in enumerate(rows_refs):
        part = dot(ref[...], mixing_ref[partner(chan, step)], 1, 1)
        mixed = part if mixed is None else mixed + part
    out_ref[...] = mixed.astype(BF16)


def synthesise(rows_ref, table_ref, grad_ref, out_ref):
    received = rows_ref[...]
    if len(table_ref.shape) == 3:
        spatial = dot(table_ref[...].reshape(received.shape[0], -1), received, 0)
    else:
        spatial = dot(table_ref[...], received)
    result = grad_ref[...].astype(F32) + spatial.reshape(grad_ref.shape)
    out_ref[...] = result.astype(BF16)


def assemble(members, piece, cols, mixed_ref, gathered_ref, out_ref):
    del mixed_ref
    head = padded(piece, 32)
    for group in range(gathered_ref.shape[0] // members):
        total = gathered_ref[group * members].astype(F32)
        for member in range(1, members):
            total = total + gathered_ref[group * members + member].astype(F32)
        block = unfold(total, head, cols)[:piece]
        out_ref[group * piece : (group + 1) * piece] = block.astype(BF16)


def finish(own_ref, other_ref, out_ref):
    chan, half = lax.axis_index("chan"), own_ref.shape[1]

    @pl.when(chan == 0)
    def _():
        out_ref[:, :half] = own_ref[...].astype(F32)
        out_ref[:, half:] = other_ref[...].astype(F32)

    @pl.when(chan != 0)
    def _():
        out_ref[:, :half] = other_ref[...].astype(F32)
        out_ref[:, half:] = own_ref[...].astype(F32)


def call(kernel, outs, operands, scratch=(), limit=None):
    sizes = [math.prod(x.shape) * x.dtype.itemsize for x in (*operands, *outs)]
    sizes += [math.prod(x.shape) * 4 for x in scratch]
    return pl.pallas_call(
        lambda *refs: kernel(*refs),
        out_shape=tuple(outs),
        in_specs=[VMEM] * len(operands),
        out_specs=(VMEM,) * len(outs),
        scratch_shapes=scratch,
        compiler_params=pltpu.CompilerParams(
            vmem_limit_bytes=limit or min(56 << 20, (6 << 20) + 4 * sum(sizes))
        ),
        cost_estimate=pl.CostEstimate(
            flops=1000000, bytes_accessed=2 * sum(sizes), transcendentals=0
        ),
    )(*operands)


def swap(blocks, axis, far=False):
    count = len(blocks)
    received = [blocks[0]]
    for step in range(1, count):
        pairs = [
            (device, partner(device, step, count if far else 0)) for device in range(count)
        ]
        received.append(lax.ppermute(blocks[step], axis, pairs))
    return received


def share(block, axis):
    return swap([block] * lax.axis_size(axis), axis)


def shape(*dims, dtype=BF16):
    return jax.ShapeDtypeStruct(dims, dtype)


def on_device(grad_out, pre_act, coeffs, legendre, mixing):
    lat_rows, lon_count, chan_cols = grad_out.shape[1:]
    mode_count = lon_count // 2
    groups = lax.axis_size("lat")
    chan_count = lax.axis_size("chan")
    members = lax.axis_size("ens")
    channels = chan_cols * chan_count
    local_modes, degrees, _ = legendre.shape
    table = analysis_matrix(lat_rows, lon_count, mode_count, groups)
    selections = expansion_tables(
        local_modes, chan_count, degrees, lat_rows, groups, members
    )
    chunk = table.shape[1]
    rows = local_modes * degrees * 2
    piece = channels // groups
    head = padded(piece, 32)
    held = pltpu.VMEM((groups, chunk, chan_cols), F32)
    part = folded(head, chan_cols)
    side = folded(chunk, chan_cols)
    both = shape(part.shape[0] + side.shape[0], side.shape[1])

    legendre_parts = share(jnp.stack(share(legendre.transpose(0, 2, 1), "ens")), "chan")
    spectral = call(
        analyse,
        [side] * groups,
        (silu_backward(grad_out[0], pre_act[0]), jnp.asarray(table)),
        (held,),
    )
    spectral = swap(spectral, "lat", far=True)
    coeffs_parts = [x.reshape(rows, channels) for x in share(coeffs[0], "chan")]
    spread, halves = call(
        prepare,
        [
            shape(chan_count, rows, groups * chunk),
            shape(chan_count, chan_cols, chan_cols),
        ],
        (*legendre_parts, *(jnp.asarray(x) for x in selections), mixing),
    )

    rows_own, piece_own, *blocks = call(
        lambda *refs: coefficients(
            groups, chan_count, piece, 1.0 / (members * mode_count), *refs
        ),
        [
            shape(chunk, chan_cols),
            shape(head, chan_cols, dtype=F32),
            *[both] * (groups - 1),
        ],
        (*spectral, spread, *coeffs_parts),
        (
            held,
            pltpu.VMEM((chan_count, rows, chan_cols), BF16),
            pltpu.VMEM((groups, head, chan_cols), F32),
        ),
    )
    blocks = swap([rows_own, *blocks], "lat", far=True)[1:]
    returned = shape(groups * chunk, chan_cols)
    total, received = call(
        add_groups, [part, returned], (rows_own, piece_own, *blocks), (held,)
    )
    (mixed,) = call(mix, [returned], (*share(received, "chan"), halves))
    if table.size < 1 << 20:
        back = jnp.asarray(np.ascontiguousarray(table.reshape(-1, lat_rows * lon_count).T))
    else:
        back = jnp.asarray(table)
    (result,) = call(
        synthesise, [shape(*grad_out.shape[1:])], (mixed, back, grad_out[0])
    )
    gathered = lax.all_gather(total, ("lat", "ens"))
    (total,) = call(
        lambda *refs: assemble(members, piece, chan_cols, *refs),
        [shape(channels, chan_cols)],
        (mixed, gathered),
    )
    (weight_grad,) = call(
        finish, [shape(channels, channels, dtype=F32)], share(total, "chan")
    )
    return (result[None], weight_grad)


def solution(mesh):
    placed = (
        P(("grp", "ens"), "lat", None, "chan"),
        P(("grp", "ens"), "lat", None, "chan"),
        P(("grp", "ens"), ("lat", "chan"), None, None, None),
        P(("lat", "chan"), None, "ens"),
        P(),
    )
    return jax.shard_map(
        on_device,
        mesh=mesh,
        in_specs=placed,
        out_specs=(P(("grp", "ens"), "lat", None, "chan"), P("grp", None)),
        check_vma=False,
    )
```

```python
import math

import jax
import jax.numpy as jnp
import numpy as np
from jax import lax
from jax.experimental import pallas as pl
from jax.experimental.pallas import tpu as pltpu
from jax.sharding import PartitionSpec as P

VMEM = pl.BlockSpec(memory_space=pltpu.VMEM)
BF16 = jnp.bfloat16
F32 = jnp.float32


def fourier_table(lon_count, mode_count):
    longitude = np.arange(lon_count, dtype=np.int32)[:, None]
    wavenumber = np.arange(mode_count, dtype=np.int32)[None, :]
    product_index = longitude * wavenumber % lon_count
    angles = np.float32(2.0 * math.pi / lon_count) * product_index.astype(np.float32)
    factor = np.float32(math.sqrt(2.0 / lon_count))
    stacked = np.stack([np.cos(angles), -np.sin(angles)], axis=2) * factor
    return stacked.reshape(lon_count, 2 * mode_count).astype(BF16)


def padded(rows, tile):
    return -(-rows // tile) * tile


def analysis_matrix(lat_rows, lon_count, mode_count, groups):
    width = 2 * mode_count // groups
    table = np.asarray(fourier_table(lon_count, mode_count)).astype(np.float32)
    table = table.T.reshape(groups, width, lon_count)
    full = np.zeros((groups, lat_rows, width, lat_rows, lon_count), np.float32)
    for row in range(lat_rows):
        full[:, row, :, row, :] = table
    full = full.reshape(groups, lat_rows * width, lat_rows * lon_count)
    out = np.zeros((groups, padded(lat_rows * width, 8), lat_rows * lon_count), np.float32)
    out[:, : lat_rows * width] = full
    return out.astype(BF16)


def expansion_tables(local_modes, chan_count, degrees, lat_rows, groups, members):
    modes = local_modes * chan_count
    width = 2 * modes
    cols = padded(lat_rows * width, 8)
    lat_count = lat_rows * groups
    row = np.arange(local_modes * degrees * 2)
    pick_rows = row[:, None] // 2 == np.arange(local_modes * degrees)[None, :]
    col = np.arange(groups * cols)
    group, inner = col // cols, col % cols
    valid = inner < lat_rows * width
    lat = group * lat_rows + inner // width
    pick_lat = (np.arange(lat_count)[:, None] == lat[None, :]) & valid[None, :]
    kind_of_row = row // (2 * degrees) * 2 + row % 2
    kind_of_row = kind_of_row[None] + 2 * local_modes * np.arange(chan_count)[:, None]
    kind_of_col = inner % width
    kinds = np.arange(width)
    return (
        pick_rows.astype(BF16),
        pick_lat.reshape(members, lat_count // members, groups * cols).astype(BF16),
        (kind_of_row[:, :, None] == kinds).astype(BF16),
        (kinds[:, None] == kind_of_col[None, :]).astype(BF16),
    )


def partner(me, step, count=0):
    return me ^ (count - step if step > 0 and count > 0 else step)


def dot(left, right, left_dim=1, right_dim=0):
    return lax.dot_general(
        left, right, (((left_dim,), (right_dim,)), ((), ())), preferred_element_type=F32
    )


def fold_rows(rows, cols):
    return padded(rows - rows // 2, 8) if cols % 128 == 64 and rows >= 16 else 0


def fold(x):
    rows, cols = x.shape
    side = fold_rows(rows, cols)
    if side == 0:
        return x
    full = cols - 64
    right = x[side:, full:]
    if rows - side < side:
        right = jnp.concatenate([right, jnp.zeros((2 * side - rows, 64), x.dtype)], axis=0)
    tail = jnp.concatenate([x[:side, full:], right], axis=1)
    if full > 128:
        tail = jnp.concatenate([tail, jnp.zeros((side, full - 128), x.dtype)], axis=1)
    return jnp.concatenate([x[:, :full], tail], axis=0)


def unfold(x, rows, cols):
    side = fold_rows(rows, cols)
    if side == 0:
        return x
    tail = x[rows:]
    last = jnp.concatenate([tail[:, :64], tail[: rows - side, 64:128]], axis=0)
    return jnp.concatenate([x[:rows], last], axis=1)


def folded(rows, cols):
    side = fold_rows(rows, cols)
    return shape(rows + side, cols - 64) if side else shape(rows, cols)


def silu_backward(cotangent, preact):
    values = preact.astype(F32)
    gate = 1.0 / (1.0 + jnp.exp(-values))
    return (cotangent.astype(F32) * gate * (1.0 + values * (1.0 - gate))).astype(BF16)


def analyse(scaled_ref, table_ref, *refs):
    groups = table_ref.shape[0]
    out_refs, held_ref = refs[:groups], refs[groups]
    scaled = scaled_ref[...].reshape(-1, scaled_ref.shape[2])
    table = table_ref[...].reshape(groups * table_ref.shape[1], -1)
    held_ref[...] = dot(table, scaled).reshape(held_ref.shape)
    me = lax.axis_index("lat")
    for step in range(groups):
        out_refs[step][...] = fold(held_ref[partner(me, step, groups)]).astype(BF16)


def prepare(*refs):
    legendre_refs = refs[:-7]
    pick_rows_ref, pick_lat_ref, row_kind_ref, col_kind_ref, mixing_ref = refs[-7:-2]
    spread_ref, mixing_out = refs[-2:]
    chan, ens = lax.axis_index("chan"), lax.axis_index("ens")
    for step in range(row_kind_ref.shape[0]):
        core = partner(chan, step)
        blocks = []
        for mode in range(legendre_refs[0].shape[1]):
            total = None
            for place in range(pick_lat_ref.shape[0]):
                pick = pick_lat_ref[partner(ens, place)]
                term = dot(legendre_refs[step][place, mode], pick, 0, 0)
                total = term if total is None else total + term
            blocks.append(total)
        block = jnp.concatenate(blocks, axis=0).astype(BF16)
        keep = dot(row_kind_ref[core], col_kind_ref[...])
        spread_ref[core] = (dot(pick_rows_ref[...], block) * keep).astype(BF16)
    halves, half, _ = mixing_out.shape
    rows = mixing_ref[pl.ds(pl.multiple_of(chan * half, half), half), :]
    for core in range(halves):
        mixing_out[core] = rows[:, core * half : (core + 1) * half]


def coefficients(groups, chan_count, piece, scale, *refs):
    recv_refs = refs[:groups]
    spread_ref = refs[groups]
    coeffs_refs = refs[groups + 1 : groups + 1 + chan_count]
    send_refs = refs[groups + 1 + chan_count : -3]
    held_ref, coef_ref, term_ref = refs[-3:]
    lat, chan = lax.axis_index("lat"), lax.axis_index("chan")
    _, chunk, cols = held_ref.shape
    for step in range(groups):
        block = unfold(recv_refs[step][...].astype(F32), chunk, cols)
        held_ref[partner(lat, step, groups)] = block
    block = held_ref[...].reshape(-1, cols).astype(BF16)
    back = None
    for core in range(chan_count):
        coef = dot(spread_ref[core], block).astype(BF16)
        coef_ref[core] = coef
        part = dot(spread_ref[core], coef, 0, 0)
        back = part if back is None else back + part
    held_ref[...] = back.reshape(held_ref.shape)
    term = None
    for step in range(chan_count):
        part = dot(coeffs_refs[step][...], coef_ref[partner(chan, step)], 0, 0)
        term = part if term is None else term + part
    term = term * scale
    if piece < term_ref.shape[1]:
        term_ref[:, piece:] = jnp.zeros_like(term_ref[:, piece:])
    for group in range(groups):
        term_ref[group, :piece] = term[group * piece : (group + 1) * piece]
    for step in range(groups):
        target = partner(lat, step, groups)
        part = fold(term_ref[target]).astype(BF16)
        send_refs[step][: part.shape[0]] = part
        send_refs[step][part.shape[0] :] = fold(held_ref[target]).astype(BF16)


def add_groups(*refs):
    recv_refs, (piece_out, rows_out, held_ref) = refs[:-3], refs[-3:]
    lat = lax.axis_index("lat")
    groups, chunk, cols = held_ref.shape
    head = piece_out.shape[0]
    total = None
    for step, ref in enumerate(recv_refs):
        part = ref[:head].astype(F32)
        total = part if total is None else total + part
        block = unfold(ref[head:].astype(F32), chunk, cols)
        held_ref[partner(lat, step, groups)] = block
    piece_out[...] = total.astype(BF16)
    rows_out[...] = held_ref[...].reshape(rows_out.shape).astype(BF16)


def mix(*refs):
    rows_refs, (mixing_ref, out_ref) = refs[:-2], refs[-2:]
    chan = lax.axis_index("chan")
    mixed = None
    for step, ref in enumerate(rows_refs):
        part = dot(ref[...], mixing_ref[partner(chan, step ^ 1)], 1, 1)
        mixed = part if mixed is None else mixed + part
    out_ref[...] = mixed.astype(BF16)


def add_members(*refs):
    term_refs, (out_ref, held_ref) = refs[:-2], refs[-2:]
    ens = lax.axis_index("ens")
    for step, ref in enumerate(term_refs):
        held_ref[partner(ens, step)] = ref[...].astype(F32)
    total = held_ref[0]
    for member in range(1, len(term_refs)):
        total = total + held_ref[member]
    out_ref[...] = total.astype(BF16)


def synthesise(rows_ref, table_ref, grad_ref, out_ref, mark_ref):
    received = rows_ref[...]
    if len(table_ref.shape) == 3:
        spatial = dot(table_ref[...].reshape(received.shape[0], -1), received, 0)
    else:
        spatial = dot(table_ref[...], received)
    result = grad_ref[...].astype(F32) + spatial.reshape(grad_ref.shape)
    out_ref[...] = result.astype(BF16)
    mark_ref[...] = jnp.zeros_like(mark_ref)


def assemble(piece, mark_ref, *refs):
    del mark_ref
    block_refs, (out_ref, held_ref) = refs[:-2], refs[-2:]
    lat = lax.axis_index("lat")
    _, head, cols = held_ref.shape
    for step, ref in enumerate(block_refs):
        held_ref[partner(lat, step)] = unfold(ref[...].astype(F32), head, cols)
    for group in range(len(block_refs)):
        out_ref[group * piece : (group + 1) * piece] = held_ref[group, :piece].astype(BF16)


def finish(own_ref, other_ref, out_ref):
    chan, half = lax.axis_index("chan"), own_ref.shape[1]

    @pl.when(chan != 0)
    def _():
        out_ref[:, :half] = own_ref[...].astype(F32)
        out_ref[:, half:] = other_ref[...].astype(F32)

    @pl.when(chan == 0)
    def _():
        out_ref[:, :half] = other_ref[...].astype(F32)
        out_ref[:, half:] = own_ref[...].astype(F32)


def call(kernel, outs, operands, scratch=(), limit=None):
    sizes = [math.prod(x.shape) * x.dtype.itemsize for x in (*operands, *outs)]
    sizes += [math.prod(x.shape) * 4 for x in scratch]
    return pl.pallas_call(
        lambda *refs: kernel(*refs),
        out_shape=tuple(outs),
        in_specs=[VMEM] * len(operands),
        out_specs=(VMEM,) * len(outs),
        scratch_shapes=scratch,
        compiler_params=pltpu.CompilerParams(
            vmem_limit_bytes=limit or min(56 << 20, (6 << 20) + 4 * sum(sizes))
        ),
        cost_estimate=pl.CostEstimate(
            flops=1000000, bytes_accessed=2 * sum(sizes), transcendentals=0
        ),
    )(*operands)


def swap(blocks, axis, far=False):
    count = len(blocks)
    received = [blocks[0]]
    for step in range(1, count):
        pairs = [
            (device, partner(device, step, count if far else 0)) for device in range(count)
        ]
        received.append(lax.ppermute(blocks[step], axis, pairs))
    return received


def share(block, axis):
    return swap([block] * lax.axis_size(axis), axis)


def cross(blocks, axis, far=False):
    count, cores = len(blocks), lax.axis_size("chan")
    received = [lax.ppermute(blocks[0], "chan", [(core, core ^ 1) for core in range(cores)])]
    for step in range(1, count):
        pairs = []
        for device in range(count):
            other = partner(device, step, count if far else 0)
            for core in range(cores):
                if axis == "lat":
                    pairs.append((device * cores + core, other * cores + (core ^ 1)))
                else:
                    pairs.append((core * count + device, (core ^ 1) * count + other))
        axes = ("lat", "chan") if axis == "lat" else ("chan", axis)
        received.append(lax.ppermute(blocks[step], axes, pairs))
    return received


def shape(*dims, dtype=BF16):
    return jax.ShapeDtypeStruct(dims, dtype)


def on_device(grad_out, pre_act, coeffs, legendre, mixing):
    lat_rows, lon_count, chan_cols = grad_out.shape[1:]
    mode_count = lon_count // 2
    groups = lax.axis_size("lat")
    chan_count = lax.axis_size("chan")
    members = lax.axis_size("ens")
    channels = chan_cols * chan_count
    local_modes, degrees, _ = legendre.shape
    table = analysis_matrix(lat_rows, lon_count, mode_count, groups)
    selections = expansion_tables(
        local_modes, chan_count, degrees, lat_rows, groups, members
    )
    chunk = table.shape[1]
    rows = local_modes * degrees * 2
    piece = channels // groups
    head = padded(piece, 32)
    held = pltpu.VMEM((groups, chunk, chan_cols), F32)
    part = folded(head, chan_cols)
    side = folded(chunk, chan_cols)
    both = shape(part.shape[0] + side.shape[0], side.shape[1])

    legendre_parts = share(jnp.stack(share(legendre.transpose(0, 2, 1), "ens")), "chan")
    spectral = call(
        analyse,
        [side] * groups,
        (silu_backward(grad_out[0], pre_act[0]), jnp.asarray(table)),
        (held,),
    )
    spectral = swap(spectral, "lat", far=True)
    coeffs_parts = [x.reshape(rows, channels) for x in share(coeffs[0], "chan")]
    spread, halves = call(
        prepare,
        [
            shape(chan_count, rows, groups * chunk),
            shape(chan_count, chan_cols, chan_cols),
        ],
        (*legendre_parts, *(jnp.asarray(x) for x in selections), mixing),
    )

    blocks = call(
        lambda *refs: coefficients(
            groups, chan_count, piece, 1.0 / (members * mode_count), *refs
        ),
        [both] * groups,
        (*spectral, spread, *coeffs_parts),
        (
            held,
            pltpu.VMEM((chan_count, rows, chan_cols), BF16),
            pltpu.VMEM((groups, head, chan_cols), F32),
        ),
    )
    blocks = cross(blocks, "lat", far=True)
    returned = shape(groups * chunk, chan_cols)
    total, received = call(
        add_groups, [part, returned], blocks, (held,)
    )
    (mixed,) = call(mix, [returned], (*share(received, "chan"), halves))
    (total,) = call(
        add_members,
        [part],
        cross([total] * members, "ens"),
        (pltpu.VMEM((members, *part.shape), F32),),
    )
    if table.size < 1 << 20:
        back = jnp.asarray(np.ascontiguousarray(table.reshape(-1, lat_rows * lon_count).T))
    else:
        back = jnp.asarray(table)
    result, mark = call(
        synthesise,
        [shape(*grad_out.shape[1:]), shape(8, 128, dtype=F32)],
        (mixed, back, grad_out[0]),
    )
    (total,) = call(
        lambda *refs: assemble(piece, *refs),
        [shape(channels, chan_cols)],
        (mark, *cross([total] * groups, "lat")),
        (pltpu.VMEM((groups, head, chan_cols), F32),),
    )
    (weight_grad,) = call(
        finish, [shape(channels, channels, dtype=F32)], share(total, "chan")
    )
    return (result[None], weight_grad)


def solution(mesh):
    placed = (
        P(("grp", "ens"), "lat", None, "chan"),
        P(("grp", "ens"), "lat", None, "chan"),
        P(("grp", "ens"), ("lat", "chan"), None, None, None),
        P(("lat", "chan"), None, "ens"),
        P(),
    )
    return jax.shard_map(
        on_device,
        mesh=mesh,
        in_specs=placed,
        out_specs=(P(("grp", "ens"), "lat", None, "chan"), P("grp", None)),
        check_vma=False,
    )
```

```python
import math

import jax
import jax.numpy as jnp
import numpy as np
from jax import lax
from jax.experimental import pallas as pl
from jax.experimental.pallas import tpu as pltpu
from jax.sharding import PartitionSpec as P

VMEM = pl.BlockSpec(memory_space=pltpu.VMEM)
BF16 = jnp.bfloat16
F32 = jnp.float32


def fourier_table(lon_count, mode_count):
    longitude = np.arange(lon_count, dtype=np.int32)[:, None]
    wavenumber = np.arange(mode_count, dtype=np.int32)[None, :]
    product_index = longitude * wavenumber % lon_count
    angles = np.float32(2.0 * math.pi / lon_count) * product_index.astype(np.float32)
    factor = np.float32(math.sqrt(2.0 / lon_count))
    stacked = np.stack([np.cos(angles), -np.sin(angles)], axis=2) * factor
    return stacked.reshape(lon_count, 2 * mode_count).astype(BF16)


def padded(rows, tile):
    return -(-rows // tile) * tile


def analysis_matrix(lat_rows, lon_count, mode_count, groups):
    width = 2 * mode_count // groups
    table = np.asarray(fourier_table(lon_count, mode_count)).astype(np.float32)
    table = table.T.reshape(groups, width, lon_count)
    full = np.zeros((groups, lat_rows, width, lat_rows, lon_count), np.float32)
    for row in range(lat_rows):
        full[:, row, :, row, :] = table
    full = full.reshape(groups, lat_rows * width, lat_rows * lon_count)
    out = np.zeros((groups, padded(lat_rows * width, 8), lat_rows * lon_count), np.float32)
    out[:, : lat_rows * width] = full
    return out.astype(BF16)


def expansion_tables(local_modes, chan_count, degrees, lat_rows, groups, members):
    modes = local_modes * chan_count
    width = 2 * modes
    cols = padded(lat_rows * width, 8)
    lat_count = lat_rows * groups
    row = np.arange(local_modes * degrees * 2)
    pick_rows = row[:, None] // 2 == np.arange(local_modes * degrees)[None, :]
    col = np.arange(groups * cols)
    group, inner = col // cols, col % cols
    valid = inner < lat_rows * width
    lat = group * lat_rows + inner // width
    pick_lat = (np.arange(lat_count)[:, None] == lat[None, :]) & valid[None, :]
    kind_of_row = row // (2 * degrees) * 2 + row % 2
    kind_of_row = kind_of_row[None] + 2 * local_modes * np.arange(chan_count)[:, None]
    kind_of_col = inner % width
    kinds = np.arange(width)
    return (
        pick_rows.astype(BF16),
        pick_lat.reshape(members, lat_count // members, groups * cols).astype(BF16),
        (kind_of_row[:, :, None] == kinds).astype(BF16),
        (kinds[:, None] == kind_of_col[None, :]).astype(BF16),
    )


def far_first(count):
    return list(range(count - 1, 0, -1))


def late_first(count):
    order = far_first(count)
    return order[1:2] + order[:1] + order[2:]


def partner(me, step, order=None):
    return me ^ (order[step - 1] if order and step > 0 else step)


def dot(left, right, left_dim=1, right_dim=0):
    return lax.dot_general(
        left, right, (((left_dim,), (right_dim,)), ((), ())), preferred_element_type=F32
    )


def fold_rows(rows, cols):
    return padded(rows - rows // 2, 8) if cols % 128 == 64 and rows >= 16 else 0


def fold(x):
    rows, cols = x.shape
    side = fold_rows(rows, cols)
    if side == 0:
        return x
    full = cols - 64
    right = x[side:, full:]
    if rows - side < side:
        right = jnp.concatenate([right, jnp.zeros((2 * side - rows, 64), x.dtype)], axis=0)
    tail = jnp.concatenate([x[:side, full:], right], axis=1)
    if full > 128:
        tail = jnp.concatenate([tail, jnp.zeros((side, full - 128), x.dtype)], axis=1)
    return jnp.concatenate([x[:, :full], tail], axis=0)


def unfold(x, rows, cols):
    side = fold_rows(rows, cols)
    if side == 0:
        return x
    tail = x[rows:]
    last = jnp.concatenate([tail[:, :64], tail[: rows - side, 64:128]], axis=0)
    return jnp.concatenate([x[:rows], last], axis=1)


def folded(rows, cols):
    side = fold_rows(rows, cols)
    return shape(rows + side, cols - 64) if side else shape(rows, cols)


def silu_backward(cotangent, preact):
    values = preact.astype(F32)
    gate = 1.0 / (1.0 + jnp.exp(-values))
    return (cotangent.astype(F32) * gate * (1.0 + values * (1.0 - gate))).astype(BF16)


def analyse(scaled_ref, table_ref, *refs):
    groups = table_ref.shape[0]
    out_refs, held_ref = refs[:groups], refs[groups]
    scaled = scaled_ref[...].reshape(-1, scaled_ref.shape[2])
    table = table_ref[...].reshape(groups * table_ref.shape[1], -1)
    held_ref[...] = dot(table, scaled).reshape(held_ref.shape)
    me = lax.axis_index("lat")
    for step in range(groups):
        out_refs[step][...] = fold(held_ref[partner(me, step, late_first(groups))]).astype(BF16)


def prepare(*refs):
    legendre_refs = refs[:-7]
    pick_rows_ref, pick_lat_ref, row_kind_ref, col_kind_ref, mixing_ref = refs[-7:-2]
    spread_ref, mixing_out = refs[-2:]
    chan, ens = lax.axis_index("chan"), lax.axis_index("ens")
    for step in range(row_kind_ref.shape[0]):
        core = partner(chan, step)
        blocks = []
        for mode in range(legendre_refs[0].shape[1]):
            total = None
            for place in range(pick_lat_ref.shape[0]):
                pick = pick_lat_ref[partner(ens, place)]
                term = dot(legendre_refs[step][place, mode], pick, 0, 0)
                total = term if total is None else total + term
            blocks.append(total)
        block = jnp.concatenate(blocks, axis=0).astype(BF16)
        keep = dot(row_kind_ref[core], col_kind_ref[...])
        spread_ref[core] = (dot(pick_rows_ref[...], block) * keep).astype(BF16)
    halves, half, _ = mixing_out.shape
    rows = mixing_ref[pl.ds(pl.multiple_of(chan * half, half), half), :]
    for core in range(halves):
        mixing_out[core] = rows[:, core * half : (core + 1) * half]


def coefficients(groups, chan_count, piece, scale, *refs):
    recv_refs = refs[:groups]
    spread_ref = refs[groups]
    coeffs_refs = refs[groups + 1 : groups + 1 + chan_count]
    send_refs = refs[groups + 1 + chan_count : -3]
    held_ref, coef_ref, term_ref = refs[-3:]
    lat, chan = lax.axis_index("lat"), lax.axis_index("chan")
    _, chunk, cols = held_ref.shape
    for step in range(groups):
        block = unfold(recv_refs[step][...].astype(F32), chunk, cols)
        held_ref[partner(lat, step, late_first(groups))] = block
    block = held_ref[...].reshape(-1, cols).astype(BF16)
    back = None
    for core in range(chan_count):
        coef = dot(spread_ref[core], block).astype(BF16)
        coef_ref[core] = coef
        part = dot(spread_ref[core], coef, 0, 0)
        back = part if back is None else back + part
    held_ref[...] = back.reshape(held_ref.shape)
    term = None
    for step in range(chan_count):
        part = dot(coeffs_refs[step][...], coef_ref[partner(chan, step)], 0, 0)
        term = part if term is None else term + part
    term = term * scale
    if piece < term_ref.shape[1]:
        term_ref[:, piece:] = jnp.zeros_like(term_ref[:, piece:])
    for group in range(groups):
        term_ref[group, :piece] = term[group * piece : (group + 1) * piece]
    for step in range(groups):
        target = partner(lat, step, far_first(groups))
        part = fold(term_ref[target]).astype(BF16)
        send_refs[step][: part.shape[0]] = part
        send_refs[step][part.shape[0] :] = fold(held_ref[target]).astype(BF16)


def add_groups(*refs):
    recv_refs, (piece_out, rows_out, held_ref) = refs[:-3], refs[-3:]
    lat = lax.axis_index("lat")
    groups, chunk, cols = held_ref.shape
    head = piece_out.shape[0]
    total = None
    for step, ref in enumerate(recv_refs):
        part = ref[:head].astype(F32)
        total = part if total is None else total + part
        block = unfold(ref[head:].astype(F32), chunk, cols)
        held_ref[partner(lat, step, far_first(groups))] = block
    piece_out[...] = total.astype(BF16)
    rows_out[...] = held_ref[...].reshape(rows_out.shape).astype(BF16)


def mix(*refs):
    rows_refs, (mixing_ref, out_ref) = refs[:-2], refs[-2:]
    chan = lax.axis_index("chan")
    mixed = None
    for step, ref in enumerate(rows_refs):
        part = dot(ref[...], mixing_ref[partner(chan, step ^ 1)], 1, 1)
        mixed = part if mixed is None else mixed + part
    out_ref[...] = mixed.astype(BF16)


def add_members(*refs):
    term_refs, (out_ref, held_ref) = refs[:-2], refs[-2:]
    ens = lax.axis_index("ens")
    for step, ref in enumerate(term_refs):
        held_ref[partner(ens, step)] = ref[...].astype(F32)
    total = held_ref[0]
    for member in range(1, len(term_refs)):
        total = total + held_ref[member]
    out_ref[...] = total.astype(BF16)


def synthesise(rows_ref, table_ref, grad_ref, out_ref, mark_ref):
    received = rows_ref[...]
    if len(table_ref.shape) == 3:
        spatial = dot(table_ref[...].reshape(received.shape[0], -1), received, 0)
    else:
        spatial = dot(table_ref[...], received)
    result = grad_ref[...].astype(F32) + spatial.reshape(grad_ref.shape)
    out_ref[...] = result.astype(BF16)
    mark_ref[...] = jnp.zeros_like(mark_ref)


def assemble(piece, mark_ref, *refs):
    del mark_ref
    block_refs, (out_ref, held_ref) = refs[:-2], refs[-2:]
    lat = lax.axis_index("lat")
    _, head, cols = held_ref.shape
    for step, ref in enumerate(block_refs):
        held_ref[partner(lat, step)] = unfold(ref[...].astype(F32), head, cols)
    for group in range(len(block_refs)):
        out_ref[group * piece : (group + 1) * piece] = held_ref[group, :piece].astype(BF16)


def finish(own_ref, other_ref, out_ref, held_ref, sems):
    chan, (rows, half), parts = lax.axis_index("chan"), own_ref.shape, sems.shape[0]
    copies = []
    for part in range(parts):
        span = pl.ds(part * (rows // parts), rows // parts)

        @pl.when(chan != 0)
        def _():
            held_ref[span, :half] = own_ref[span].astype(F32)
            held_ref[span, half:] = other_ref[span].astype(F32)

        @pl.when(chan == 0)
        def _():
            held_ref[span, :half] = other_ref[span].astype(F32)
            held_ref[span, half:] = own_ref[span].astype(F32)

        copy = pltpu.make_async_copy(held_ref.at[span], out_ref.at[span], sems.at[part])
        copy.start()
        copies.append(copy)
    for copy in copies:
        copy.wait()


def call(kernel, outs, operands, scratch=(), out_space=pltpu.VMEM):
    sizes = [math.prod(x.shape) * x.dtype.itemsize for x in (*operands, *outs)]
    sizes += [math.prod(x.shape) * 4 for x in scratch]
    return pl.pallas_call(
        lambda *refs: kernel(*refs),
        out_shape=tuple(outs),
        in_specs=[VMEM] * len(operands),
        out_specs=(pl.BlockSpec(memory_space=out_space),) * len(outs),
        scratch_shapes=scratch,
        compiler_params=pltpu.CompilerParams(
            vmem_limit_bytes=min(56 << 20, (6 << 20) + 4 * sum(sizes))
        ),
        cost_estimate=pl.CostEstimate(
            flops=1000000, bytes_accessed=2 * sum(sizes), transcendentals=0
        ),
    )(*operands)


def swap(blocks, axis, order=None):
    count = len(blocks)
    received = [blocks[0]]
    for step in range(1, count):
        pairs = [(device, partner(device, step, order)) for device in range(count)]
        received.append(lax.ppermute(blocks[step], axis, pairs))
    return received


def share(block, axis):
    return swap([block] * lax.axis_size(axis), axis)


def cross(blocks, axis, order=None):
    count, cores = len(blocks), lax.axis_size("chan")
    received = [lax.ppermute(blocks[0], "chan", [(core, core ^ 1) for core in range(cores)])]
    for step in range(1, count):
        pairs = []
        for device in range(count):
            other = partner(device, step, order)
            for core in range(cores):
                if axis == "lat":
                    pairs.append((device * cores + core, other * cores + (core ^ 1)))
                else:
                    pairs.append((core * count + device, (core ^ 1) * count + other))
        axes = ("lat", "chan") if axis == "lat" else ("chan", axis)
        received.append(lax.ppermute(blocks[step], axes, pairs))
    return received


def shape(*dims, dtype=BF16):
    return jax.ShapeDtypeStruct(dims, dtype)


def on_device(grad_out, pre_act, coeffs, legendre, mixing):
    lat_rows, lon_count, chan_cols = grad_out.shape[1:]
    mode_count = lon_count // 2
    groups = lax.axis_size("lat")
    chan_count = lax.axis_size("chan")
    members = lax.axis_size("ens")
    channels = chan_cols * chan_count
    local_modes, degrees, _ = legendre.shape
    table = analysis_matrix(lat_rows, lon_count, mode_count, groups)
    selections = expansion_tables(
        local_modes, chan_count, degrees, lat_rows, groups, members
    )
    chunk = table.shape[1]
    rows = local_modes * degrees * 2
    piece = channels // groups
    head = padded(piece, 32)
    held = pltpu.VMEM((groups, chunk, chan_cols), F32)
    part = folded(head, chan_cols)
    side = folded(chunk, chan_cols)
    both = shape(part.shape[0] + side.shape[0], side.shape[1])

    legendre_parts = share(jnp.stack(share(legendre.transpose(0, 2, 1), "ens")), "chan")
    spectral = call(
        analyse,
        [side] * groups,
        (silu_backward(grad_out[0], pre_act[0]), jnp.asarray(table)),
        (held,),
    )
    spectral = swap(spectral, "lat", late_first(groups))
    coeffs_parts = [x.reshape(rows, channels) for x in share(coeffs[0], "chan")]
    spread, halves = call(
        prepare,
        [
            shape(chan_count, rows, groups * chunk),
            shape(chan_count, chan_cols, chan_cols),
        ],
        (*legendre_parts, *(jnp.asarray(x) for x in selections), mixing),
    )

    blocks = call(
        lambda *refs: coefficients(
            groups, chan_count, piece, 1.0 / (members * mode_count), *refs
        ),
        [both] * groups,
        (*spectral, spread, *coeffs_parts),
        (
            held,
            pltpu.VMEM((chan_count, rows, chan_cols), BF16),
            pltpu.VMEM((groups, head, chan_cols), F32),
        ),
    )
    blocks = cross(blocks, "lat", far_first(groups))
    returned = shape(groups * chunk, chan_cols)
    total, received = call(
        add_groups, [part, returned], blocks, (held,)
    )
    (mixed,) = call(mix, [returned], (*share(received, "chan"), halves))
    (total,) = call(
        add_members,
        [part],
        cross([total] * members, "ens"),
        (pltpu.VMEM((members, *part.shape), F32),),
    )
    if table.size < 1 << 20:
        back = jnp.asarray(np.ascontiguousarray(table.reshape(-1, lat_rows * lon_count).T))
    else:
        back = jnp.asarray(table)
    result, mark = call(
        synthesise,
        [shape(*grad_out.shape[1:]), shape(8, 128, dtype=F32)],
        (mixed, back, grad_out[0]),
    )
    (total,) = call(
        lambda *refs: assemble(piece, *refs),
        [shape(channels, chan_cols)],
        (mark, *cross([total] * groups, "lat")),
        (pltpu.VMEM((groups, head, chan_cols), F32),),
    )
    (weight_grad,) = call(
        finish,
        [shape(channels, channels, dtype=F32)],
        share(total, "chan"),
        (pltpu.VMEM((channels, channels), F32), pltpu.SemaphoreType.DMA((3,))),
        pl.ANY,
    )
    return (result[None], weight_grad)


def solution(mesh):
    placed = (
        P(("grp", "ens"), "lat", None, "chan"),
        P(("grp", "ens"), "lat", None, "chan"),
        P(("grp", "ens"), ("lat", "chan"), None, None, None),
        P(("lat", "chan"), None, "ens"),
        P(),
    )
    return jax.shard_map(
        on_device,
        mesh=mesh,
        in_specs=placed,
        out_specs=(P(("grp", "ens"), "lat", None, "chan"), P("grp", None)),
        check_vma=False,
    )
```

```python
import math

import jax
import jax.numpy as jnp
import numpy as np
from jax import lax
from jax.experimental import pallas as pl
from jax.experimental.pallas import tpu as pltpu
from jax.sharding import PartitionSpec as P

VMEM = pl.BlockSpec(memory_space=pltpu.VMEM)
BF16 = jnp.bfloat16
F32 = jnp.float32


def fourier_table(lon_count, mode_count):
    longitude = np.arange(lon_count, dtype=np.int32)[:, None]
    wavenumber = np.arange(mode_count, dtype=np.int32)[None, :]
    product_index = longitude * wavenumber % lon_count
    angles = np.float32(2.0 * math.pi / lon_count) * product_index.astype(np.float32)
    factor = np.float32(math.sqrt(2.0 / lon_count))
    stacked = np.stack([np.cos(angles), -np.sin(angles)], axis=2) * factor
    return stacked.reshape(lon_count, 2 * mode_count).astype(BF16)


def padded(rows, tile):
    return -(-rows // tile) * tile


def analysis_matrix(lat_rows, lon_count, mode_count, groups):
    width = 2 * mode_count // groups
    table = np.asarray(fourier_table(lon_count, mode_count)).astype(np.float32)
    table = table.T.reshape(groups, width, lon_count)
    full = np.zeros((groups, lat_rows, width, lat_rows, lon_count), np.float32)
    for row in range(lat_rows):
        full[:, row, :, row, :] = table
    full = full.reshape(groups, lat_rows * width, lat_rows * lon_count)
    out = np.zeros((groups, padded(lat_rows * width, 8), lat_rows * lon_count), np.float32)
    out[:, : lat_rows * width] = full
    return out.astype(BF16)


def expansion_tables(local_modes, chan_count, degrees, lat_rows, groups, members):
    modes = local_modes * chan_count
    width = 2 * modes
    cols = padded(lat_rows * width, 8)
    lat_count = lat_rows * groups
    row = np.arange(local_modes * degrees * 2)
    pick_rows = row[:, None] // 2 == np.arange(local_modes * degrees)[None, :]
    col = np.arange(groups * cols)
    group, inner = col // cols, col % cols
    valid = inner < lat_rows * width
    lat = group * lat_rows + inner // width
    pick_lat = (np.arange(lat_count)[:, None] == lat[None, :]) & valid[None, :]
    kind_of_row = row // (2 * degrees) * 2 + row % 2
    kind_of_row = kind_of_row[None] + 2 * local_modes * np.arange(chan_count)[:, None]
    kind_of_col = inner % width
    kinds = np.arange(width)
    return (
        pick_rows.astype(BF16),
        pick_lat.reshape(members, lat_count // members, groups * cols).astype(BF16),
        (kind_of_row[:, :, None] == kinds).astype(BF16),
        (kinds[:, None] == kind_of_col[None, :]).astype(BF16),
    )


def partner(me, step, count=0):
    return me ^ (count - step if step > 0 and count > 0 else step)


def dot(left, right, left_dim=1, right_dim=0):
    return lax.dot_general(
        left, right, (((left_dim,), (right_dim,)), ((), ())), preferred_element_type=F32
    )


def fold_rows(rows, cols):
    return padded(rows - rows // 2, 8) if cols % 128 == 64 and rows >= 16 else 0


def fold(x):
    rows, cols = x.shape
    side = fold_rows(rows, cols)
    if side == 0:
        return x
    full = cols - 64
    right = x[side:, full:]
    if rows - side < side:
        right = jnp.concatenate([right, jnp.zeros((2 * side - rows, 64), x.dtype)], axis=0)
    tail = jnp.concatenate([x[:side, full:], right], axis=1)
    if full > 128:
        tail = jnp.concatenate([tail, jnp.zeros((side, full - 128), x.dtype)], axis=1)
    return jnp.concatenate([x[:, :full], tail], axis=0)


def unfold(x, rows, cols):
    side = fold_rows(rows, cols)
    if side == 0:
        return x
    tail = x[rows:]
    last = jnp.concatenate([tail[:, :64], tail[: rows - side, 64:128]], axis=0)
    return jnp.concatenate([x[:rows], last], axis=1)


def folded(rows, cols):
    side = fold_rows(rows, cols)
    return shape(rows + side, cols - 64) if side else shape(rows, cols)


def silu_backward(cotangent, preact):
    values = preact.astype(F32)
    gate = 1.0 / (1.0 + jnp.exp(-values))
    return (cotangent.astype(F32) * gate * (1.0 + values * (1.0 - gate))).astype(BF16)


def analyse(scaled_ref, table_ref, coeffs_ref, *refs):
    groups = table_ref.shape[0]
    out_refs, held_ref = refs[:groups], refs[groups]
    scaled = scaled_ref[...].reshape(-1, scaled_ref.shape[2])
    table = table_ref[...].reshape(groups * table_ref.shape[1], -1)
    held_ref[...] = dot(table, scaled).reshape(held_ref.shape)
    me = lax.axis_index("lat")
    for step in range(groups):
        block = fold(held_ref[partner(me, step, groups)]).astype(BF16)
        out_refs[step][: block.shape[0]] = block
    rows, channels = coeffs_ref.shape
    for place in range(channels // 128):
        first = out_refs[1].shape[0] + place * rows
        out_refs[0][first : first + rows] = coeffs_ref[:, place * 128 : (place + 1) * 128]


def prepare(*refs):
    legendre_refs = refs[:-7]
    pick_rows_ref, pick_lat_ref, row_kind_ref, col_kind_ref, mixing_ref = refs[-7:-2]
    spread_ref, mixing_out = refs[-2:]
    chan, ens = lax.axis_index("chan"), lax.axis_index("ens")
    for step in range(row_kind_ref.shape[0]):
        core = partner(chan, step)
        blocks = []
        for mode in range(legendre_refs[0].shape[1]):
            total = None
            for place in range(pick_lat_ref.shape[0]):
                pick = pick_lat_ref[partner(ens, place)]
                term = dot(legendre_refs[step][place, mode], pick, 0, 0)
                total = term if total is None else total + term
            blocks.append(total)
        block = jnp.concatenate(blocks, axis=0).astype(BF16)
        keep = dot(row_kind_ref[core], col_kind_ref[...])
        spread_ref[core] = (dot(pick_rows_ref[...], block) * keep).astype(BF16)
    halves, half, _ = mixing_out.shape
    rows = mixing_ref[pl.ds(pl.multiple_of(chan * half, half), half), :]
    for core in range(halves):
        mixing_out[core] = rows[:, core * half : (core + 1) * half]


def coefficients(groups, chan_count, piece, scale, *refs):
    recv_refs = refs[:groups]
    spread_ref, coeffs_ref = refs[groups : groups + 2]
    send_refs = refs[groups + 2 : -3]
    held_ref, coef_ref, term_ref = refs[-3:]
    lat, chan = lax.axis_index("lat"), lax.axis_index("chan")
    _, chunk, cols = held_ref.shape
    for step in range(groups):
        block = recv_refs[step][: recv_refs[1].shape[0]].astype(F32)
        held_ref[partner(lat, step, groups)] = unfold(block, chunk, cols)
    block = held_ref[...].reshape(-1, cols).astype(BF16)
    back = None
    for core in range(chan_count):
        coef = dot(spread_ref[core], block).astype(BF16)
        coef_ref[core] = coef
        part = dot(spread_ref[core], coef, 0, 0)
        back = part if back is None else back + part
    held_ref[...] = back.reshape(held_ref.shape)
    rows, channels = coeffs_ref.shape
    first = recv_refs[1].shape[0]
    others = [
        recv_refs[0][first + place * rows : first + (place + 1) * rows]
        for place in range(channels // 128)
    ]
    stored = [coeffs_ref[...], jnp.concatenate(others, axis=1)]
    term = None
    for step in range(chan_count):
        part = dot(stored[step], coef_ref[partner(chan, step)], 0, 0)
        term = part if term is None else term + part
    term = term * scale
    if piece < term_ref.shape[1]:
        term_ref[:, piece:] = jnp.zeros_like(term_ref[:, piece:])
    for group in range(groups):
        term_ref[group, :piece] = term[group * piece : (group + 1) * piece]
    for step in range(groups):
        target = partner(lat, step, groups)
        part = fold(term_ref[target]).astype(BF16)
        send_refs[step][: part.shape[0]] = part
        send_refs[step][part.shape[0] :] = fold(held_ref[target]).astype(BF16)


def add_groups(*refs):
    recv_refs, (piece_out, rows_out, held_ref) = refs[:-3], refs[-3:]
    lat = lax.axis_index("lat")
    groups, chunk, cols = held_ref.shape
    head = piece_out.shape[0]
    total = None
    for step, ref in enumerate(recv_refs):
        part = ref[:head].astype(F32)
        total = part if total is None else total + part
        block = unfold(ref[head:].astype(F32), chunk, cols)
        held_ref[partner(lat, step, groups)] = block
    piece_out[...] = total.astype(BF16)
    rows_out[...] = held_ref[...].reshape(rows_out.shape).astype(BF16)


def mix(*refs):
    rows_refs, (mixing_ref, out_ref) = refs[:-2], refs[-2:]
    chan = lax.axis_index("chan")
    mixed = None
    for step, ref in enumerate(rows_refs):
        part = dot(ref[...], mixing_ref[partner(chan, step)], 1, 1)
        mixed = part if mixed is None else mixed + part
    out_ref[...] = mixed.astype(BF16)


def add_members(*refs):
    term_refs, (out_ref, held_ref) = refs[:-2], refs[-2:]
    ens = lax.axis_index("ens")
    for step, ref in enumerate(term_refs):
        held_ref[partner(ens, step)] = ref[...].astype(F32)
    total = held_ref[0]
    for member in range(1, len(term_refs)):
        total = total + held_ref[member]
    out_ref[...] = total.astype(BF16)


def synthesise(rows_ref, table_ref, grad_ref, out_ref, mark_ref):
    received = rows_ref[...]
    if len(table_ref.shape) == 3:
        spatial = dot(table_ref[...].reshape(received.shape[0], -1), received, 0)
    else:
        spatial = dot(table_ref[...], received)
    result = grad_ref[...].astype(F32) + spatial.reshape(grad_ref.shape)
    out_ref[...] = result.astype(BF16)
    mark_ref[...] = jnp.zeros_like(mark_ref)


def assemble(piece, mark_ref, *refs):
    del mark_ref
    block_refs, (out_ref, held_ref) = refs[:-2], refs[-2:]
    lat = lax.axis_index("lat")
    _, head, cols = held_ref.shape
    for step, ref in enumerate(block_refs):
        held_ref[partner(lat, step)] = unfold(ref[...].astype(F32), head, cols)
    for group in range(len(block_refs)):
        out_ref[group * piece : (group + 1) * piece] = held_ref[group, :piece].astype(BF16)


def finish(own_ref, other_ref, out_ref):
    chan, half = lax.axis_index("chan"), own_ref.shape[1]

    @pl.when(chan == 0)
    def _():
        out_ref[:, :half] = own_ref[...].astype(F32)
        out_ref[:, half:] = other_ref[...].astype(F32)

    @pl.when(chan != 0)
    def _():
        out_ref[:, :half] = other_ref[...].astype(F32)
        out_ref[:, half:] = own_ref[...].astype(F32)


def call(kernel, outs, operands, scratch=(), limit=None):
    sizes = [math.prod(x.shape) * x.dtype.itemsize for x in (*operands, *outs)]
    sizes += [math.prod(x.shape) * 4 for x in scratch]
    return pl.pallas_call(
        lambda *refs: kernel(*refs),
        out_shape=tuple(outs),
        in_specs=[VMEM] * len(operands),
        out_specs=(VMEM,) * len(outs),
        scratch_shapes=scratch,
        compiler_params=pltpu.CompilerParams(
            vmem_limit_bytes=limit or min(56 << 20, (6 << 20) + 4 * sum(sizes))
        ),
        cost_estimate=pl.CostEstimate(
            flops=1000000, bytes_accessed=2 * sum(sizes), transcendentals=0
        ),
    )(*operands)


def swap(blocks, axis, far=False):
    count = len(blocks)
    received = [blocks[0]]
    for step in range(1, count):
        pairs = [
            (device, partner(device, step, count if far else 0)) for device in range(count)
        ]
        received.append(lax.ppermute(blocks[step], axis, pairs))
    return received


def share(block, axis):
    return swap([block] * lax.axis_size(axis), axis)


def cross(blocks, axis, far=False):
    count, cores = len(blocks), lax.axis_size("chan")
    received = [lax.ppermute(blocks[0], "chan", [(core, core ^ 1) for core in range(cores)])]
    for step in range(1, count):
        pairs = []
        for device in range(count):
            other = partner(device, step, count if far else 0)
            for core in range(cores):
                if axis == "lat":
                    pairs.append((device * cores + core, other * cores + (core ^ 1)))
                else:
                    pairs.append((core * count + device, (core ^ 1) * count + other))
        axes = ("lat", "chan") if axis == "lat" else ("chan", axis)
        received.append(lax.ppermute(blocks[step], axes, pairs))
    return received


def shape(*dims, dtype=BF16):
    return jax.ShapeDtypeStruct(dims, dtype)


def on_device(grad_out, pre_act, coeffs, legendre, mixing):
    lat_rows, lon_count, chan_cols = grad_out.shape[1:]
    mode_count = lon_count // 2
    groups = lax.axis_size("lat")
    chan_count = lax.axis_size("chan")
    members = lax.axis_size("ens")
    channels = chan_cols * chan_count
    local_modes, degrees, _ = legendre.shape
    table = analysis_matrix(lat_rows, lon_count, mode_count, groups)
    selections = expansion_tables(
        local_modes, chan_count, degrees, lat_rows, groups, members
    )
    chunk = table.shape[1]
    rows = local_modes * degrees * 2
    piece = channels // groups
    head = padded(piece, 32)
    held = pltpu.VMEM((groups, chunk, chan_cols), F32)
    part = folded(head, chan_cols)
    side = folded(chunk, chan_cols)
    both = shape(part.shape[0] + side.shape[0], side.shape[1])

    legendre_parts = share(jnp.stack(share(legendre.transpose(0, 2, 1), "ens")), "chan")
    stored = coeffs[0].reshape(rows, channels)
    spectral = call(
        analyse,
        [shape(side.shape[0] + rows * channels // 128, 128), *[side] * (groups - 1)],
        (silu_backward(grad_out[0], pre_act[0]), jnp.asarray(table), stored),
        (held,),
    )
    spectral = cross(spectral, "lat", far=True)
    spread, halves = call(
        prepare,
        [
            shape(chan_count, rows, groups * chunk),
            shape(chan_count, chan_cols, chan_cols),
        ],
        (*legendre_parts, *(jnp.asarray(x) for x in selections), mixing),
    )

    blocks = call(
        lambda *refs: coefficients(
            groups, chan_count, piece, 1.0 / (members * mode_count), *refs
        ),
        [both] * groups,
        (*spectral, spread, stored),
        (
            held,
            pltpu.VMEM((chan_count, rows, chan_cols), BF16),
            pltpu.VMEM((groups, head, chan_cols), F32),
        ),
    )
    blocks = cross(blocks, "lat", far=True)
    returned = shape(groups * chunk, chan_cols)
    total, received = call(
        add_groups, [part, returned], blocks, (held,)
    )
    (mixed,) = call(mix, [returned], (*share(received, "chan"), halves))
    (total,) = call(
        add_members,
        [part],
        cross([total] * members, "ens"),
        (pltpu.VMEM((members, *part.shape), F32),),
    )
    if table.size < 1 << 20:
        back = jnp.asarray(np.ascontiguousarray(table.reshape(-1, lat_rows * lon_count).T))
    else:
        back = jnp.asarray(table)
    result, mark = call(
        synthesise,
        [shape(*grad_out.shape[1:]), shape(8, 128, dtype=F32)],
        (mixed, back, grad_out[0]),
    )
    (total,) = call(
        lambda *refs: assemble(piece, *refs),
        [shape(channels, chan_cols)],
        (mark, *cross([total] * groups, "lat")),
        (pltpu.VMEM((groups, head, chan_cols), F32),),
    )
    (weight_grad,) = call(
        finish, [shape(channels, channels, dtype=F32)], share(total, "chan")
    )
    return (result[None], weight_grad)


def solution(mesh):
    placed = (
        P(("grp", "ens"), "lat", None, "chan"),
        P(("grp", "ens"), "lat", None, "chan"),
        P(("grp", "ens"), ("lat", "chan"), None, None, None),
        P(("lat", "chan"), None, "ens"),
        P(),
    )
    return jax.shard_map(
        on_device,
        mesh=mesh,
        in_specs=placed,
        out_specs=(P(("grp", "ens"), "lat", None, "chan"), P("grp", None)),
        check_vma=False,
    )
```

```python
import math

import jax
import jax.numpy as jnp
import numpy as np
from jax import lax
from jax.experimental import pallas as pl
from jax.experimental.pallas import tpu as pltpu
from jax.sharding import PartitionSpec as P

VMEM = pl.BlockSpec(memory_space=pltpu.VMEM)
BF16 = jnp.bfloat16
F32 = jnp.float32


def fourier_table(lon_count, mode_count):
    longitude = np.arange(lon_count, dtype=np.int32)[:, None]
    wavenumber = np.arange(mode_count, dtype=np.int32)[None, :]
    product_index = longitude * wavenumber % lon_count
    angles = np.float32(2.0 * math.pi / lon_count) * product_index.astype(np.float32)
    factor = np.float32(math.sqrt(2.0 / lon_count))
    stacked = np.stack([np.cos(angles), -np.sin(angles)], axis=2) * factor
    return stacked.reshape(lon_count, 2 * mode_count).astype(BF16)


def padded(rows, tile):
    return -(-rows // tile) * tile


def analysis_matrix(lat_rows, lon_count, mode_count, groups):
    width = 2 * mode_count // groups
    table = np.asarray(fourier_table(lon_count, mode_count)).astype(np.float32)
    table = table.T.reshape(groups, width, lon_count)
    full = np.zeros((groups, lat_rows, width, lat_rows, lon_count), np.float32)
    for row in range(lat_rows):
        full[:, row, :, row, :] = table
    full = full.reshape(groups, lat_rows * width, lat_rows * lon_count)
    out = np.zeros((groups, padded(lat_rows * width, 8), lat_rows * lon_count), np.float32)
    out[:, : lat_rows * width] = full
    return out.astype(BF16)


def expansion_tables(local_modes, chan_count, degrees, lat_rows, groups, members):
    modes = local_modes * chan_count
    width = 2 * modes
    cols = padded(lat_rows * width, 8)
    lat_count = lat_rows * groups
    row = np.arange(local_modes * degrees * 2)
    pick_rows = row[:, None] // 2 == np.arange(local_modes * degrees)[None, :]
    col = np.arange(groups * cols)
    group, inner = col // cols, col % cols
    valid = inner < lat_rows * width
    lat = group * lat_rows + inner // width
    pick_lat = (np.arange(lat_count)[:, None] == lat[None, :]) & valid[None, :]
    kind_of_row = row // (2 * degrees) * 2 + row % 2
    kind_of_row = kind_of_row[None] + 2 * local_modes * np.arange(chan_count)[:, None]
    kind_of_col = inner % width
    kinds = np.arange(width)
    return (
        pick_rows.astype(BF16),
        pick_lat.reshape(members, lat_count // members, groups * cols).astype(BF16),
        (kind_of_row[:, :, None] == kinds).astype(BF16),
        (kinds[:, None] == kind_of_col[None, :]).astype(BF16),
    )


def partner(me, step, count=0):
    return me ^ (count - step if step > 0 and count > 0 else step)


def dot(left, right, left_dim=1, right_dim=0):
    return lax.dot_general(
        left, right, (((left_dim,), (right_dim,)), ((), ())), preferred_element_type=F32
    )


def fold_rows(rows, cols):
    return padded(rows - rows // 2, 8) if cols % 128 == 64 and rows >= 16 else 0


def fold(x):
    rows, cols = x.shape
    side = fold_rows(rows, cols)
    if side == 0:
        return x
    full = cols - 64
    right = x[side:, full:]
    if rows - side < side:
        right = jnp.concatenate([right, jnp.zeros((2 * side - rows, 64), x.dtype)], axis=0)
    tail = jnp.concatenate([x[:side, full:], right], axis=1)
    if full > 128:
        tail = jnp.concatenate([tail, jnp.zeros((side, full - 128), x.dtype)], axis=1)
    return jnp.concatenate([x[:, :full], tail], axis=0)


def unfold(x, rows, cols):
    side = fold_rows(rows, cols)
    if side == 0:
        return x
    tail = x[rows:]
    last = jnp.concatenate([tail[:, :64], tail[: rows - side, 64:128]], axis=0)
    return jnp.concatenate([x[:rows], last], axis=1)


def folded(rows, cols):
    side = fold_rows(rows, cols)
    return shape(rows + side, cols - 64) if side else shape(rows, cols)


def silu_backward(cotangent, preact):
    values = preact.astype(F32)
    gate = 1.0 / (1.0 + jnp.exp(-values))
    return (cotangent.astype(F32) * gate * (1.0 + values * (1.0 - gate))).astype(BF16)


def analyse(scaled_ref, table_ref, *refs):
    groups = table_ref.shape[0]
    out_refs, held_ref = refs[:groups], refs[groups]
    scaled = scaled_ref[...].reshape(-1, scaled_ref.shape[2])
    table = table_ref[...].reshape(groups * table_ref.shape[1], -1)
    held_ref[...] = dot(table, scaled).reshape(held_ref.shape)
    me = lax.axis_index("lat")
    for step in range(groups):
        out_refs[step][...] = fold(held_ref[partner(me, step, groups)]).astype(BF16)


def prepare(*refs):
    legendre_refs = refs[:-7]
    pick_rows_ref, pick_lat_ref, row_kind_ref, col_kind_ref, mixing_ref = refs[-7:-2]
    spread_ref, mixing_out = refs[-2:]
    chan, ens = lax.axis_index("chan"), lax.axis_index("ens")
    for step in range(row_kind_ref.shape[0]):
        core = partner(chan, step)
        blocks = []
        for mode in range(legendre_refs[0].shape[1]):
            total = None
            for place in range(pick_lat_ref.shape[0]):
                pick = pick_lat_ref[partner(ens, place)]
                term = dot(legendre_refs[step][place, mode], pick, 0, 0)
                total = term if total is None else total + term
            blocks.append(total)
        block = jnp.concatenate(blocks, axis=0).astype(BF16)
        keep = dot(row_kind_ref[core], col_kind_ref[...])
        spread_ref[core] = (dot(pick_rows_ref[...], block) * keep).astype(BF16)
    halves, half, _ = mixing_out.shape
    rows = mixing_ref[pl.ds(pl.multiple_of(chan * half, half), half), :]
    for core in range(halves):
        mixing_out[core] = rows[:, core * half : (core + 1) * half]


def coefficients(groups, chan_count, piece, scale, *refs):
    recv_refs = refs[:groups]
    spread_ref = refs[groups]
    coeffs_refs = refs[groups + 1 : groups + 1 + chan_count]
    send_refs = refs[groups + 1 + chan_count : -3]
    held_ref, coef_ref, term_ref = refs[-3:]
    lat, chan = lax.axis_index("lat"), lax.axis_index("chan")
    _, chunk, cols = held_ref.shape
    for step in range(groups):
        block = unfold(recv_refs[step][...].astype(F32), chunk, cols)
        held_ref[partner(lat, step, groups)] = block
    block = held_ref[...].reshape(-1, cols).astype(BF16)
    back = None
    for core in range(chan_count):
        coef = dot(spread_ref[core], block).astype(BF16)
        coef_ref[core] = coef
        part = dot(spread_ref[core], coef, 0, 0)
        back = part if back is None else back + part
    held_ref[...] = back.reshape(held_ref.shape)
    term = None
    for step in range(chan_count):
        part = dot(coeffs_refs[step][...], coef_ref[partner(chan, step)], 0, 0)
        term = part if term is None else term + part
    term = term * scale
    if piece < term_ref.shape[1]:
        term_ref[:, piece:] = jnp.zeros_like(term_ref[:, piece:])
    for group in range(groups):
        term_ref[group, :piece] = term[group * piece : (group + 1) * piece]
    for step in range(groups):
        target = partner(lat, step, groups)
        part = fold(term_ref[target]).astype(BF16)
        send_refs[step - 1][: part.shape[0]] = part
        send_refs[step - 1][part.shape[0] :] = fold(held_ref[target]).astype(BF16)


def add_groups(*refs):
    recv_refs, (piece_out, rows_out, held_ref) = refs[:-3], refs[-3:]
    lat = lax.axis_index("lat")
    groups, chunk, cols = held_ref.shape
    head = piece_out.shape[0]
    total = None
    for place, ref in enumerate(recv_refs):
        step = (place + 1) % groups
        part = ref[:head].astype(F32)
        total = part if total is None else total + part
        block = unfold(ref[head:].astype(F32), chunk, cols)
        held_ref[partner(lat, step, groups)] = block
    piece_out[...] = total.astype(BF16)
    rows_out[...] = held_ref[...].reshape(rows_out.shape).astype(BF16)


def mix(*refs):
    rows_refs, (mixing_ref, out_ref) = refs[:-2], refs[-2:]
    chan = lax.axis_index("chan")
    mixed = None
    for step, ref in enumerate(rows_refs):
        part = dot(ref[...], mixing_ref[partner(chan, step ^ 1)], 1, 1)
        mixed = part if mixed is None else mixed + part
    out_ref[...] = mixed.astype(BF16)


def add_members(mark_ref, *refs):
    del mark_ref
    term_refs, (out_ref, held_ref) = refs[:-2], refs[-2:]
    ens = lax.axis_index("ens")
    for step, ref in enumerate(term_refs):
        held_ref[partner(ens, step)] = ref[...].astype(F32)
    total = held_ref[0]
    for member in range(1, len(term_refs)):
        total = total + held_ref[member]
    out_ref[...] = total.astype(BF16)


def synthesise(rows_ref, table_ref, grad_ref, out_ref, mark_ref):
    received = rows_ref[...]
    if len(table_ref.shape) == 3:
        spatial = dot(table_ref[...].reshape(received.shape[0], -1), received, 0)
    else:
        spatial = dot(table_ref[...], received)
    result = grad_ref[...].astype(F32) + spatial.reshape(grad_ref.shape)
    out_ref[...] = result.astype(BF16)
    mark_ref[...] = jnp.zeros_like(mark_ref)


def assemble(piece, *refs):
    block_refs, (out_ref, held_ref) = refs[:-2], refs[-2:]
    lat = lax.axis_index("lat")
    _, head, cols = held_ref.shape
    for step, ref in enumerate(block_refs):
        held_ref[partner(lat, step)] = unfold(ref[...].astype(F32), head, cols)
    for group in range(len(block_refs)):
        out_ref[group * piece : (group + 1) * piece] = held_ref[group, :piece].astype(BF16)


def finish(piece, own_ref, *refs):
    piece_refs, (out_ref, held_ref) = refs[:-2], refs[-2:]
    lat, chan = lax.axis_index("lat"), lax.axis_index("chan")
    half, head = own_ref.shape[1], held_ref.shape[1]
    for step, ref in enumerate(piece_refs):
        held_ref[partner(lat, step)] = unfold(ref[...].astype(F32), head, half)

    @pl.when(chan != 0)
    def _():
        out_ref[:, :half] = own_ref[...].astype(F32)
        for group in range(len(piece_refs)):
            out_ref[group * piece : (group + 1) * piece, half:] = held_ref[group, :piece]

    @pl.when(chan == 0)
    def _():
        for group in range(len(piece_refs)):
            out_ref[group * piece : (group + 1) * piece, :half] = held_ref[group, :piece]
        out_ref[:, half:] = own_ref[...].astype(F32)


def call(kernel, outs, operands, scratch=(), limit=None):
    sizes = [math.prod(x.shape) * x.dtype.itemsize for x in (*operands, *outs)]
    sizes += [math.prod(x.shape) * 4 for x in scratch]
    return pl.pallas_call(
        lambda *refs: kernel(*refs),
        out_shape=tuple(outs),
        in_specs=[VMEM] * len(operands),
        out_specs=(VMEM,) * len(outs),
        scratch_shapes=scratch,
        compiler_params=pltpu.CompilerParams(
            vmem_limit_bytes=limit or min(56 << 20, (6 << 20) + 4 * sum(sizes))
        ),
        cost_estimate=pl.CostEstimate(
            flops=1000000, bytes_accessed=2 * sum(sizes), transcendentals=0
        ),
    )(*operands)


def swap(blocks, axis, far=False):
    count = len(blocks)
    received = [blocks[0]]
    for step in range(1, count):
        pairs = [
            (device, partner(device, step, count if far else 0)) for device in range(count)
        ]
        received.append(lax.ppermute(blocks[step], axis, pairs))
    return received


def share(block, axis):
    return swap([block] * lax.axis_size(axis), axis)


def cross(blocks, axis, far=False):
    count, cores = len(blocks), lax.axis_size("chan")
    received = []
    for step in range(1, count):
        pairs = []
        for device in range(count):
            other = partner(device, step, count if far else 0)
            for core in range(cores):
                if axis == "lat":
                    pairs.append((device * cores + core, other * cores + (core ^ 1)))
                else:
                    pairs.append((core * count + device, (core ^ 1) * count + other))
        axes = ("lat", "chan") if axis == "lat" else ("chan", axis)
        received.append(lax.ppermute(blocks[step], axes, pairs))
    return [turn(blocks[0]), *received]


def turn(block):
    cores = lax.axis_size("chan")
    return lax.ppermute(block, "chan", [(core, core ^ 1) for core in range(cores)])


def shape(*dims, dtype=BF16):
    return jax.ShapeDtypeStruct(dims, dtype)


def on_device(grad_out, pre_act, coeffs, legendre, mixing):
    lat_rows, lon_count, chan_cols = grad_out.shape[1:]
    mode_count = lon_count // 2
    groups = lax.axis_size("lat")
    chan_count = lax.axis_size("chan")
    members = lax.axis_size("ens")
    channels = chan_cols * chan_count
    local_modes, degrees, _ = legendre.shape
    table = analysis_matrix(lat_rows, lon_count, mode_count, groups)
    selections = expansion_tables(
        local_modes, chan_count, degrees, lat_rows, groups, members
    )
    chunk = table.shape[1]
    rows = local_modes * degrees * 2
    piece = channels // groups
    head = padded(piece, 32)
    held = pltpu.VMEM((groups, chunk, chan_cols), F32)
    part = folded(head, chan_cols)
    side = folded(chunk, chan_cols)
    both = shape(part.shape[0] + side.shape[0], side.shape[1])

    legendre_parts = share(jnp.stack(share(legendre.transpose(0, 2, 1), "ens")), "chan")
    spectral = call(
        analyse,
        [side] * groups,
        (silu_backward(grad_out[0], pre_act[0]), jnp.asarray(table)),
        (held,),
    )
    spectral = swap(spectral, "lat", far=True)
    coeffs_parts = [x.reshape(rows, channels) for x in share(coeffs[0], "chan")]
    spread, halves = call(
        prepare,
        [
            shape(chan_count, rows, groups * chunk),
            shape(chan_count, chan_cols, chan_cols),
        ],
        (*legendre_parts, *(jnp.asarray(x) for x in selections), mixing),
    )

    blocks = call(
        lambda *refs: coefficients(
            groups, chan_count, piece, 1.0 / (members * mode_count), *refs
        ),
        [both] * groups,
        (*spectral, spread, *coeffs_parts),
        (
            held,
            pltpu.VMEM((chan_count, rows, chan_cols), BF16),
            pltpu.VMEM((groups, head, chan_cols), F32),
        ),
    )
    blocks = cross([blocks[-1], *blocks[:-1]], "lat", far=True)
    blocks = [*blocks[1:], blocks[0]]
    returned = shape(groups * chunk, chan_cols)
    total, received = call(
        add_groups, [part, returned], blocks, (held,)
    )
    (mixed,) = call(mix, [returned], (*share(received, "chan"), halves))
    if table.size < 1 << 20:
        back = jnp.asarray(np.ascontiguousarray(table.reshape(-1, lat_rows * lon_count).T))
    else:
        back = jnp.asarray(table)
    result, mark = call(
        synthesise,
        [shape(*grad_out.shape[1:]), shape(8, 128, dtype=F32)],
        (mixed, back, grad_out[0]),
    )
    (total,) = call(
        add_members,
        [part],
        (mark, *cross([total] * members, "ens")),
        (pltpu.VMEM((members, *part.shape), F32),),
    )
    gathered = cross([total] * groups, "lat")
    passed = [total, *[turn(block) for block in gathered[1:]]]
    pieces_held = pltpu.VMEM((groups, head, chan_cols), F32)
    (assembled,) = call(
        lambda *refs: assemble(piece, *refs),
        [shape(channels, chan_cols)],
        gathered,
        (pieces_held,),
    )
    (weight_grad,) = call(
        lambda *refs: finish(piece, *refs),
        [shape(channels, channels, dtype=F32)],
        (assembled, *passed),
        (pieces_held,),
    )
    return (result[None], weight_grad)


def solution(mesh):
    placed = (
        P(("grp", "ens"), "lat", None, "chan"),
        P(("grp", "ens"), "lat", None, "chan"),
        P(("grp", "ens"), ("lat", "chan"), None, None, None),
        P(("lat", "chan"), None, "ens"),
        P(),
    )
    return jax.shard_map(
        on_device,
        mesh=mesh,
        in_specs=placed,
        out_specs=(P(("grp", "ens"), "lat", None, "chan"), P("grp", None)),
        check_vma=False,
    )
```

```python
import math

import jax
import jax.numpy as jnp
import numpy as np
from jax import lax
from jax.experimental import pallas as pl
from jax.experimental.pallas import tpu as pltpu
from jax.sharding import PartitionSpec as P

VMEM = pl.BlockSpec(memory_space=pltpu.VMEM)
BF16 = jnp.bfloat16
F32 = jnp.float32


def fourier_table(lon_count, mode_count):
    longitude = np.arange(lon_count, dtype=np.int32)[:, None]
    wavenumber = np.arange(mode_count, dtype=np.int32)[None, :]
    product_index = longitude * wavenumber % lon_count
    angles = np.float32(2.0 * math.pi / lon_count) * product_index.astype(np.float32)
    factor = np.float32(math.sqrt(2.0 / lon_count))
    stacked = np.stack([np.cos(angles), -np.sin(angles)], axis=2) * factor
    return stacked.reshape(lon_count, 2 * mode_count).astype(BF16)


def padded(rows, tile):
    return -(-rows // tile) * tile


def analysis_matrix(lat_rows, lon_count, mode_count, groups):
    width = 2 * mode_count // groups
    table = np.asarray(fourier_table(lon_count, mode_count)).astype(np.float32)
    table = table.T.reshape(groups, width, lon_count)
    full = np.zeros((groups, lat_rows, width, lat_rows, lon_count), np.float32)
    for row in range(lat_rows):
        full[:, row, :, row, :] = table
    full = full.reshape(groups, lat_rows * width, lat_rows * lon_count)
    out = np.zeros((groups, padded(lat_rows * width, 8), lat_rows * lon_count), np.float32)
    out[:, : lat_rows * width] = full
    return out.astype(BF16)


def expansion_tables(local_modes, chan_count, degrees, lat_rows, groups, members):
    modes = local_modes * chan_count
    width = 2 * modes
    cols = padded(lat_rows * width, 8)
    lat_count = lat_rows * groups
    row = np.arange(local_modes * degrees * 2)
    pick_rows = row[:, None] // 2 == np.arange(local_modes * degrees)[None, :]
    col = np.arange(groups * cols)
    group, inner = col // cols, col % cols
    valid = inner < lat_rows * width
    lat = group * lat_rows + inner // width
    pick_lat = (np.arange(lat_count)[:, None] == lat[None, :]) & valid[None, :]
    kind_of_row = row // (2 * degrees) * 2 + row % 2
    kind_of_row = kind_of_row[None] + 2 * local_modes * np.arange(chan_count)[:, None]
    kind_of_col = inner % width
    kinds = np.arange(width)
    return (
        pick_rows.astype(BF16),
        pick_lat.reshape(members, lat_count // members, groups * cols).astype(BF16),
        (kind_of_row[:, :, None] == kinds).astype(BF16),
        (kinds[:, None] == kind_of_col[None, :]).astype(BF16),
    )


def partner(me, step, count=0):
    return me ^ (count - step if step > 0 and count > 0 else step)


def dot(left, right, left_dim=1, right_dim=0):
    return lax.dot_general(
        left, right, (((left_dim,), (right_dim,)), ((), ())), preferred_element_type=F32
    )


def fold_rows(rows, cols):
    return padded(rows - rows // 2, 8) if cols % 128 == 64 and rows >= 16 else 0


def fold(x):
    rows, cols = x.shape
    side = fold_rows(rows, cols)
    if side == 0:
        return x
    full = cols - 64
    right = x[side:, full:]
    if rows - side < side:
        right = jnp.concatenate([right, jnp.zeros((2 * side - rows, 64), x.dtype)], axis=0)
    tail = jnp.concatenate([x[:side, full:], right], axis=1)
    if full > 128:
        tail = jnp.concatenate([tail, jnp.zeros((side, full - 128), x.dtype)], axis=1)
    return jnp.concatenate([x[:, :full], tail], axis=0)


def unfold(x, rows, cols):
    side = fold_rows(rows, cols)
    if side == 0:
        return x
    tail = x[rows:]
    last = jnp.concatenate([tail[:, :64], tail[: rows - side, 64:128]], axis=0)
    return jnp.concatenate([x[:rows], last], axis=1)


def folded(rows, cols):
    side = fold_rows(rows, cols)
    return shape(rows + side, cols - 64) if side else shape(rows, cols)


def silu_backward(cotangent, preact):
    values = preact.astype(F32)
    gate = 1.0 / (1.0 + jnp.exp(-values))
    return (cotangent.astype(F32) * gate * (1.0 + values * (1.0 - gate))).astype(BF16)


def analyse(scaled_ref, table_ref, *refs):
    groups = table_ref.shape[0]
    out_refs, held_ref = refs[:groups], refs[groups]
    scaled = scaled_ref[...].reshape(-1, scaled_ref.shape[2])
    table = table_ref[...].reshape(groups * table_ref.shape[1], -1)
    held_ref[...] = dot(table, scaled).reshape(held_ref.shape)
    me = lax.axis_index("lat")
    for step in range(groups):
        out_refs[step][...] = fold(held_ref[partner(me, step, groups)]).astype(BF16)


def prepare(*refs):
    legendre_refs, spread_ref = refs[:-5], refs[-1]
    pick_rows_ref, pick_lat_ref, row_kind_ref, col_kind_ref = refs[-5:-1]
    chan, ens = lax.axis_index("chan"), lax.axis_index("ens")
    for step in range(row_kind_ref.shape[0]):
        core = partner(chan, step)
        blocks = []
        for mode in range(legendre_refs[0].shape[1]):
            total = None
            for place in range(pick_lat_ref.shape[0]):
                pick = pick_lat_ref[partner(ens, place)]
                term = dot(legendre_refs[step][place, mode], pick, 0, 0)
                total = term if total is None else total + term
            blocks.append(total)
        block = jnp.concatenate(blocks, axis=0).astype(BF16)
        keep = dot(row_kind_ref[core], col_kind_ref[...])
        spread_ref[core] = (dot(pick_rows_ref[...], block) * keep).astype(BF16)


def coefficients(groups, chan_count, piece, scale, *refs):
    recv_refs = refs[:groups]
    spread_ref = refs[groups]
    coeffs_refs = refs[groups + 1 : groups + 1 + chan_count]
    send_refs = refs[groups + 1 + chan_count : -3]
    held_ref, coef_ref, term_ref = refs[-3:]
    lat, chan = lax.axis_index("lat"), lax.axis_index("chan")
    _, chunk, cols = held_ref.shape
    for step in range(groups):
        block = unfold(recv_refs[step][...].astype(F32), chunk, cols)
        held_ref[partner(lat, step, groups)] = block
    block = held_ref[...].reshape(-1, cols).astype(BF16)
    spread = spread_ref[...].reshape(-1, spread_ref.shape[2])
    coef = dot(spread, block).astype(BF16)
    coef_ref[...] = coef.reshape(coef_ref.shape)
    held_ref[...] = dot(spread, coef, 0, 0).reshape(held_ref.shape)
    term = None
    for step in range(chan_count):
        part = dot(coeffs_refs[step][...], coef_ref[partner(chan, step)], 0, 0)
        term = part if term is None else term + part
    term = term * scale
    if piece < term_ref.shape[1]:
        term_ref[:, piece:] = jnp.zeros_like(term_ref[:, piece:])
    for group in range(groups):
        term_ref[group, :piece] = term[group * piece : (group + 1) * piece]
    for step in range(groups):
        target = partner(lat, step, groups)
        part = fold(term_ref[target]).astype(BF16)
        send_refs[step - 1][: part.shape[0]] = part
        send_refs[step - 1][part.shape[0] :] = fold(held_ref[target]).astype(BF16)


def add_groups(*refs):
    recv_refs, (piece_out, rows_out, held_ref) = refs[:-3], refs[-3:]
    lat = lax.axis_index("lat")
    groups, chunk, cols = held_ref.shape
    head = piece_out.shape[0]
    total = None
    for place, ref in enumerate(recv_refs):
        step = (place + 1) % groups
        part = ref[:head].astype(F32)
        total = part if total is None else total + part
        block = unfold(ref[head:].astype(F32), chunk, cols)
        held_ref[partner(lat, step, groups)] = block
    piece_out[...] = total.astype(BF16)
    rows_out[...] = held_ref[...].reshape(rows_out.shape).astype(BF16)


def mix(*refs):
    rows_refs, (mixing_ref, out_ref, held_ref) = refs[:-3], refs[-3:]
    chan = lax.axis_index("chan")
    for step, ref in enumerate(rows_refs):
        held_ref[partner(chan, step ^ 1)] = ref[...]
    half = out_ref.shape[1]
    matrix = mixing_ref[pl.ds(pl.multiple_of(chan * half, half), half), :]
    rows = jnp.concatenate([held_ref[core] for core in range(len(rows_refs))], axis=1)
    out_ref[...] = dot(rows, matrix, 1, 1).astype(BF16)


def add_members(mark_ref, *refs):
    del mark_ref
    term_refs, (out_ref, held_ref) = refs[:-2], refs[-2:]
    ens = lax.axis_index("ens")
    for step, ref in enumerate(term_refs):
        held_ref[partner(ens, step)] = ref[...].astype(F32)
    total = held_ref[0]
    for member in range(1, len(term_refs)):
        total = total + held_ref[member]
    out_ref[...] = total.astype(BF16)


def synthesise(rows_ref, table_ref, grad_ref, out_ref, mark_ref):
    received = rows_ref[...]
    if len(table_ref.shape) == 3:
        spatial = dot(table_ref[...].reshape(received.shape[0], -1), received, 0)
    else:
        spatial = dot(table_ref[...], received)
    result = grad_ref[...].astype(F32) + spatial.reshape(grad_ref.shape)
    out_ref[...] = result.astype(BF16)
    mark_ref[...] = jnp.zeros_like(mark_ref)


def assemble(piece, *refs):
    block_refs, (out_ref, held_ref) = refs[:-2], refs[-2:]
    lat = lax.axis_index("lat")
    _, head, cols = held_ref.shape
    for step, ref in enumerate(block_refs):
        held_ref[partner(lat, step)] = unfold(ref[...].astype(F32), head, cols)
    for group in range(len(block_refs)):
        out_ref[group * piece : (group + 1) * piece] = held_ref[group, :piece].astype(BF16)


def finish(piece, own_ref, *refs):
    piece_refs, (out_ref, held_ref) = refs[:-2], refs[-2:]
    lat, chan = lax.axis_index("lat"), lax.axis_index("chan")
    half, head = own_ref.shape[1], held_ref.shape[1]
    for step, ref in enumerate(piece_refs):
        held_ref[partner(lat, step)] = unfold(ref[...].astype(F32), head, half)

    @pl.when(chan != 0)
    def _():
        out_ref[:, :half] = own_ref[...].astype(F32)
        for group in range(len(piece_refs)):
            out_ref[group * piece : (group + 1) * piece, half:] = held_ref[group, :piece]

    @pl.when(chan == 0)
    def _():
        for group in range(len(piece_refs)):
            out_ref[group * piece : (group + 1) * piece, :half] = held_ref[group, :piece]
        out_ref[:, half:] = own_ref[...].astype(F32)


def call(kernel, outs, operands, scratch=(), limit=None):
    sizes = [math.prod(x.shape) * x.dtype.itemsize for x in (*operands, *outs)]
    sizes += [math.prod(x.shape) * 4 for x in scratch]
    return pl.pallas_call(
        lambda *refs: kernel(*refs),
        out_shape=tuple(outs),
        in_specs=[VMEM] * len(operands),
        out_specs=(VMEM,) * len(outs),
        scratch_shapes=scratch,
        compiler_params=pltpu.CompilerParams(
            vmem_limit_bytes=limit or min(56 << 20, (6 << 20) + 4 * sum(sizes))
        ),
        cost_estimate=pl.CostEstimate(
            flops=1000000, bytes_accessed=2 * sum(sizes), transcendentals=0
        ),
    )(*operands)


def swap(blocks, axis, far=False):
    count = len(blocks)
    received = [blocks[0]]
    for step in range(1, count):
        pairs = [
            (device, partner(device, step, count if far else 0)) for device in range(count)
        ]
        received.append(lax.ppermute(blocks[step], axis, pairs))
    return received


def share(block, axis):
    return swap([block] * lax.axis_size(axis), axis)


def cross(blocks, axis, far=False):
    count, cores = len(blocks), lax.axis_size("chan")
    received = []
    for step in range(1, count):
        pairs = []
        for device in range(count):
            other = partner(device, step, count if far else 0)
            for core in range(cores):
                if axis == "lat":
                    pairs.append((device * cores + core, other * cores + (core ^ 1)))
                else:
                    pairs.append((core * count + device, (core ^ 1) * count + other))
        axes = ("lat", "chan") if axis == "lat" else ("chan", axis)
        received.append(lax.ppermute(blocks[step], axes, pairs))
    return [turn(blocks[0]), *received]


def turn(block):
    cores = lax.axis_size("chan")
    return lax.ppermute(block, "chan", [(core, core ^ 1) for core in range(cores)])


def shape(*dims, dtype=BF16):
    return jax.ShapeDtypeStruct(dims, dtype)


def on_device(grad_out, pre_act, coeffs, legendre, mixing):
    lat_rows, lon_count, chan_cols = grad_out.shape[1:]
    mode_count = lon_count // 2
    groups = lax.axis_size("lat")
    chan_count = lax.axis_size("chan")
    members = lax.axis_size("ens")
    channels = chan_cols * chan_count
    local_modes, degrees, _ = legendre.shape
    table = analysis_matrix(lat_rows, lon_count, mode_count, groups)
    selections = expansion_tables(
        local_modes, chan_count, degrees, lat_rows, groups, members
    )
    chunk = table.shape[1]
    rows = local_modes * degrees * 2
    piece = channels // groups
    head = padded(piece, 32)
    held = pltpu.VMEM((groups, chunk, chan_cols), F32)
    part = folded(head, chan_cols)
    side = folded(chunk, chan_cols)
    both = shape(part.shape[0] + side.shape[0], side.shape[1])

    legendre_parts = share(jnp.stack(share(legendre.transpose(0, 2, 1), "ens")), "chan")
    spectral = call(
        analyse,
        [side] * groups,
        (silu_backward(grad_out[0], pre_act[0]), jnp.asarray(table)),
        (held,),
    )
    spectral = swap(spectral, "lat", far=True)
    coeffs_parts = [x.reshape(rows, channels) for x in share(coeffs[0], "chan")]
    (spread,) = call(
        prepare,
        [shape(chan_count, rows, groups * chunk)],
        (*legendre_parts, *(jnp.asarray(x) for x in selections)),
    )

    blocks = call(
        lambda *refs: coefficients(
            groups, chan_count, piece, 1.0 / (members * mode_count), *refs
        ),
        [both] * groups,
        (*spectral, spread, *coeffs_parts),
        (
            held,
            pltpu.VMEM((chan_count, rows, chan_cols), BF16),
            pltpu.VMEM((groups, head, chan_cols), F32),
        ),
    )
    blocks = cross([blocks[-1], *blocks[:-1]], "lat", far=True)
    blocks = [*blocks[1:], blocks[0]]
    returned = shape(groups * chunk, chan_cols)
    total, received = call(
        add_groups, [part, returned], blocks, (held,)
    )
    (mixed,) = call(
        mix,
        [returned],
        (*share(received, "chan"), mixing),
        (pltpu.VMEM((chan_count, *returned.shape), BF16),),
    )
    if table.size < 1 << 20:
        back = jnp.asarray(np.ascontiguousarray(table.reshape(-1, lat_rows * lon_count).T))
    else:
        back = jnp.asarray(table)
    result, mark = call(
        synthesise,
        [shape(*grad_out.shape[1:]), shape(8, 128, dtype=F32)],
        (mixed, back, grad_out[0]),
    )
    (total,) = call(
        add_members,
        [part],
        (mark, *cross([total] * members, "ens")),
        (pltpu.VMEM((members, *part.shape), F32),),
    )
    gathered = cross([total] * groups, "lat")
    passed = [total, *[turn(block) for block in gathered[1:]]]
    pieces_held = pltpu.VMEM((groups, head, chan_cols), F32)
    (assembled,) = call(
        lambda *refs: assemble(piece, *refs),
        [shape(channels, chan_cols)],
        gathered,
        (pieces_held,),
    )
    (weight_grad,) = call(
        lambda *refs: finish(piece, *refs),
        [shape(channels, channels, dtype=F32)],
        (assembled, *passed),
        (pieces_held,),
    )
    return (result[None], weight_grad)


def solution(mesh):
    placed = (
        P(("grp", "ens"), "lat", None, "chan"),
        P(("grp", "ens"), "lat", None, "chan"),
        P(("grp", "ens"), ("lat", "chan"), None, None, None),
        P(("lat", "chan"), None, "ens"),
        P(),
    )
    return jax.shard_map(
        on_device,
        mesh=mesh,
        in_specs=placed,
        out_specs=(P(("grp", "ens"), "lat", None, "chan"), P("grp", None)),
        check_vma=False,
    )
```

```python
import math

import jax
import jax.numpy as jnp
import numpy as np
from jax import lax
from jax.experimental import pallas as pl
from jax.experimental.pallas import tpu as pltpu
from jax.sharding import PartitionSpec as P

VMEM = pl.BlockSpec(memory_space=pltpu.VMEM)
BF16 = jnp.bfloat16
F32 = jnp.float32


def fourier_table(lon_count, mode_count):
    longitude = np.arange(lon_count, dtype=np.int32)[:, None]
    wavenumber = np.arange(mode_count, dtype=np.int32)[None, :]
    product_index = longitude * wavenumber % lon_count
    angles = np.float32(2.0 * math.pi / lon_count) * product_index.astype(np.float32)
    factor = np.float32(math.sqrt(2.0 / lon_count))
    stacked = np.stack([np.cos(angles), -np.sin(angles)], axis=2) * factor
    return stacked.reshape(lon_count, 2 * mode_count).astype(BF16)


def padded(rows, tile):
    return -(-rows // tile) * tile


def analysis_matrix(lat_rows, lon_count, mode_count, groups):
    width = 2 * mode_count // groups
    table = np.asarray(fourier_table(lon_count, mode_count)).astype(np.float32)
    table = table.T.reshape(groups, width, lon_count)
    full = np.zeros((groups, lat_rows, width, lat_rows, lon_count), np.float32)
    for row in range(lat_rows):
        full[:, row, :, row, :] = table
    full = full.reshape(groups, lat_rows * width, lat_rows * lon_count)
    out = np.zeros((groups, padded(lat_rows * width, 8), lat_rows * lon_count), np.float32)
    out[:, : lat_rows * width] = full
    return out.astype(BF16)


def expansion_tables(local_modes, chan_count, degrees, lat_rows, groups, members):
    modes = local_modes * chan_count
    width = 2 * modes
    cols = padded(lat_rows * width, 8)
    lat_count = lat_rows * groups
    row = np.arange(local_modes * degrees * 2)
    pick_rows = row[:, None] // 2 == np.arange(local_modes * degrees)[None, :]
    col = np.arange(groups * cols)
    group, inner = col // cols, col % cols
    valid = inner < lat_rows * width
    lat = group * lat_rows + inner // width
    pick_lat = (np.arange(lat_count)[:, None] == lat[None, :]) & valid[None, :]
    kind_of_row = row // (2 * degrees) * 2 + row % 2
    kind_of_row = kind_of_row[None] + 2 * local_modes * np.arange(chan_count)[:, None]
    kind_of_col = inner % width
    kinds = np.arange(width)
    keep = kind_of_row[:, :, None] == kind_of_col[None, None, :]
    if keep.size < 1 << 20:
        kept = (keep.astype(BF16),)
    else:
        kept = (
            (kind_of_row[:, :, None] == kinds).astype(BF16),
            (kinds[:, None] == kind_of_col[None, :]).astype(BF16),
        )
    return (
        pick_rows.astype(BF16),
        pick_lat.reshape(members, lat_count // members, groups * cols).astype(BF16),
        *kept,
    )


def partner(me, step, count=0):
    return me ^ (count - step if step > 0 and count > 0 else step)


def dot(left, right, left_dim=1, right_dim=0):
    return lax.dot_general(
        left, right, (((left_dim,), (right_dim,)), ((), ())), preferred_element_type=F32
    )


def fold_rows(rows, cols):
    return padded(rows - rows // 2, 8) if cols % 128 == 64 and rows >= 16 else 0


def fold(x):
    rows, cols = x.shape
    side = fold_rows(rows, cols)
    if side == 0:
        return x
    full = cols - 64
    right = x[side:, full:]
    if rows - side < side:
        right = jnp.concatenate([right, jnp.zeros((2 * side - rows, 64), x.dtype)], axis=0)
    tail = jnp.concatenate([x[:side, full:], right], axis=1)
    if full > 128:
        tail = jnp.concatenate([tail, jnp.zeros((side, full - 128), x.dtype)], axis=1)
    return jnp.concatenate([x[:, :full], tail], axis=0)


def unfold(x, rows, cols):
    side = fold_rows(rows, cols)
    if side == 0:
        return x
    tail = x[rows:]
    last = jnp.concatenate([tail[:, :64], tail[: rows - side, 64:128]], axis=0)
    return jnp.concatenate([x[:rows], last], axis=1)


def folded(rows, cols):
    side = fold_rows(rows, cols)
    return shape(rows + side, cols - 64) if side else shape(rows, cols)


def silu_backward(cotangent, preact):
    values = preact.astype(F32)
    gate = 1.0 / (1.0 + jnp.exp(-values))
    return (cotangent.astype(F32) * gate * (1.0 + values * (1.0 - gate))).astype(BF16)


def analyse(scaled_ref, table_ref, *refs):
    groups = table_ref.shape[0]
    out_refs, held_ref = refs[:groups], refs[groups]
    scaled = scaled_ref[...].reshape(-1, scaled_ref.shape[2])
    table = table_ref[...].reshape(groups * table_ref.shape[1], -1)
    held_ref[...] = dot(table, scaled).reshape(held_ref.shape)
    me = lax.axis_index("lat")
    for step in range(groups):
        out_refs[step][...] = fold(held_ref[partner(me, step, groups)]).astype(BF16)


def prepare(*refs):
    cores, spread_ref = lax.axis_size("chan"), refs[-1]
    legendre_refs = refs[:cores]
    pick_rows_ref, pick_lat_ref, *keep_refs = refs[cores:-1]
    chan, ens = lax.axis_index("chan"), lax.axis_index("ens")
    for step in range(cores):
        core = partner(chan, step)
        blocks = []
        for mode in range(legendre_refs[0].shape[1]):
            total = None
            for place in range(pick_lat_ref.shape[0]):
                pick = pick_lat_ref[partner(ens, place)]
                term = dot(legendre_refs[step][place, mode], pick, 0, 0)
                total = term if total is None else total + term
            blocks.append(total)
        block = jnp.concatenate(blocks, axis=0).astype(BF16)
        if len(keep_refs) == 2:
            keep = dot(keep_refs[0][core], keep_refs[1][...])
        else:
            keep = keep_refs[0][core].astype(F32)
        spread_ref[core] = (dot(pick_rows_ref[...], block) * keep).astype(BF16)


def coefficients(groups, chan_count, piece, scale, *refs):
    recv_refs = refs[:groups]
    spread_ref = refs[groups]
    coeffs_refs = refs[groups + 1 : groups + 1 + chan_count]
    send_refs = refs[groups + 1 + chan_count : -3]
    held_ref, coef_ref, term_ref = refs[-3:]
    lat, chan = lax.axis_index("lat"), lax.axis_index("chan")
    _, chunk, cols = held_ref.shape
    for step in range(groups):
        block = unfold(recv_refs[step][...].astype(F32), chunk, cols)
        held_ref[partner(lat, step, groups)] = block
    block = held_ref[...].reshape(-1, cols).astype(BF16)
    spread = spread_ref[...].reshape(-1, spread_ref.shape[2])
    coef = dot(spread, block).astype(BF16)
    coef_ref[...] = coef.reshape(coef_ref.shape)
    held_ref[...] = dot(spread, coef, 0, 0).reshape(held_ref.shape)
    term = None
    for step in range(chan_count):
        part = dot(coeffs_refs[step][...], coef_ref[partner(chan, step)], 0, 0)
        term = part if term is None else term + part
    term = term * scale
    if piece < term_ref.shape[1]:
        term_ref[:, piece:] = jnp.zeros_like(term_ref[:, piece:])
    for group in range(groups):
        term_ref[group, :piece] = term[group * piece : (group + 1) * piece]
    for step in range(groups):
        target = partner(lat, step, groups)
        part = fold(term_ref[target]).astype(BF16)
        send_refs[step - 1][: part.shape[0]] = part
        send_refs[step - 1][part.shape[0] :] = fold(held_ref[target]).astype(BF16)


def add_groups(*refs):
    recv_refs, (piece_out, rows_out, held_ref) = refs[:-3], refs[-3:]
    lat = lax.axis_index("lat")
    groups, chunk, cols = held_ref.shape
    head = piece_out.shape[0]
    total = None
    for place, ref in enumerate(recv_refs):
        step = (place + 1) % groups
        part = ref[:head].astype(F32)
        total = part if total is None else total + part
        block = unfold(ref[head:].astype(F32), chunk, cols)
        held_ref[partner(lat, step, groups)] = block
    piece_out[...] = total.astype(BF16)
    rows_out[...] = held_ref[...].reshape(rows_out.shape).astype(BF16)


def mix(*refs):
    rows_refs, (mixing_ref, out_ref, held_ref) = refs[:-3], refs[-3:]
    chan = lax.axis_index("chan")
    for step, ref in enumerate(rows_refs):
        held_ref[partner(chan, step ^ 1)] = ref[...]
    half = out_ref.shape[1]
    matrix = mixing_ref[pl.ds(pl.multiple_of(chan * half, half), half), :]
    rows = jnp.concatenate([held_ref[core] for core in range(len(rows_refs))], axis=1)
    out_ref[...] = dot(rows, matrix, 1, 1).astype(BF16)


def add_members(mark_ref, *refs):
    del mark_ref
    term_refs, (out_ref, held_ref) = refs[:-2], refs[-2:]
    ens = lax.axis_index("ens")
    for step, ref in enumerate(term_refs):
        held_ref[partner(ens, step)] = ref[...].astype(F32)
    total = held_ref[0]
    for member in range(1, len(term_refs)):
        total = total + held_ref[member]
    out_ref[...] = total.astype(BF16)


def synthesise(rows_ref, table_ref, grad_ref, out_ref, mark_ref):
    received = rows_ref[...]
    if len(table_ref.shape) == 3:
        spatial = dot(table_ref[...].reshape(received.shape[0], -1), received, 0)
    else:
        spatial = dot(table_ref[...], received)
    result = grad_ref[...].astype(F32) + spatial.reshape(grad_ref.shape)
    out_ref[...] = result.astype(BF16)
    mark_ref[...] = jnp.zeros_like(mark_ref)


def assemble(piece, *refs):
    block_refs, (out_ref, held_ref) = refs[:-2], refs[-2:]
    lat = lax.axis_index("lat")
    _, head, cols = held_ref.shape
    for step, ref in enumerate(block_refs):
        held_ref[partner(lat, step)] = unfold(ref[...].astype(F32), head, cols)
    for group in range(len(block_refs)):
        out_ref[group * piece : (group + 1) * piece] = held_ref[group, :piece].astype(BF16)


def finish(piece, own_ref, *refs):
    piece_refs, (out_ref, held_ref) = refs[:-2], refs[-2:]
    lat, chan = lax.axis_index("lat"), lax.axis_index("chan")
    half, head = own_ref.shape[1], held_ref.shape[1]
    for step, ref in enumerate(piece_refs):
        held_ref[partner(lat, step)] = unfold(ref[...].astype(F32), head, half)

    @pl.when(chan != 0)
    def _():
        out_ref[:, :half] = own_ref[...].astype(F32)
        for group in range(len(piece_refs)):
            out_ref[group * piece : (group + 1) * piece, half:] = held_ref[group, :piece]

    @pl.when(chan == 0)
    def _():
        for group in range(len(piece_refs)):
            out_ref[group * piece : (group + 1) * piece, :half] = held_ref[group, :piece]
        out_ref[:, half:] = own_ref[...].astype(F32)


def call(kernel, outs, operands, scratch=(), limit=None):
    sizes = [math.prod(x.shape) * x.dtype.itemsize for x in (*operands, *outs)]
    sizes += [math.prod(x.shape) * 4 for x in scratch]
    return pl.pallas_call(
        lambda *refs: kernel(*refs),
        out_shape=tuple(outs),
        in_specs=[VMEM] * len(operands),
        out_specs=(VMEM,) * len(outs),
        scratch_shapes=scratch,
        compiler_params=pltpu.CompilerParams(
            vmem_limit_bytes=limit or min(56 << 20, (6 << 20) + 4 * sum(sizes))
        ),
        cost_estimate=pl.CostEstimate(
            flops=1000000, bytes_accessed=2 * sum(sizes), transcendentals=0
        ),
    )(*operands)


def swap(blocks, axis, far=False):
    count = len(blocks)
    received = [blocks[0]]
    for step in range(1, count):
        pairs = [
            (device, partner(device, step, count if far else 0)) for device in range(count)
        ]
        received.append(lax.ppermute(blocks[step], axis, pairs))
    return received


def share(block, axis):
    return swap([block] * lax.axis_size(axis), axis)


def cross(blocks, axis, far=False):
    count, cores = len(blocks), lax.axis_size("chan")
    received = []
    for step in range(1, count):
        pairs = []
        for device in range(count):
            other = partner(device, step, count if far else 0)
            for core in range(cores):
                if axis == "lat":
                    pairs.append((device * cores + core, other * cores + (core ^ 1)))
                else:
                    pairs.append((core * count + device, (core ^ 1) * count + other))
        axes = ("lat", "chan") if axis == "lat" else ("chan", axis)
        received.append(lax.ppermute(blocks[step], axes, pairs))
    return [turn(blocks[0]), *received]


def turn(block):
    cores = lax.axis_size("chan")
    return lax.ppermute(block, "chan", [(core, core ^ 1) for core in range(cores)])


def shape(*dims, dtype=BF16):
    return jax.ShapeDtypeStruct(dims, dtype)


def on_device(grad_out, pre_act, coeffs, legendre, mixing):
    lat_rows, lon_count, chan_cols = grad_out.shape[1:]
    mode_count = lon_count // 2
    groups = lax.axis_size("lat")
    chan_count = lax.axis_size("chan")
    members = lax.axis_size("ens")
    channels = chan_cols * chan_count
    local_modes, degrees, _ = legendre.shape
    table = analysis_matrix(lat_rows, lon_count, mode_count, groups)
    selections = expansion_tables(
        local_modes, chan_count, degrees, lat_rows, groups, members
    )
    chunk = table.shape[1]
    rows = local_modes * degrees * 2
    piece = channels // groups
    head = padded(piece, 32)
    held = pltpu.VMEM((groups, chunk, chan_cols), F32)
    part = folded(head, chan_cols)
    side = folded(chunk, chan_cols)
    both = shape(part.shape[0] + side.shape[0], side.shape[1])

    legendre_parts = share(jnp.stack(share(legendre.transpose(0, 2, 1), "ens")), "chan")
    spectral = call(
        analyse,
        [side] * groups,
        (silu_backward(grad_out[0], pre_act[0]), jnp.asarray(table)),
        (held,),
    )
    spectral = swap(spectral, "lat", far=True)
    coeffs_parts = [x.reshape(rows, channels) for x in share(coeffs[0], "chan")]
    (spread,) = call(
        prepare,
        [shape(chan_count, rows, groups * chunk)],
        (*legendre_parts, *(jnp.asarray(x) for x in selections)),
    )

    blocks = call(
        lambda *refs: coefficients(
            groups, chan_count, piece, 1.0 / (members * mode_count), *refs
        ),
        [both] * groups,
        (*spectral, spread, *coeffs_parts),
        (
            held,
            pltpu.VMEM((chan_count, rows, chan_cols), BF16),
            pltpu.VMEM((groups, head, chan_cols), F32),
        ),
    )
    blocks = cross([blocks[-1], *blocks[:-1]], "lat", far=True)
    blocks = [*blocks[1:], blocks[0]]
    returned = shape(groups * chunk, chan_cols)
    total, received = call(
        add_groups, [part, returned], blocks, (held,)
    )
    (mixed,) = call(
        mix,
        [returned],
        (*share(received, "chan"), mixing),
        (pltpu.VMEM((chan_count, *returned.shape), BF16),),
    )
    if table.size < 1 << 20:
        back = jnp.asarray(np.ascontiguousarray(table.reshape(-1, lat_rows * lon_count).T))
    else:
        back = jnp.asarray(table)
    result, mark = call(
        synthesise,
        [shape(*grad_out.shape[1:]), shape(8, 128, dtype=F32)],
        (mixed, back, grad_out[0]),
    )
    (total,) = call(
        add_members,
        [part],
        (mark, *cross([total] * members, "ens")),
        (pltpu.VMEM((members, *part.shape), F32),),
    )
    gathered = cross([total] * groups, "lat")
    passed = [total, *[turn(block) for block in gathered[1:]]]
    pieces_held = pltpu.VMEM((groups, head, chan_cols), F32)
    (assembled,) = call(
        lambda *refs: assemble(piece, *refs),
        [shape(channels, chan_cols)],
        gathered,
        (pieces_held,),
    )
    (weight_grad,) = call(
        lambda *refs: finish(piece, *refs),
        [shape(channels, channels, dtype=F32)],
        (assembled, *passed),
        (pieces_held,),
    )
    return (result[None], weight_grad)


def solution(mesh):
    placed = (
        P(("grp", "ens"), "lat", None, "chan"),
        P(("grp", "ens"), "lat", None, "chan"),
        P(("grp", "ens"), ("lat", "chan"), None, None, None),
        P(("lat", "chan"), None, "ens"),
        P(),
    )
    return jax.shard_map(
        on_device,
        mesh=mesh,
        in_specs=placed,
        out_specs=(P(("grp", "ens"), "lat", None, "chan"), P("grp", None)),
        check_vma=False,
    )
```

```python
import math

import jax
import jax.numpy as jnp
import numpy as np
from jax import lax
from jax.experimental import pallas as pl
from jax.experimental.pallas import tpu as pltpu
from jax.sharding import PartitionSpec as P

VMEM = pl.BlockSpec(memory_space=pltpu.VMEM)
BF16 = jnp.bfloat16
F32 = jnp.float32


def fourier_table(lon_count, mode_count):
    longitude = np.arange(lon_count, dtype=np.int32)[:, None]
    wavenumber = np.arange(mode_count, dtype=np.int32)[None, :]
    product_index = longitude * wavenumber % lon_count
    angles = np.float32(2.0 * math.pi / lon_count) * product_index.astype(np.float32)
    factor = np.float32(math.sqrt(2.0 / lon_count))
    stacked = np.stack([np.cos(angles), -np.sin(angles)], axis=2) * factor
    return stacked.reshape(lon_count, 2 * mode_count).astype(BF16)


def padded(rows, tile):
    return -(-rows // tile) * tile


def analysis_matrix(lat_rows, lon_count, mode_count, groups):
    width = 2 * mode_count // groups
    table = np.asarray(fourier_table(lon_count, mode_count)).astype(np.float32)
    table = table.T.reshape(groups, width, lon_count)
    full = np.zeros((groups, lat_rows, width, lat_rows, lon_count), np.float32)
    for row in range(lat_rows):
        full[:, row, :, row, :] = table
    full = full.reshape(groups, lat_rows * width, lat_rows * lon_count)
    out = np.zeros((groups, padded(lat_rows * width, 8), lat_rows * lon_count), np.float32)
    out[:, : lat_rows * width] = full
    return out.astype(BF16)


def expansion_tables(local_modes, chan_count, degrees, lat_rows, groups, members):
    modes = local_modes * chan_count
    width = 2 * modes
    cols = padded(lat_rows * width, 8)
    lat_count = lat_rows * groups
    row = np.arange(local_modes * degrees * 2)
    pick_rows = row[:, None] // 2 == np.arange(local_modes * degrees)[None, :]
    col = np.arange(groups * cols)
    group, inner = col // cols, col % cols
    valid = inner < lat_rows * width
    lat = group * lat_rows + inner // width
    pick_lat = (np.arange(lat_count)[:, None] == lat[None, :]) & valid[None, :]
    kind_of_row = row // (2 * degrees) * 2 + row % 2
    kind_of_row = kind_of_row[None] + 2 * local_modes * np.arange(chan_count)[:, None]
    kind_of_col = inner % width
    kinds = np.arange(width)
    return (
        pick_rows.astype(BF16),
        pick_lat.reshape(members, lat_count // members, groups * cols).astype(BF16),
        (kind_of_row[:, :, None] == kinds).astype(BF16),
        (kinds[:, None] == kind_of_col[None, :]).astype(BF16),
    )


def partner(me, step, count=0):
    return me ^ (count - step if step > 0 and count > 0 else step)


def dot(left, right, left_dim=1, right_dim=0):
    return lax.dot_general(
        left, right, (((left_dim,), (right_dim,)), ((), ())), preferred_element_type=F32
    )


def fold_rows(rows, cols):
    return padded(rows - rows // 2, 8) if cols % 128 == 64 and rows >= 16 else 0


def fold(x):
    rows, cols = x.shape
    side = fold_rows(rows, cols)
    if side == 0:
        return x
    full = cols - 64
    right = x[side:, full:]
    if rows - side < side:
        right = jnp.concatenate([right, jnp.zeros((2 * side - rows, 64), x.dtype)], axis=0)
    tail = jnp.concatenate([x[:side, full:], right], axis=1)
    if full > 128:
        tail = jnp.concatenate([tail, jnp.zeros((side, full - 128), x.dtype)], axis=1)
    return jnp.concatenate([x[:, :full], tail], axis=0)


def unfold(x, rows, cols):
    side = fold_rows(rows, cols)
    if side == 0:
        return x
    tail = x[rows:]
    last = jnp.concatenate([tail[:, :64], tail[: rows - side, 64:128]], axis=0)
    return jnp.concatenate([x[:rows], last], axis=1)


def folded(rows, cols):
    side = fold_rows(rows, cols)
    return shape(rows + side, cols - 64) if side else shape(rows, cols)


def silu_backward(cotangent, preact):
    values = preact.astype(F32)
    gate = 1.0 / (1.0 + jnp.exp(-values))
    return (cotangent.astype(F32) * gate * (1.0 + values * (1.0 - gate))).astype(BF16)


def analyse(scaled_ref, table_ref, *refs):
    groups = table_ref.shape[0]
    out_refs, held_ref = refs[:groups], refs[groups]
    scaled = scaled_ref[...].reshape(-1, scaled_ref.shape[2])
    table = table_ref[...].reshape(groups * table_ref.shape[1], -1)
    held_ref[...] = dot(table, scaled).reshape(held_ref.shape)
    me = lax.axis_index("lat")
    for step in range(groups):
        out_refs[step][...] = fold(held_ref[partner(me, step, groups)]).astype(BF16)


def prepare(*refs):
    legendre_refs, spread_ref = refs[:-5], refs[-1]
    pick_rows_ref, pick_lat_ref, row_kind_ref, col_kind_ref = refs[-5:-1]
    chan, ens = lax.axis_index("chan"), lax.axis_index("ens")
    for step in range(row_kind_ref.shape[0]):
        core = partner(chan, step)
        blocks = []
        for mode in range(legendre_refs[0].shape[1]):
            total = None
            for place in range(pick_lat_ref.shape[0]):
                pick = pick_lat_ref[partner(ens, place)]
                term = dot(legendre_refs[step][place, mode], pick, 0, 0)
                total = term if total is None else total + term
            blocks.append(total)
        block = jnp.concatenate(blocks, axis=0).astype(BF16)
        keep = dot(row_kind_ref[core], col_kind_ref[...])
        spread_ref[core] = (dot(pick_rows_ref[...], block) * keep).astype(BF16)


def coefficients(groups, chan_count, piece, *refs):
    recv_refs = refs[:groups]
    spread_ref = refs[groups]
    coeffs_refs = refs[groups + 1 : groups + 1 + chan_count]
    send_refs = refs[groups + 1 + chan_count : -3]
    held_ref, coef_ref, term_ref = refs[-3:]
    lat, chan = lax.axis_index("lat"), lax.axis_index("chan")
    _, chunk, cols = held_ref.shape
    for step in range(groups):
        block = unfold(recv_refs[step][...].astype(F32), chunk, cols)
        held_ref[partner(lat, step, groups)] = block
    block = held_ref[...].reshape(-1, cols).astype(BF16)
    spread = spread_ref[...].reshape(-1, spread_ref.shape[2])
    coef = dot(spread, block).astype(BF16)
    coef_ref[...] = coef.reshape(coef_ref.shape)
    held_ref[...] = dot(spread, coef, 0, 0).reshape(held_ref.shape)
    term = None
    for step in range(chan_count):
        part = dot(coeffs_refs[step][...], coef_ref[partner(chan, step)], 0, 0)
        term = part if term is None else term + part
    if piece < term_ref.shape[1]:
        term_ref[:, piece:] = jnp.zeros_like(term_ref[:, piece:])
    for group in range(groups):
        term_ref[group, :piece] = term[group * piece : (group + 1) * piece]
    for step in range(groups):
        target = partner(lat, step, groups)
        part = fold(term_ref[target]).astype(BF16)
        send_refs[step - 1][: part.shape[0]] = part
        send_refs[step - 1][part.shape[0] :] = fold(held_ref[target]).astype(BF16)


def add_groups(scale, *refs):
    recv_refs, (piece_out, rows_out, held_ref) = refs[:-3], refs[-3:]
    lat = lax.axis_index("lat")
    groups, chunk, cols = held_ref.shape
    head = piece_out.shape[0]
    total = None
    for place, ref in enumerate(recv_refs):
        step = (place + 1) % groups
        part = ref[:head].astype(F32)
        total = part if total is None else total + part
        block = unfold(ref[head:].astype(F32), chunk, cols)
        held_ref[partner(lat, step, groups)] = block
    piece_out[...] = (total * scale).astype(BF16)
    rows_out[...] = held_ref[...].reshape(rows_out.shape).astype(BF16)


def mix(*refs):
    rows_refs, (mixing_ref, out_ref, held_ref) = refs[:-3], refs[-3:]
    chan = lax.axis_index("chan")
    for step, ref in enumerate(rows_refs):
        held_ref[partner(chan, step ^ 1)] = ref[...]
    half = out_ref.shape[1]
    matrix = mixing_ref[pl.ds(pl.multiple_of(chan * half, half), half), :]
    rows = jnp.concatenate([held_ref[core] for core in range(len(rows_refs))], axis=1)
    out_ref[...] = dot(rows, matrix, 1, 1).astype(BF16)


def add_members(mark_ref, *refs):
    del mark_ref
    term_refs, (out_ref, held_ref) = refs[:-2], refs[-2:]
    ens = lax.axis_index("ens")
    for step, ref in enumerate(term_refs):
        held_ref[partner(ens, step)] = ref[...].astype(F32)
    total = held_ref[0]
    for member in range(1, len(term_refs)):
        total = total + held_ref[member]
    out_ref[...] = total.astype(BF16)


def synthesise(rows_ref, table_ref, grad_ref, out_ref, mark_ref):
    received = rows_ref[...]
    if len(table_ref.shape) == 3:
        spatial = dot(table_ref[...].reshape(received.shape[0], -1), received, 0)
    else:
        spatial = dot(table_ref[...], received)
    result = grad_ref[...].astype(F32) + spatial.reshape(grad_ref.shape)
    out_ref[...] = result.astype(BF16)
    mark_ref[...] = jnp.zeros_like(mark_ref)


def assemble(piece, *refs):
    block_refs, (out_ref, held_ref) = refs[:-2], refs[-2:]
    lat = lax.axis_index("lat")
    _, head, cols = held_ref.shape
    for step, ref in enumerate(block_refs):
        held_ref[partner(lat, step)] = unfold(ref[...].astype(F32), head, cols)
    for group in range(len(block_refs)):
        out_ref[group * piece : (group + 1) * piece] = held_ref[group, :piece].astype(BF16)


def finish(piece, own_ref, *refs):
    piece_refs, (out_ref, held_ref) = refs[:-2], refs[-2:]
    lat, chan = lax.axis_index("lat"), lax.axis_index("chan")
    half, head = own_ref.shape[1], held_ref.shape[1]
    for step, ref in enumerate(piece_refs):
        held_ref[partner(lat, step)] = unfold(ref[...].astype(F32), head, half)

    @pl.when(chan != 0)
    def _():
        out_ref[:, :half] = own_ref[...].astype(F32)
        for group in range(len(piece_refs)):
            out_ref[group * piece : (group + 1) * piece, half:] = held_ref[group, :piece]

    @pl.when(chan == 0)
    def _():
        for group in range(len(piece_refs)):
            out_ref[group * piece : (group + 1) * piece, :half] = held_ref[group, :piece]
        out_ref[:, half:] = own_ref[...].astype(F32)


def call(kernel, outs, operands, scratch=(), limit=None):
    sizes = [math.prod(x.shape) * x.dtype.itemsize for x in (*operands, *outs)]
    sizes += [math.prod(x.shape) * 4 for x in scratch]
    return pl.pallas_call(
        lambda *refs: kernel(*refs),
        out_shape=tuple(outs),
        in_specs=[VMEM] * len(operands),
        out_specs=(VMEM,) * len(outs),
        scratch_shapes=scratch,
        compiler_params=pltpu.CompilerParams(
            vmem_limit_bytes=limit or min(56 << 20, (6 << 20) + 4 * sum(sizes))
        ),
        cost_estimate=pl.CostEstimate(
            flops=1000000, bytes_accessed=2 * sum(sizes), transcendentals=0
        ),
    )(*operands)


def swap(blocks, axis, far=False):
    count = len(blocks)
    received = [blocks[0]]
    for step in range(1, count):
        pairs = [
            (device, partner(device, step, count if far else 0)) for device in range(count)
        ]
        received.append(lax.ppermute(blocks[step], axis, pairs))
    return received


def share(block, axis):
    return swap([block] * lax.axis_size(axis), axis)


def cross(blocks, axis, far=False):
    count, cores = len(blocks), lax.axis_size("chan")
    received = []
    for step in range(1, count):
        pairs = []
        for device in range(count):
            other = partner(device, step, count if far else 0)
            for core in range(cores):
                if axis == "lat":
                    pairs.append((device * cores + core, other * cores + (core ^ 1)))
                else:
                    pairs.append((core * count + device, (core ^ 1) * count + other))
        axes = ("lat", "chan") if axis == "lat" else ("chan", axis)
        received.append(lax.ppermute(blocks[step], axes, pairs))
    return [turn(blocks[0]), *received]


def turn(block):
    cores = lax.axis_size("chan")
    return lax.ppermute(block, "chan", [(core, core ^ 1) for core in range(cores)])


def shape(*dims, dtype=BF16):
    return jax.ShapeDtypeStruct(dims, dtype)


def on_device(grad_out, pre_act, coeffs, legendre, mixing):
    lat_rows, lon_count, chan_cols = grad_out.shape[1:]
    mode_count = lon_count // 2
    groups = lax.axis_size("lat")
    chan_count = lax.axis_size("chan")
    members = lax.axis_size("ens")
    channels = chan_cols * chan_count
    local_modes, degrees, _ = legendre.shape
    table = analysis_matrix(lat_rows, lon_count, mode_count, groups)
    selections = expansion_tables(
        local_modes, chan_count, degrees, lat_rows, groups, members
    )
    chunk = table.shape[1]
    rows = local_modes * degrees * 2
    piece = channels // groups
    head = padded(piece, 32)
    held = pltpu.VMEM((groups, chunk, chan_cols), F32)
    part = folded(head, chan_cols)
    side = folded(chunk, chan_cols)
    both = shape(part.shape[0] + side.shape[0], side.shape[1])

    legendre_parts = share(jnp.stack(share(legendre.transpose(0, 2, 1), "ens")), "chan")
    spectral = call(
        analyse,
        [side] * groups,
        (silu_backward(grad_out[0], pre_act[0]), jnp.asarray(table)),
        (held,),
    )
    spectral = swap(spectral, "lat", far=True)
    coeffs_parts = [x.reshape(rows, channels) for x in share(coeffs[0], "chan")]
    (spread,) = call(
        prepare,
        [shape(chan_count, rows, groups * chunk)],
        (*legendre_parts, *(jnp.asarray(x) for x in selections)),
    )

    blocks = call(
        lambda *refs: coefficients(
            groups, chan_count, piece, *refs
        ),
        [both] * groups,
        (*spectral, spread, *coeffs_parts),
        (
            held,
            pltpu.VMEM((chan_count, rows, chan_cols), BF16),
            pltpu.VMEM((groups, head, chan_cols), F32),
        ),
    )
    blocks = cross([blocks[-1], *blocks[:-1]], "lat", far=True)
    blocks = [*blocks[1:], blocks[0]]
    returned = shape(groups * chunk, chan_cols)
    total, received = call(
        lambda *refs: add_groups(1.0 / (members * mode_count), *refs),
        [part, returned],
        blocks,
        (held,),
    )
    (mixed,) = call(
        mix,
        [returned],
        (*share(received, "chan"), mixing),
        (pltpu.VMEM((chan_count, *returned.shape), BF16),),
    )
    if table.size < 1 << 20:
        back = jnp.asarray(np.ascontiguousarray(table.reshape(-1, lat_rows * lon_count).T))
    else:
        back = jnp.asarray(table)
    result, mark = call(
        synthesise,
        [shape(*grad_out.shape[1:]), shape(8, 128, dtype=F32)],
        (mixed, back, grad_out[0]),
    )
    (total,) = call(
        add_members,
        [part],
        (mark, *cross([total] * members, "ens")),
        (pltpu.VMEM((members, *part.shape), F32),),
    )
    gathered = cross([total] * groups, "lat")
    passed = [total, *[turn(block) for block in gathered[1:]]]
    pieces_held = pltpu.VMEM((groups, head, chan_cols), F32)
    (assembled,) = call(
        lambda *refs: assemble(piece, *refs),
        [shape(channels, chan_cols)],
        gathered,
        (pieces_held,),
    )
    (weight_grad,) = call(
        lambda *refs: finish(piece, *refs),
        [shape(channels, channels, dtype=F32)],
        (assembled, *passed),
        (pieces_held,),
    )
    return (result[None], weight_grad)


def solution(mesh):
    placed = (
        P(("grp", "ens"), "lat", None, "chan"),
        P(("grp", "ens"), "lat", None, "chan"),
        P(("grp", "ens"), ("lat", "chan"), None, None, None),
        P(("lat", "chan"), None, "ens"),
        P(),
    )
    return jax.shard_map(
        on_device,
        mesh=mesh,
        in_specs=placed,
        out_specs=(P(("grp", "ens"), "lat", None, "chan"), P("grp", None)),
        check_vma=False,
    )
```
